32 devices in a mesh: rows: 8 (over z, x), seg: 4 (over y, core).
Axes of the slice: x: 2, y: 2, z: 4, core: 2. Of those that a mesh axis runs over, the one named last changes fastest.
Arguments:
- tokens: bfloat16 [24576, 1152], P(('rows', 'seg')), may hold values from -4 to 4
- condition: bfloat16 [32, 4, 1152], P(('rows', 'seg')), may hold values from -4 to 4
- segment_ids: int32 [32, 768], P(('rows', 'seg')), may hold values from 0 to 3, never falling along the last dimension, each value on 1 to 256 neighbouring positions
- cotangent: bfloat16 [24576, 1152], P(('rows', 'seg')), may hold values from -4 to 4
- modulation_master: float32 [1152, 6912], P('rows'), may hold values from -0.1875 to 0.1875
- modulation_first: float32 [1152, 6912], P('rows'), may hold values from -31.353468 to 31.353468
- modulation_second: float32 [1152, 6912], P('rows'), may hold values from 1.96608 to 31.45728
- attention_master: float32 [1152, 3456], P('rows'), may hold values from -0.1875 to 0.1875
- attention_first: float32 [1152, 3456], P('rows'), may hold values from -31.353468 to 31.353468
- attention_second: float32 [1152, 3456], P('rows'), may hold values from 1.96608 to 31.45728
- projection_master: float32 [1152, 1152], P('rows'), may hold values from -0.5 to 0.5
- projection_first: float32 [1152, 1152], P('rows'), may hold values from -31.353468 to 31.353468
- projection_second: float32 [1152, 1152], P('rows'), may hold values from 1.96608 to 31.45728
- expand_master: float32 [1152, 4608], P('rows'), may hold values from -0.1875 to 0.1875
- expand_first: float32 [1152, 4608], P('rows'), may hold values from -31.353468 to 31.353468
- expand_second: float32 [1152, 4608], P('rows'), may hold values from 1.96608 to 31.45728
- contract_master: float32 [4608, 1152], P('rows'), may hold values from -0.09375 to 0.09375
- contract_first: float32 [4608, 1152], P('rows'), may hold values from -31.353468 to 31.353468
- contract_second: float32 [4608, 1152], P('rows'), may hold values from 1.96608 to 31.45728
- bias_master: float32 [16128], P('rows'), may hold values from -0.6 to 0.6
- bias_first: float32 [16128], P('rows'), may hold values from -31.353468 to 31.353468
- bias_second: float32 [16128], P('rows'), may hold values from 1.96608 to 31.45728
Outputs:
- output: bfloat16 [24576, 1152], P(('rows', 'seg'))
- back_tokens: bfloat16 [24576, 1152], P(('rows', 'seg'))
- modulation_new: float32 [1152, 6912], P('rows')
- modulation_first_new: float32 [1152, 6912], P('rows')
- modulation_second_new: float32 [1152, 6912], P('rows')
- attention_new: float32 [1152, 3456], P('rows')
- attention_first_new: float32 [1152, 3456], P('rows')
- attention_second_new: float32 [1152, 3456], P('rows')
- projection_new: float32 [1152, 1152], P('rows')
- projection_first_new: float32 [1152, 1152], P('rows')
- projection_second_new: float32 [1152, 1152], P('rows')
- expand_new: float32 [1152, 4608], P('rows')
- expand_first_new: float32 [1152, 4608], P('rows')
- expand_second_new: float32 [1152, 4608], P('rows')
- contract_new: float32 [4608, 1152], P('rows')
- contract_first_new: float32 [4608, 1152], P('rows')
- contract_second_new: float32 [4608, 1152], P('rows')
- bias_new: float32 [16128], P('rows')
- bias_first_new: float32 [16128], P('rows')
- bias_second_new: float32 [16128], P('rows')
The draws below stay inside these ranges and needn't reach their ends.
Inputs may be any that keep to these rules, and one draw needn't show every extreme that they name: `segment_ids`: within each row part the ids never fall and every id occurs; a segment holds 1 to 256 tokens, and one segment of each part exactly 256.
All inputs are finite; a program needn't handle non-finite values.
Results may differ from the reference program's by a relative error of at most 0.013.
The reference program's roundings to bfloat16 on the way count: a program that leaves them out, or rounds other values in their place, can miss the bound.
Values may be sent and summed in bfloat16 or wider, within the bound.
A program may use at most 248 MiB of HBM per device.

```python
import math
import jax
import jax.numpy as jnp
import numpy as np
from jax import lax

HEADS = 16
HEAD_DIM = 72
D = 1152
FF = 4608
IMG = 256
TOK_DEV = 768
SEG_DEV = 4
STEP = 10
BLEN = 16128
BLOCKS = 32
TOKENS = 24576


def drawn_values(key, shape, scale):
    values = jnp.clip(jax.random.normal(key, shape, jnp.float32), -4.0, 4.0)
    return values * scale


def draw_tokens(key, part):
    return drawn_values(jax.random.fold_in(key, 11), (TOKENS, D), 1.0).astype(jnp.bfloat16)


def draw_condition(key, part):
    return drawn_values(jax.random.fold_in(key, 13), (BLOCKS, SEG_DEV, D), 1.0).astype(jnp.bfloat16)


def draw_cotangent(key, part):
    return drawn_values(jax.random.fold_in(key, 17), (TOKENS, D), 1.0).astype(jnp.bfloat16)


def draw_bias_master(key, part):
    return drawn_values(jax.random.fold_in(key, 19), (BLEN,), 0.15)


def block_levels(key, shape, cuts, least, high):
    factor_of = 1.0
    for dim, parts in cuts:
        draws = jax.random.uniform(jax.random.fold_in(jax.random.fold_in(key, 6), dim), (parts,), jnp.float32, least / len(cuts), high / len(cuts))
        factor_of = factor_of * jnp.repeat(jnp.exp(draws), shape[dim] // parts).reshape((-1,) + (1,) * (len(shape) - 1 - dim))
    return factor_of


def profile(count, total, limit, slope):
    portions = [(1 << 20) // math.isqrt(rank ** slope) + 1 for rank in range(2, count + 1)]
    spare, holding = total - limit - (count - 1), [1] * (count - 1)
    while spare > 0:
        free = [i for i in range(count - 1) if holding[i] < limit]
        pool, remaining = sum([portions[i] for i in free]), spare
        for i in free:
            addition = min(limit - holding[i], max(1, remaining * portions[i] // pool), spare)
            holding[i] = holding[i] + addition
            spare = spare - addition
    return np.array([limit] + holding)


def uneven(key, number_of, total, limit, slope):
    if number_of == 2:
        one = jax.random.randint(key, (), max(1, total - limit), min(limit, total - 1) + 1)
        return jnp.stack([one, total - one])
    tallies = jnp.asarray(profile(number_of, total, limit, slope), jnp.int32)
    couples = (number_of - 1) // 2
    donor, receiver = tallies[1:1 + 2 * couples:2], tallies[2:2 + 2 * couples:2]
    room = jnp.minimum(donor - 1, limit - receiver)
    passed = jax.random.randint(jax.random.fold_in(key, 1), (couples,), 0, 1 << 20) % (room + 1)
    tallies = tallies.at[1:1 + 2 * couples:2].set(donor - passed).at[2:2 + 2 * couples:2].set(receiver + passed)
    return tallies[jax.random.permutation(jax.random.fold_in(key, 2), number_of)]


def bell_draw(own_key, extent, deviation, bound, cuts=(), kind=jnp.bfloat16):
    array = deviation * jax.random.normal(own_key, extent, jnp.float32)
    if cuts:
        array = array * block_levels(own_key, extent, cuts, -0.22, 0.18)
    return jnp.clip(array, -bound, bound).astype(kind)


def setup_inputs(seed: int = 0) -> dict:
    arg_keys = jax.random.split(jax.random.key(seed), 23)
    return {
        "tokens": draw_tokens(jax.random.fold_in(arg_keys[22], 71), 0),
        "condition": draw_condition(jax.random.fold_in(arg_keys[22], 71), 0),
        "segment_ids": jax.vmap(lambda own: jnp.searchsorted(jnp.cumsum(uneven(own, SEG_DEV, TOK_DEV, IMG, 1)), jnp.arange(TOK_DEV), side="right"))(jax.random.split(arg_keys[2], BLOCKS)).reshape((BLOCKS, TOK_DEV)).astype(jnp.int32),
        "cotangent": draw_cotangent(jax.random.fold_in(arg_keys[22], 71), 0),
        "modulation_master": bell_draw(arg_keys[4], (D, 6 * D), D ** -0.5, 0.1875, ((0, 8),), jnp.float32),
        "modulation_first": bell_draw(arg_keys[5], (D, 6 * D), (0.044 * TOKENS ** 0.5), 31.353468, ((0, 8),), jnp.float32),
        "modulation_second": jnp.clip(jnp.exp(math.log(31.45728) - 2.7725887 * jax.random.uniform(arg_keys[6], (D, 6 * D), jnp.float32) ** block_levels(arg_keys[6], (D, 6 * D), ((0, 8),), -0.2, 0.2)), 1.96608, 31.45728),
        "attention_master": bell_draw(arg_keys[7], (D, 3 * D), D ** -0.5, 0.1875, ((0, 8),), jnp.float32),
        "attention_first": bell_draw(arg_keys[8], (D, 3 * D), (0.044 * TOKENS ** 0.5), 31.353468, ((0, 8),), jnp.float32),
        "attention_second": jnp.clip(jnp.exp(math.log(31.45728) - 2.7725887 * jax.random.uniform(arg_keys[9], (D, 3 * D), jnp.float32) ** block_levels(arg_keys[9], (D, 3 * D), ((0, 8),), -0.2, 0.2)), 1.96608, 31.45728),
        "projection_master": bell_draw(arg_keys[10], (D, D), (D // 8) ** -0.5, 0.5, ((0, 8),), jnp.float32),
        "projection_first": bell_draw(arg_keys[11], (D, D), (0.044 * TOKENS ** 0.5), 31.353468, ((0, 8),), jnp.float32),
        "projection_second": jnp.clip(jnp.exp(math.log(31.45728) - 2.7725887 * jax.random.uniform(arg_keys[12], (D, D), jnp.float32) ** block_levels(arg_keys[12], (D, D), ((0, 8),), -0.2, 0.2)), 1.96608, 31.45728),
        "expand_master": bell_draw(arg_keys[13], (D, FF), D ** -0.5, 0.1875, ((0, 8),), jnp.float32),
        "expand_first": bell_draw(arg_keys[14], (D, FF), (0.044 * TOKENS ** 0.5), 31.353468, ((0, 8),), jnp.float32),
        "expand_second": jnp.clip(jnp.exp(math.log(31.45728) - 2.7725887 * jax.random.uniform(arg_keys[15], (D, FF), jnp.float32) ** block_levels(arg_keys[15], (D, FF), ((0, 8),), -0.2, 0.2)), 1.96608, 31.45728),
        "contract_master": bell_draw(arg_keys[16], (FF, D), FF ** -0.5, 0.09375, ((0, 8),), jnp.float32),
        "contract_first": bell_draw(arg_keys[17], (FF, D), (0.044 * TOKENS ** 0.5), 31.353468, ((0, 8),), jnp.float32),
        "contract_second": jnp.clip(jnp.exp(math.log(31.45728) - 2.7725887 * jax.random.uniform(arg_keys[18], (FF, D), jnp.float32) ** block_levels(arg_keys[18], (FF, D), ((0, 8),), -0.2, 0.2)), 1.96608, 31.45728),
        "bias_master": draw_bias_master(jax.random.fold_in(arg_keys[22], 71), 0),
        "bias_first": bell_draw(arg_keys[20], (BLEN,), (0.044 * TOKENS ** 0.5), 31.353468, ((0, 8),), jnp.float32),
        "bias_second": jnp.clip(jnp.exp(math.log(31.45728) - 2.7725887 * jax.random.uniform(arg_keys[21], (BLEN,), jnp.float32) ** block_levels(arg_keys[21], (BLEN,), ((0, 8),), -0.2, 0.2)), 1.96608, 31.45728),
    }


@jax.custom_vjp
def low(v):
    return lax.optimization_barrier(v.astype(jnp.bfloat16)).astype(jnp.float32)

@jax.custom_vjp
def low_back(v):
    return v

def low_keep(v):
    return (low(v), None)

def low_pass(kept, grad):
    return (grad,)

def back_keep(v):
    return (v, None)

def back_low(kept, grad):
    return (low(grad),)
low.defvjp(low_keep, low_pass)
low_back.defvjp(back_keep, back_low)
highest = lax.Precision.HIGHEST
beta_first = 0.9
beta_second = 0.999
learning = 0.06
weight_decay = 0.1
adam_epsilon = 1e-08
norm_epsilon = 1e-06

def layer_norm(values):
    center = values - lax.optimization_barrier(jnp.mean(values, axis=-1, keepdims=True))
    return center * lax.rsqrt(lax.optimization_barrier(jnp.mean(center * center, axis=-1, keepdims=True)) + norm_epsilon)

def split_bias(biases, width, hidden):
    edges = [0, width, 2 * width, 3 * width, 3 * width + hidden, 4 * width + hidden, 10 * width + hidden]
    return [biases[edges[number]:edges[number + 1]] for number in range(6)]

def adam_update(gradient, master, first, second):
    first_new = beta_first * first + (1.0 - beta_first) * gradient
    second_new = beta_second * second + (1.0 - beta_second) * gradient * gradient
    first_hat = first_new / (1.0 - beta_first ** STEP)
    second_hat = second_new / (1.0 - beta_second ** STEP)
    master_new = master - learning * (first_hat / (jnp.sqrt(second_hat) + adam_epsilon) + weight_decay * master)
    return (master_new, first_new, second_new)

def reference(tokens, condition, segment_ids, cotangent, modulation_master, modulation_first, modulation_second, attention_master, attention_first, attention_second, projection_master, projection_first, projection_second, expand_master, expand_first, expand_second, contract_master, contract_first, contract_second, bias_master, bias_first, bias_second):
    cond_silu = low(jax.nn.silu(condition.astype(jnp.float32)))

    def whole(tokens_wide, mod_master, att_master, proj_master, exp_master, con_master, biases_master):
        modulation_weight = low(mod_master)
        attention_weight = low(att_master)
        projection_weight = low(proj_master)
        expand_weight = low(exp_master)
        contract_weight = low(con_master)
        query_bias, value_bias, projection_bias, expand_bias, contract_bias, modulation_bias = split_bias(low(biases_master), D, FF)

        def one_block(operands):
            block_tokens, block_cond, segments = operands
            modulation = jnp.dot(block_cond, modulation_weight, precision=highest) + modulation_bias
            onehot = (segments[:, None] == jnp.arange(SEG_DEV, dtype=jnp.int32)[None, :]).astype(jnp.float32)
            per_token = jnp.dot(onehot, modulation, precision=highest)
            shift_one, scale_one, gate_one, shift_two, scale_two, gate_two = jnp.split(per_token, 6, axis=1)
            hidden_one = low(layer_norm(block_tokens) * (1.0 + scale_one) + shift_one)
            triple = jnp.dot(hidden_one, attention_weight, precision=highest)
            query = low(low_back(triple[:, :D] + query_bias))
            key = low(low_back(triple[:, D:2 * D]))
            value = low(low_back(triple[:, 2 * D:] + value_bias))
            query_heads = query.reshape(TOK_DEV, HEADS, HEAD_DIM)
            key_heads = key.reshape(TOK_DEV, HEADS, HEAD_DIM)
            value_heads = value.reshape(TOK_DEV, HEADS, HEAD_DIM)
            scores = jnp.einsum('qhd,khd->hqk', query_heads, key_heads, precision=highest) * HEAD_DIM ** (-0.5)
            same = segments[:, None] == segments[None, :]
            scores = low_back(jnp.where(same[None], scores, -1e+30))
            softened = low(jax.nn.softmax(scores, axis=-1))
            mixed = jnp.einsum('hqk,khd->qhd', softened, value_heads, precision=highest).reshape(TOK_DEV, D)
            attended = low(low_back(mixed))
            projected = low_back(jnp.dot(attended, projection_weight, precision=highest) + projection_bias)
            middle = block_tokens + gate_one * projected
            hidden_two = low(layer_norm(middle) * (1.0 + scale_two) + shift_two)
            before = low_back(jnp.dot(hidden_two, expand_weight, precision=highest) + expand_bias)
            activated = low(jax.nn.gelu(before, approximate=True))
            feedforward = low_back(jnp.dot(activated, contract_weight, precision=highest) + contract_bias)
            return middle + gate_two * feedforward
        blocks = lax.map(jax.checkpoint(one_block), (tokens_wide.reshape(BLOCKS, TOK_DEV, D), cond_silu, segment_ids))
        return blocks.reshape(TOKENS, D)
    output, pullback = jax.vjp(whole, tokens.astype(jnp.float32), modulation_master, attention_master, projection_master, expand_master, contract_master, bias_master)
    gradients = pullback(cotangent.astype(jnp.float32))
    new_mod = adam_update(gradients[1], modulation_master, modulation_first, modulation_second)
    new_att = adam_update(gradients[2], attention_master, attention_first, attention_second)
    new_proj = adam_update(gradients[3], projection_master, projection_first, projection_second)
    new_exp = adam_update(gradients[4], expand_master, expand_first, expand_second)
    new_con = adam_update(gradients[5], contract_master, contract_first, contract_second)
    new_bias = adam_update(gradients[6], bias_master, bias_first, bias_second)
    return (output.astype(jnp.bfloat16), gradients[0].astype(jnp.bfloat16), new_mod[0], new_mod[1], new_mod[2], new_att[0], new_att[1], new_att[2], new_proj[0], new_proj[1], new_proj[2], new_exp[0], new_exp[1], new_exp[2], new_con[0], new_con[1], new_con[2], new_bias[0], new_bias[1], new_bias[2])
```

```python
from functools import partial

import jax
import jax.numpy as jnp
from jax import lax
from jax.experimental import pallas as pl
from jax.experimental.pallas import tpu as pltpu
from jax.sharding import PartitionSpec as P

HEAD_DIM = 72
STEP = 10

bf16 = jnp.bfloat16
f32 = jnp.float32
highest = lax.Precision.HIGHEST
beta_first = 0.9
beta_second = 0.999
learning = 0.06
weight_decay = 0.1
adam_epsilon = 1e-08
norm_epsilon = 1e-06

ROW_X = [(z * 2 + x, z * 2 + 1 - x) for z in range(4) for x in range(2)]
ROW_Z = [
    [(z * 2 + x, (z + k) % 4 * 2 + x) for z in range(4) for x in range(2)] for k in range(4)
]
SEG_Y = [(y * 2 + c, (1 - y) * 2 + c) for y in range(2) for c in range(2)]
SEG_C = [(y * 2 + c, y * 2 + 1 - c) for y in range(2) for c in range(2)]


def over_x(v):
    return lax.ppermute(v, "rows", ROW_X)


def over_z(v, k):
    return lax.ppermute(v, "rows", ROW_Z[k])


def over_y(v):
    return lax.ppermute(v, "seg", SEG_Y)


def over_core(v):
    return lax.ppermute(v, "seg", SEG_C)


def place():
    row = lax.axis_index("rows")
    seg = lax.axis_index("seg")
    return row % 2, seg // 2, row // 2, seg % 2


def layer_norm(values):
    center = values - jnp.mean(values, axis=-1, keepdims=True)
    inverse = lax.rsqrt(jnp.mean(center * center, axis=-1, keepdims=True) + norm_epsilon)
    return (center * inverse, inverse)


def norm_back(upstream, normed, inverse):
    return inverse * (
        upstream
        - jnp.mean(upstream, axis=-1, keepdims=True)
        - normed * jnp.mean(upstream * normed, axis=-1, keepdims=True)
    )


def outer(left, right, precision=None):
    return lax.dot_general(
        left,
        right,
        (((0,), (0,)), ((), ())),
        precision=precision,
        preferred_element_type=f32,
    )


def dot(left, right):
    return jnp.dot(left, right, preferred_element_type=f32)


def back_dot(left, right):
    return lax.dot_general(left, right, (((1,), (1,)), ((), ())), preferred_element_type=f32)


def to_heads(values):
    return values.reshape(values.shape[0], -1, HEAD_DIM).transpose(1, 0, 2)


def from_heads(values):
    return values.transpose(1, 0, 2).reshape(values.shape[1], -1)


def soft_weights(same, query, key):
    scores = back_dot(query, key) * HEAD_DIM ** (-0.5)
    scores = jnp.where(same, scores, -1e30)
    powers = jnp.exp(scores - jnp.max(scores, axis=-1, keepdims=True))
    return powers / jnp.sum(powers, axis=-1, keepdims=True)


def attend_head(same, operands):
    query, key, value = operands
    softened = soft_weights(same, query, key).astype(bf16)
    return dot(softened, value).astype(bf16)


def head_back(same, operands):
    query, key, value, upstream = operands
    softened = soft_weights(same, query, key)
    back_value = outer(softened.astype(bf16), upstream)
    back_soft = back_dot(upstream, value)
    back_score = (
        softened * (back_soft - jnp.sum(back_soft * softened, axis=-1, keepdims=True))
    ).astype(bf16)
    scale = HEAD_DIM ** (-0.5)
    back_query = dot(back_score, key) * scale
    back_key = outer(back_score, query) * scale
    return (back_query.astype(bf16), back_key.astype(bf16), back_value.astype(bf16))


def adam_update(gradient, master, first, second):
    first_new = beta_first * first + (1.0 - beta_first) * gradient
    second_new = beta_second * second + (1.0 - beta_second) * gradient * gradient
    first_hat = first_new / (1.0 - beta_first**STEP)
    second_hat = second_new / (1.0 - beta_second**STEP)
    master_new = master - learning * (
        first_hat / (jnp.sqrt(second_hat) + adam_epsilon) + weight_decay * master
    )
    return (master_new, first_new, second_new)


def remote(src, dst, send, recv, device):
    return pltpu.make_async_remote_copy(
        src_ref=src,
        dst_ref=dst,
        send_sem=send,
        recv_sem=recv,
        device_id=device,
        device_id_type=pl.DeviceIdType.MESH,
    )


def greet(peers):
    barrier = pltpu.get_barrier_semaphore()
    for peer in peers:
        pl.semaphore_signal(
            barrier, inc=1, device_id=peer, device_id_type=pl.DeviceIdType.MESH
        )
    pl.semaphore_wait(barrier, len(peers))


def gather_kernel(own, w_nat, w_con, w, z_s, z_r, x_s, x_r, y_s, y_r, c_s, c_r, load_sem, out_sem):
    row, seg = lax.axis_index("rows"), lax.axis_index("seg")
    x, z = row % 2, row // 2
    y, c = seg // 2, seg % 2
    n = own.shape[1]
    units = own.shape[0] // 2
    piece = n // 3
    part = pl.multiple_of(y * piece, piece)
    third = pl.multiple_of(y * 2 * piece, piece)
    far = [lax.rem(z + 4 - k, 4) for k in range(4)]
    loads = []
    for u in range(units):
        copy = pltpu.make_async_copy(
            own.at[2 * u + c, pl.ds(part, 2 * piece)],
            w.at[2 * u + c, row, pl.ds(part, 2 * piece)],
            load_sem.at[u],
        )
        copy.start()
        loads.append(copy)
    z_peers = [(lax.rem(z + k, 4) * 2 + x, seg) for k in (1, 2, 3)]
    x_peer, y_peer, c_peer = (row + 1 - 2 * x, seg), (row, seg + 2 - 4 * y), (row, seg + 1 - 2 * c)
    greet(z_peers + [x_peer, y_peer, c_peer])
    sent = []

    def along_z(u, k):
        ref = w.at[2 * u + c, row, pl.ds(part, 2 * piece)]
        return remote(ref, ref, z_s.at[u, k - 1], z_r.at[u, k - 1], z_peers[k - 1])

    def along_x(u, k):
        ref = w.at[2 * u + c, far[k] * 2 + x, pl.ds(part, 2 * piece)]
        return remote(ref, ref, x_s.at[u, k], x_r.at[u, k], x_peer)

    def along_y(u, k):
        ref = w.at[2 * u + c, pl.ds(far[k] * 2, 2), pl.ds(third, piece)]
        return remote(ref, ref, y_s.at[u, k], y_r.at[u, k], y_peer)

    def across(u, k):
        ref = w.at[2 * u + c, pl.ds(far[k] * 2, 2)]
        return remote(ref, ref, c_s.at[u, k], c_r.at[u, k], c_peer)

    def go(copy):
        copy.start()
        sent.append(copy)

    steps = [(u, k) for u in range(units) for k in (0, 1, 3, 2)]
    outs = []
    for j in range(len(steps) + 3):
        if j < len(steps):
            u, k = steps[j]
            if k == 0:
                for later in [0, 1] if u == 0 else [u + 1]:
                    if later < units:
                        loads[later].wait()
                        for hop in (1, 3, 2):
                            go(along_z(later, hop))
            else:
                along_z(u, k).wait_recv()
            go(along_x(u, k))
        if 0 <= j - 1 < len(steps):
            along_x(*steps[j - 1]).wait_recv()
            go(along_y(*steps[j - 1]))
        if 0 <= j - 2 < len(steps):
            along_y(*steps[j - 2]).wait_recv()
            go(across(*steps[j - 2]))
        if 0 <= j - 3 < len(steps):
            u, k = steps[j - 3]
            across(u, k).wait_recv()
            if k == 2:
                for b in (2 * u, 2 * u + 1):
                    dst = w_nat.at[b] if u < 4 else w_con.at[:, b - 8]
                    copy = pltpu.make_async_copy(w.at[b], dst, out_sem.at[b])
                    copy.start()
                    outs.append(copy)
    for copy in sent:
        copy.wait_send()
    for copy in outs:
        copy.wait()


def gather_fast(attention, projection, expand, contract):
    width = projection.shape[1]
    n = attention.shape[0]
    blocks = [attention[:, j * width : (j + 1) * width] for j in range(3)] + [projection]
    blocks += [expand[:, j * width : (j + 1) * width] for j in range(4)]
    blocks += [contract[j * n : (j + 1) * n] for j in range(4)]
    own = jnp.stack([block.astype(bf16) for block in blocks])
    sems = pltpu.SemaphoreType.DMA
    w_nat, w_con = pl.pallas_call(
        gather_kernel,
        out_shape=(
            jax.ShapeDtypeStruct((8, 8, n, width), bf16),
            jax.ShapeDtypeStruct((8, 4, n, width), bf16),
        ),
        in_specs=[pl.BlockSpec(memory_space=pl.ANY)],
        out_specs=(pl.BlockSpec(memory_space=pl.ANY),) * 2,
        scratch_shapes=[pltpu.VMEM((12, 8, n, width), bf16)]
        + [sems((6, 3))] * 2
        + [sems((6, 4))] * 6
        + [sems((6,)), sems((12,))],
        compiler_params=pltpu.CompilerParams(
            collective_id=0, has_side_effects=True, vmem_limit_bytes=48 << 20
        ),
        name="gather_weights",
    )(own)
    w_nat = w_nat.reshape(8, 8 * n, width)
    return (
        (w_nat[0], w_nat[1], w_nat[2]),
        w_nat[3],
        (w_nat[4], w_nat[5], w_nat[6], w_nat[7]),
        w_con.reshape(32 * n, width),
    )


def gather_plain(attention, projection, expand, contract):
    def whole(part):
        return lax.all_gather(part.astype(bf16), "rows", axis=0, tiled=True)

    width = projection.shape[1]
    att, proj, exp, con = map(whole, (attention, projection, expand, contract))
    return (
        tuple(att[:, j * width : (j + 1) * width] for j in range(3)),
        proj,
        tuple(exp[:, j * width : (j + 1) * width] for j in range(4)),
        con,
    )


def reduce_unit(part):
    x, y, z, c = place()
    part = part.reshape(8, 3, part.shape[0] // 24, part.shape[1])
    there = lax.dynamic_index_in_dim(part, 1 - y, 1, False)
    here = lax.dynamic_index_in_dim(part, y, 1, False)
    here = here.astype(f32) + over_y(there).astype(f32)
    pair = jnp.stack([here.astype(bf16), part[:, 2]], axis=1)
    pair = pair.reshape((4, 2) + pair.shape[1:])
    there = lax.dynamic_index_in_dim(pair, 1 - x, 1, False)
    here = lax.dynamic_index_in_dim(pair, x, 1, False)
    quad = (here.astype(f32) + over_x(there).astype(f32)).astype(bf16)

    def level(k):
        return lax.dynamic_index_in_dim(quad, lax.rem(z + k, 4), 0, False)

    total = level(0).astype(f32)
    for k in (1, 2, 3):
        total = total + over_z(level(k), k).astype(f32)
    total = total.astype(bf16)
    back = over_y(total)
    last = (total[1].astype(f32) + back[1].astype(f32)).astype(bf16)
    first = jnp.where(y == 0, total[0], back[0])
    second = jnp.where(y == 0, back[0], total[0])
    mine = jnp.concatenate([first, second, last])
    other = over_core(mine)
    return (
        jnp.where(c == 0, mine, other).astype(f32),
        jnp.where(c == 0, other, mine).astype(f32),
    )


def reduce_fast(early, hidden_one, attended, hidden_two, activated, back_feed, back_before):
    x, y, z, c = place()
    width = hidden_one.shape[1]

    def pick(first, second, which):
        return jnp.where(which == 0, first, second)

    act = activated.T.reshape(8, 4, width // 8, activated.shape[0])
    feed_far = over_core(back_feed)
    results = {}
    for unit in range(2):
        mine, there = (
            lax.dynamic_index_in_dim(act, 2 * unit + which, 1, False).reshape(width, -1)
            for which in (c, 1 - c)
        )
        far = over_core(there)
        results["con", unit] = reduce_unit((dot(mine, back_feed) + dot(far, feed_far)).astype(bf16))
    two_far = over_core(hidden_two)
    for unit in range(2):
        first, second = (
            back_before[:, (2 * unit + j) * width : (2 * unit + j + 1) * width] for j in range(2)
        )
        far = over_core(pick(second, first, c))
        results["exp", unit] = reduce_unit(
            (outer(hidden_two, pick(first, second, c)) + outer(two_far, far)).astype(bf16)
        )
    one_far, att_far = over_core(hidden_one), over_core(attended)

    def late(back_query, back_key, back_value, back_project):
        far = over_core(pick(back_project, back_key, c))
        left, left_far = pick(hidden_one, attended, c), pick(one_far, att_far, c)
        first = reduce_unit(
            (outer(left, pick(back_key, back_project, c)) + outer(left_far, far)).astype(bf16)
        )
        far = over_core(pick(back_value, back_query, c))
        second = reduce_unit(
            (outer(hidden_one, pick(back_query, back_value, c)) + outer(one_far, far)).astype(bf16)
        )
        con = jnp.concatenate(results["con", 0] + results["con", 1], axis=0)
        exp = jnp.concatenate(results["exp", 0] + results["exp", 1], axis=1)
        att = jnp.concatenate([second[0], first[0], second[1]], axis=1)
        return att, first[1], exp, con

    return late


def reduce_plain(early, hidden_one, attended, hidden_two, activated, back_feed, back_before):
    def total(left, right):
        part = lax.psum_scatter(
            outer(left, right).astype(bf16), "rows", scatter_dimension=0, tiled=True
        )
        return lax.psum(part.astype(f32), "seg")

    con = total(activated, back_feed)
    exp = total(hidden_two, back_before)

    def late(back_query, back_key, back_value, back_project):
        att = total(hidden_one, jnp.concatenate([back_query, back_key, back_value], axis=1))
        return att, total(attended, back_project), exp, con

    return late


def on_device(
    fast,
    tokens,
    condition,
    segment_ids,
    cotangent,
    modulation_master,
    modulation_first,
    modulation_second,
    attention_master,
    attention_first,
    attention_second,
    projection_master,
    projection_first,
    projection_second,
    expand_master,
    expand_first,
    expand_second,
    contract_master,
    contract_first,
    contract_second,
    bias_master,
    bias_first,
    bias_second,
):
    width = tokens.shape[1]
    hidden = expand_master.shape[1]
    shard = modulation_master.shape[0]
    n_seg = condition.shape[1]
    row = lax.axis_index("rows")
    segments = segment_ids[0]
    onehot = (segments[:, None] == jnp.arange(n_seg, dtype=jnp.int32)[None, :]).astype(f32)
    same = segments[:, None] == segments[None, :]
    tokens_wide = tokens.astype(f32)
    upstream = cotangent.astype(f32)

    cond_silu = jax.nn.silu(condition[0].astype(f32)).astype(bf16)
    cond_seg = lax.all_gather(cond_silu, "rows", axis=0, tiled=True)
    cond_mine = lax.dynamic_slice_in_dim(cond_seg, row * shard, shard, axis=1)
    partial_mod = dot(cond_mine, modulation_master.astype(bf16))
    modulation = lax.psum_scatter(partial_mod, "rows", scatter_dimension=0, tiled=True)
    biases = lax.all_gather(bias_master.astype(bf16), "rows", axis=0, tiled=True).astype(f32)
    query_bias, value_bias, projection_bias = (
        biases[j * width : (j + 1) * width] for j in range(3)
    )
    expand_bias = biases[3 * width : 3 * width + hidden]
    contract_bias = biases[3 * width + hidden : 4 * width + hidden]
    modulation = modulation + biases[4 * width + hidden :]

    gather = gather_fast if fast else gather_plain
    w_att, w_proj, w_exp, w_con = gather(
        attention_master, projection_master, expand_master, contract_master
    )

    per_token = jnp.dot(onehot, modulation, precision=highest)
    shift_one, scale_one, gate_one, shift_two, scale_two, gate_two = jnp.split(per_token, 6, axis=1)
    normed_one, inverse_one = layer_norm(tokens_wide)
    hidden_one = (normed_one * (1.0 + scale_one) + shift_one).astype(bf16)
    query = (dot(hidden_one, w_att[0]) + query_bias).astype(bf16)
    key = dot(hidden_one, w_att[1]).astype(bf16)
    value = (dot(hidden_one, w_att[2]) + value_bias).astype(bf16)
    heads = (to_heads(query), to_heads(key), to_heads(value))
    attended = from_heads(lax.map(partial(attend_head, same), heads))
    projected = dot(attended, w_proj) + projection_bias
    middle = tokens_wide + gate_one * projected
    normed_two, inverse_two = layer_norm(middle)
    hidden_two = (normed_two * (1.0 + scale_two) + shift_two).astype(bf16)
    before = (
        jnp.concatenate([dot(hidden_two, part) for part in w_exp], axis=1) + expand_bias
    )
    activated = jax.nn.gelu(before, approximate=True).astype(bf16)
    feedforward = dot(activated, w_con) + contract_bias
    output = middle + gate_two * feedforward

    back_gate_two = upstream * feedforward
    back_feed = (upstream * gate_two).astype(bf16)
    back_active = back_dot(back_feed, w_con)
    gelu_pull = jax.vjp(partial(jax.nn.gelu, approximate=True), before)[1]
    back_before = gelu_pull(back_active)[0].astype(bf16)
    reduce = reduce_fast if fast else reduce_plain
    late = reduce(None, hidden_one, attended, hidden_two, activated, back_feed, back_before)
    back_hidden_two = sum(
        back_dot(back_before[:, j * width : (j + 1) * width], w_exp[j]) for j in range(4)
    )
    back_middle = upstream + norm_back(back_hidden_two * (1.0 + scale_two), normed_two, inverse_two)
    back_gate_one = back_middle * projected
    back_project = (back_middle * gate_one).astype(bf16)
    back_attend = back_dot(back_project, w_proj).astype(bf16)
    back_heads = lax.map(partial(head_back, same), heads + (to_heads(back_attend),))
    back_query, back_key, back_value = (from_heads(part) for part in back_heads)
    grad_att, grad_proj, grad_exp, grad_con = late(back_query, back_key, back_value, back_project)
    back_hidden_one = (
        back_dot(back_query, w_att[0]) + back_dot(back_key, w_att[1]) + back_dot(back_value, w_att[2])
    )
    back_tokens = back_middle + norm_back(
        back_hidden_one * (1.0 + scale_one), normed_one, inverse_one
    )
    back_modulation = jnp.concatenate(
        [
            outer(onehot, part, highest)
            for part in (
                back_hidden_one,
                back_hidden_one * normed_one,
                back_gate_one,
                back_hidden_two,
                back_hidden_two * normed_two,
                back_gate_two,
            )
        ],
        axis=1,
    )
    columns = jnp.concatenate(
        [
            jnp.sum(part.astype(f32), axis=0)
            for part in (back_query, back_value, back_project, back_before, back_feed)
        ]
    )
    payload = jnp.concatenate([back_modulation, columns.reshape(n_seg, -1)], axis=1)
    everyone = lax.all_gather(payload, ("rows", "seg"), axis=0, tiled=True)
    cond_all = lax.all_gather(cond_silu, ("rows", "seg"), axis=0, tiled=True)
    mod_all = everyone[:, : 6 * width]
    cond_rows = lax.dynamic_slice_in_dim(cond_all, row * shard, shard, axis=1)
    grad_mod = outer(cond_rows.astype(f32), mod_all, highest)
    devices = everyone.shape[0] // n_seg
    rest = jnp.sum(everyone[:, 6 * width :].reshape(devices, -1), axis=0)
    grad_bias = lax.dynamic_slice_in_dim(
        jnp.concatenate([rest, jnp.sum(mod_all, axis=0)]),
        row * bias_master.shape[0],
        bias_master.shape[0],
    )
    results = [
        adam_update(*operands)
        for operands in (
            (grad_mod, modulation_master, modulation_first, modulation_second),
            (grad_att, attention_master, attention_first, attention_second),
            (grad_proj, projection_master, projection_first, projection_second),
            (grad_exp, expand_master, expand_first, expand_second),
            (grad_con, contract_master, contract_first, contract_second),
            (grad_bias, bias_master, bias_first, bias_second),
        )
    ]
    flat = tuple((item for result in results for item in result))
    return (output.astype(bf16), back_tokens.astype(bf16)) + flat


def solution(mesh):
    both = ("rows", "seg")
    fast = mesh.shape["rows"] == 8 and mesh.shape["seg"] == 4
    token, matrix, vector = P(both, None), P("rows", None), P("rows")
    in_specs = (token, P(both, None, None), token, token) + (matrix,) * 15 + (vector,) * 3
    out_specs = (token, token) + (matrix,) * 15 + (vector,) * 3
    return jax.shard_map(
        partial(on_device, fast),
        mesh=mesh,
        in_specs=in_specs,
        out_specs=out_specs,
        check_vma=False,
    )
```

```python
from functools import partial

import jax
import jax.numpy as jnp
from jax import lax
from jax.experimental import pallas as pl
from jax.experimental.pallas import tpu as pltpu
from jax.sharding import PartitionSpec as P

HEAD_DIM = 72
STEP = 10
SPAN = 256
EXP_SCALE = HEAD_DIM**-0.5 * 1.4426950408889634

bf16 = jnp.bfloat16
f32 = jnp.float32
highest = lax.Precision.HIGHEST
beta_first = 0.9
beta_second = 0.999
learning = 0.06
weight_decay = 0.1
adam_epsilon = 1e-08
norm_epsilon = 1e-06

ROW_X = [(z * 2 + x, z * 2 + 1 - x) for z in range(4) for x in range(2)]
ROW_Z = [
    [(z * 2 + x, (z + k) % 4 * 2 + x) for z in range(4) for x in range(2)] for k in range(4)
]
SEG_Y = [(y * 2 + c, (1 - y) * 2 + c) for y in range(2) for c in range(2)]
SEG_C = [(y * 2 + c, y * 2 + 1 - c) for y in range(2) for c in range(2)]


def over_x(v):
    return lax.ppermute(v, "rows", ROW_X)


def over_z(v, k):
    return lax.ppermute(v, "rows", ROW_Z[k])


def over_y(v):
    return lax.ppermute(v, "seg", SEG_Y)


def over_core(v):
    return lax.ppermute(v, "seg", SEG_C)


def place():
    row = lax.axis_index("rows")
    seg = lax.axis_index("seg")
    return row % 2, seg // 2, row // 2, seg % 2


def layer_norm(values):
    center = values - jnp.mean(values, axis=-1, keepdims=True)
    inverse = lax.rsqrt(jnp.mean(center * center, axis=-1, keepdims=True) + norm_epsilon)
    return (center * inverse, inverse)


def norm_back(upstream, normed, inverse):
    return inverse * (
        upstream
        - jnp.mean(upstream, axis=-1, keepdims=True)
        - normed * jnp.mean(upstream * normed, axis=-1, keepdims=True)
    )


def outer(left, right, precision=None):
    return lax.dot_general(
        left,
        right,
        (((0,), (0,)), ((), ())),
        precision=precision,
        preferred_element_type=f32,
    )


def dot(left, right):
    return jnp.dot(left, right, preferred_element_type=f32)


def back_dot(left, right):
    return lax.dot_general(left, right, (((1,), (1,)), ((), ())), preferred_element_type=f32)


def spread(starts, source, padded, out):
    rows=source.shape[0]
    padded[0:rows,:]=source[...]
    padded[rows:,:]=jnp.zeros((padded.shape[0]-rows,padded.shape[1]),bf16)
    def one(s,_):
        start=starts[s]
        base=pl.multiple_of(start//128*128,128)
        row=lax.broadcasted_iota(jnp.int32,(SPAN,SPAN+128),0)
        col=lax.broadcasted_iota(jnp.int32,(SPAN,SPAN+128),1)
        pick=(col==row+(start-base))&(row<starts[s+1]-start)
        out[s]=dot(pick.astype(bf16),padded[pl.ds(base,SPAN+128),:]).astype(bf16)
        return 0
    lax.fori_loop(0,out.shape[0],one,0)

def unspread(starts, slabs, out):
    n=slabs.shape[0]; rows=out.shape[0]
    def one(i,_):
        row=lax.broadcasted_iota(jnp.int32,(SPAN,1),0)+i*SPAN
        home=row
        for s in range(1,n):
            home=home+jnp.where(row>=starts[s],SPAN-(starts[s]-starts[s-1]),0)
        pick=(lax.broadcasted_iota(jnp.int32,(SPAN,n*SPAN),1)==home).astype(bf16)
        out[pl.ds(pl.multiple_of(i*SPAN,SPAN),SPAN),:]=dot(pick,slabs[...].reshape(n*SPAN,slabs.shape[2])).astype(bf16)
        return 0
    lax.fori_loop(0,rows//SPAN,one,0)

def attend_kernel(starts, q, k, v, out, qs, ks, vs, wide, os):
    for src,dst in ((q,qs),(k,ks),(v,vs)): spread(starts,src,wide,dst)
    n=qs.shape[0]
    def seg(s,_):
        length=starts[s+1]-starts[s]
        outside=jnp.where(lax.broadcasted_iota(jnp.int32,(SPAN,1),0)<length,0.0,-1e30)
        for h in range(qs.shape[2]//HEAD_DIM):
            cols=slice(h*HEAD_DIM,(h+1)*HEAD_DIM)
            score=back_dot(ks[s,:,cols],qs[s,:,cols])+outside
            power=jnp.exp2((score-jnp.max(score,axis=0,keepdims=True))*EXP_SCALE)
            soft=(power*(1.0/jnp.sum(power,axis=0,keepdims=True))).astype(bf16)
            os[s,:,cols]=outer(soft,vs[s,:,cols]).astype(bf16)
        return 0
    lax.fori_loop(0,n,seg,0)
    unspread(starts,os,out)

def back_kernel(starts, qs, ks, vs, up, dq, dk, dv, wide, ups, dqs, dks, dvs):
    spread(starts,up,wide,ups)
    n=qs.shape[0]; scale=HEAD_DIM**-0.5
    def seg(s,_):
        length=starts[s+1]-starts[s]
        outside=jnp.where(lax.broadcasted_iota(jnp.int32,(SPAN,1),0)<length,0.0,-1e30)
        for h in range(qs.shape[2]//HEAD_DIM):
            cols=slice(h*HEAD_DIM,(h+1)*HEAD_DIM)
            query,key,value,upstream=qs[s,:,cols],ks[s,:,cols],vs[s,:,cols],ups[s,:,cols]
            score=back_dot(key,query)+outside
            power=jnp.exp2((score-jnp.max(score,axis=0,keepdims=True))*EXP_SCALE)
            soft=power*(1.0/jnp.sum(power,axis=0,keepdims=True))
            back_soft=back_dot(value,upstream)
            mean=jnp.sum(back_soft*soft,axis=0,keepdims=True)
            back_score=(soft*(back_soft-mean)).astype(bf16)
            dvs[s,:,cols]=dot(soft.astype(bf16),upstream).astype(bf16)
            dks[s,:,cols]=(dot(back_score,query)*scale).astype(bf16)
            dqs[s,:,cols]=(outer(back_score,key)*scale).astype(bf16)
        return 0
    lax.fori_loop(0,n,seg,0)
    for slabs,out in ((dqs,dq),(dks,dk),(dvs,dv)): unspread(starts,slabs,out)

VM = pl.BlockSpec(memory_space=pltpu.VMEM)
SM = pl.BlockSpec(memory_space=pltpu.SMEM)
ANY = pl.BlockSpec(memory_space=pl.ANY)
def attend(starts,q,k,v):
    n=starts.shape[0]-1; rows,width=q.shape
    slab=jax.ShapeDtypeStruct((n,SPAN,width),bf16)
    return pl.pallas_call(attend_kernel,out_shape=(jax.ShapeDtypeStruct(q.shape,bf16),slab,slab,slab),
        in_specs=[SM,VM,VM,VM],out_specs=(VM,)*4,
        scratch_shapes=[pltpu.VMEM((rows+SPAN,width),bf16),pltpu.VMEM((n,SPAN,width),bf16)],
        compiler_params=pltpu.CompilerParams(vmem_limit_bytes=56<<20),
        cost_estimate=pl.CostEstimate(flops=2*2*16*n*SPAN*SPAN*128,bytes_accessed=rows*width*14,transcendentals=16*n*SPAN*SPAN),name="attend")(starts,q,k,v)
def attend_back(starts,qs,ks,vs,up):
    n=starts.shape[0]-1; rows,width=up.shape
    slab=pltpu.VMEM((n,SPAN,width),bf16); o=jax.ShapeDtypeStruct(up.shape,bf16)
    return pl.pallas_call(back_kernel,out_shape=(o,o,o),
        in_specs=[SM,VM,VM,VM,VM],out_specs=(VM,)*3,
        scratch_shapes=[pltpu.VMEM((rows+SPAN,width),bf16)]+[slab]*4,
        compiler_params=pltpu.CompilerParams(vmem_limit_bytes=56<<20),
        cost_estimate=pl.CostEstimate(flops=5*2*16*n*SPAN*SPAN*128,bytes_accessed=rows*width*14,transcendentals=16*n*SPAN*SPAN),name="attend_back")(starts,qs,ks,vs,up)


def adam_update(gradient, master, first, second):
    first_new = beta_first * first + (1.0 - beta_first) * gradient
    second_new = beta_second * second + (1.0 - beta_second) * gradient * gradient
    first_hat = first_new / (1.0 - beta_first**STEP)
    second_hat = second_new / (1.0 - beta_second**STEP)
    master_new = master - learning * (
        first_hat / (jnp.sqrt(second_hat) + adam_epsilon) + weight_decay * master
    )
    return (master_new, first_new, second_new)


def remote(src, dst, send, recv, device):
    return pltpu.make_async_remote_copy(
        src_ref=src,
        dst_ref=dst,
        send_sem=send,
        recv_sem=recv,
        device_id=device,
        device_id_type=pl.DeviceIdType.MESH,
    )


def greet(peers):
    barrier = pltpu.get_barrier_semaphore()
    for peer in peers:
        pl.semaphore_signal(
            barrier, inc=1, device_id=peer, device_id_type=pl.DeviceIdType.MESH
        )
    pl.semaphore_wait(barrier, len(peers))


def gather_kernel(
    own, cond, bias, w_mod, *refs
):
    w_out, (w_con, modulation, biases), rest = refs[:8], refs[8:11], refs[11:]
    w, conds, parts, x_parts, z_parts, small_s, small_r, part_s, part_r = rest[:9]
    z_s, z_r, x_s, x_r, y_s, y_r, c_s, c_r, load_sem, out_sem = rest[9:]
    row, seg = lax.axis_index("rows"), lax.axis_index("seg")
    x, z = row % 2, row // 2
    y, c = seg // 2, seg % 2
    n = own.shape[1]
    width = own.shape[2]
    units = own.shape[0] // 2
    piece = n // 3
    part = pl.multiple_of(y * piece, piece)
    third = pl.multiple_of(y * 2 * piece, piece)
    far = [lax.rem(z + 4 - k, 4) for k in range(4)]
    loads = []
    for u in range(units):
        copy = pltpu.make_async_copy(
            own.at[2 * u + c, pl.ds(part, 2 * piece)],
            w.at[2 * u + c, row, pl.ds(part, 2 * piece)],
            load_sem.at[u],
        )
        copy.start()
        loads.append(copy)
    z_peers = [(lax.rem(z + k, 4) * 2 + x, seg) for k in (1, 2, 3)]
    x_peer, y_peer, c_peer = (row + 1 - 2 * x, seg), (row, seg + 2 - 4 * y), (row, seg + 1 - 2 * c)
    cross_peers = [(lax.rem(z + k, 4) * 2 + 1 - x, seg) for k in (1, 2, 3)]
    row_peers = z_peers + cross_peers + [x_peer]
    greet(row_peers + [y_peer, c_peer])
    sent = []

    small = []
    for i, peer in enumerate(row_peers):
        small.append(remote(cond.at[peer[0]], conds.at[row], small_s.at[i], small_r.at[i], peer))
        small.append(remote(bias, biases.at[row], small_s.at[7 + i], small_r.at[7 + i], peer))
    for copy in small:
        copy.start()
        sent.append(copy)
    conds[row] = cond[row]
    biases[row] = bias[...]

    def to_x():
        return remote(parts.at[:, 1 - x], x_parts, part_s.at[0], part_r.at[0], x_peer)

    def to_z(k):
        src = parts.at[lax.rem(z + k, 4), x]
        return remote(src, z_parts.at[k - 1], part_s.at[k], part_r.at[k], z_peers[k - 1])

    def multiply():
        for copy in small:
            copy.wait_recv()
        left = conds[...].reshape(-1, conds.shape[2])[:, : w_mod.shape[0]].astype(bf16)
        half = w_mod.shape[1] // 2
        upper = lax.broadcasted_iota(jnp.int32, (left.shape[0], 1), 0) % 8 < 4
        for start in range(0, half, width):
            both = jnp.where(
                upper,
                dot(left, w_mod[:, start : start + width]),
                dot(left, w_mod[:, half + start : half + start + width]),
            )
            parts[:, :, :, start : start + width] = both.reshape(4, 2, 8, width)
        go(to_x())

    def sum_x():
        to_x().wait_recv()
        for level in range(4):
            parts[level, x] = parts[level, x] + x_parts[level]
        for k in (1, 3, 2):
            go(to_z(k))

    def sum_z():
        for k in (1, 3, 2):
            to_z(k).wait_recv()
        modulation[...] = parts[z, x] + z_parts[0] + z_parts[1] + z_parts[2]

    def along_z(u, k):
        ref = w.at[2 * u + c, row, pl.ds(part, 2 * piece)]
        return remote(ref, ref, z_s.at[u, k - 1], z_r.at[u, k - 1], z_peers[k - 1])

    def along_x(u, k):
        ref = w.at[2 * u + c, far[k] * 2 + x, pl.ds(part, 2 * piece)]
        return remote(ref, ref, x_s.at[u, k], x_r.at[u, k], x_peer)

    def along_y(u, k):
        ref = w.at[2 * u + c, pl.ds(far[k] * 2, 2), pl.ds(third, piece)]
        return remote(ref, ref, y_s.at[u, k], y_r.at[u, k], y_peer)

    def across(u, k):
        ref = w.at[2 * u + c, pl.ds(far[k] * 2, 2)]
        return remote(ref, ref, c_s.at[u, k], c_r.at[u, k], c_peer)

    def go(copy):
        copy.start()
        sent.append(copy)

    steps = [(u, k) for u in range(units) for k in (0, 1, 3, 2)]
    outs = []
    for j in range(len(steps) + 3):
        if j < len(steps):
            u, k = steps[j]
            if k == 0:
                for later in [0, 1] if u == 0 else [u + 1]:
                    if later < units:
                        loads[later].wait()
                        for hop in (1, 3, 2):
                            go(along_z(later, hop))
            else:
                along_z(u, k).wait_recv()
            go(along_x(u, k))
            if j == 0:
                multiply()
            if j == 2:
                sum_x()
            if j == 6:
                sum_z()
        if 0 <= j - 1 < len(steps):
            along_x(*steps[j - 1]).wait_recv()
            go(along_y(*steps[j - 1]))
        if 0 <= j - 2 < len(steps):
            along_y(*steps[j - 2]).wait_recv()
            go(across(*steps[j - 2]))
        if 0 <= j - 3 < len(steps):
            u, k = steps[j - 3]
            across(u, k).wait_recv()
            if k == 2:
                for b in (2 * u, 2 * u + 1):
                    dst = w_out[b] if u < 4 else w_con.at[:, b - 8]
                    copy = pltpu.make_async_copy(w.at[b], dst, out_sem.at[b])
                    copy.start()
                    outs.append(copy)
    for copy in sent:
        copy.wait_send()
    for copy in outs:
        copy.wait()


def gather_fast(attention, projection, expand, contract, cond_silu, bias_low, mod_low):
    width = projection.shape[1]
    n = attention.shape[0]
    blocks = [attention[:, j * width : (j + 1) * width] for j in range(3)] + [projection]
    blocks += [expand[:, j * width : (j + 1) * width] for j in range(4)]
    blocks += [contract[j * n : (j + 1) * n] for j in range(4)]
    own = jnp.stack([block.astype(bf16) for block in blocks])
    n_seg = cond_silu.shape[0]
    cond = cond_silu.astype(f32).reshape(n_seg, 8, n).transpose(1, 0, 2)
    cond = jnp.pad(jnp.concatenate([cond, cond], axis=1), ((0, 0), (0, 0), (0, 256 - n)))
    n_bias = bias_low.shape[0]
    bias = jnp.pad(bias_low, (0, 2048 - n_bias)).reshape(16, 128)
    sems = pltpu.SemaphoreType.DMA
    outs = pl.pallas_call(
        gather_kernel,
        out_shape=(jax.ShapeDtypeStruct((8, n, width), bf16),) * 8
        + (
            jax.ShapeDtypeStruct((8, 4, n, width), bf16),
            jax.ShapeDtypeStruct((8, 3 * width), f32),
            jax.ShapeDtypeStruct((8, 16, 128), bf16),
        ),
        in_specs=[ANY, VM, VM, VM],
        out_specs=(ANY,) * 9 + (VM, VM),
        scratch_shapes=[
            pltpu.VMEM((12, 8, n, width), bf16),
            pltpu.VMEM((8, 8, 256), f32),
            pltpu.VMEM((4, 2, 8, 3 * width), f32),
            pltpu.VMEM((4, 8, 3 * width), f32),
            pltpu.VMEM((3, 8, 3 * width), f32),
            sems((14,)),
            sems((14,)),
            sems((4,)),
            sems((4,)),
        ]
        + [sems((6, 3))] * 2
        + [sems((6, 4))] * 6
        + [sems((6,)), sems((12,))],
        compiler_params=pltpu.CompilerParams(
            collective_id=0, has_side_effects=True, vmem_limit_bytes=50 << 20
        ),
        name="gather_weights",
    )(own, cond, bias, mod_low)
    w = [block.reshape(8 * n, width) for block in outs[:8]]
    modulation = jnp.concatenate([outs[9][:n_seg], outs[9][n_seg:]], axis=1)
    biases = outs[10].reshape(8, 2048)[:, :n_bias].reshape(-1)
    return tuple(w[:3]), w[3], tuple(w[4:]), outs[8].reshape(32 * n, width), modulation, biases


def gather_plain(attention, projection, expand, contract, cond_silu, bias_low, mod_low):
    def whole(part):
        return lax.all_gather(part.astype(bf16), "rows", axis=0, tiled=True)

    width = projection.shape[1]
    att, proj, exp, con = map(whole, (attention, projection, expand, contract))
    shard = mod_low.shape[0]
    cond = lax.all_gather(cond_silu, "rows", axis=0, tiled=True)
    cond = lax.dynamic_slice_in_dim(cond, lax.axis_index("rows") * shard, shard, axis=1)
    modulation = lax.psum_scatter(dot(cond, mod_low), "rows", scatter_dimension=0, tiled=True)
    return (
        tuple(att[:, j * width : (j + 1) * width] for j in range(3)),
        proj,
        tuple(exp[:, j * width : (j + 1) * width] for j in range(4)),
        con,
        modulation,
        whole(bias_low),
    )


def reduce_kernel(
    blocks, out, d, y_in, x_in, z_in, total, y2_in, grad, load, y_s, y_r, x_s, x_r, z_s, z_r, y2_s, y2_r, c_s, c_r, store
):
    row, seg = lax.axis_index("rows"), lax.axis_index("seg")
    x, z = row % 2, row // 2
    y, c = seg // 2, seg % 2
    units, _, n, width = blocks.shape
    piece = n // 3
    part = pl.multiple_of(y * piece, piece)
    mine = pl.multiple_of(y * 2 * piece, piece)
    theirs = pl.multiple_of((1 - y) * 2 * piece, piece)
    level = [lax.rem(z + k, 4) for k in range(4)]
    z_peers = [(level[k] * 2 + x, seg) for k in range(4)]
    x_peer, y_peer, c_peer = (row + 1 - 2 * x, seg), (row, seg + 2 - 4 * y), (row, seg + 1 - 2 * c)
    loads = []
    for u in range(units):
        copy = pltpu.make_async_copy(blocks.at[u], d.at[u], load.at[u])
        copy.start()
        loads.append(copy)
    greet(z_peers[1:] + [x_peer, y_peer, c_peer])
    sent = []

    def add(*terms):
        result = terms[0].astype(f32)
        for term in terms[1:]:
            result = result + term.astype(f32)
        return result.astype(bf16)

    def to_y(u, k):
        src = d.at[u, pl.ds(level[k] * 2, 2), pl.ds(theirs, piece)]
        return remote(src, y_in.at[u, k], y_s.at[u, k], y_r.at[u, k], y_peer)

    def to_x(u, k):
        src = d.at[u, level[k] * 2 + 1 - x, pl.ds(part, 2 * piece)]
        return remote(src, x_in.at[u, k], x_s.at[u, k], x_r.at[u, k], x_peer)

    def to_z(u, k):
        src = d.at[u, level[k] * 2 + x, pl.ds(part, 2 * piece)]
        return remote(src, z_in.at[u, k - 1], z_s.at[u, k - 1], z_r.at[u, k - 1], z_peers[k])

    def to_y_again(u):
        return remote(total.at[u], y2_in.at[u], y2_s.at[u], y2_r.at[u], y_peer)

    def to_core(u):
        ref = grad.at[u, c]
        return remote(ref, ref, c_s.at[u], c_r.at[u], c_peer)

    def go(copy):
        copy.start()
        sent.append(copy)

    steps = [(u, k) for u in range(units) for k in (1, 3, 2, 0)]
    ahead = 5
    outs = []

    def first(j):
        u, k = steps[j]
        if k == 1:
            loads[u].wait()
        go(to_y(u, k))

    for j in range(ahead):
        first(j)
    for j in range(len(steps) + 8):
        if j + ahead < len(steps):
            first(j + ahead)
        if j < len(steps):
            u, k = steps[j]
            to_y(u, k).wait_recv()
            for side in range(2):
                r = level[k] * 2 + side
                d[u, r, pl.ds(mine, piece)] = add(d[u, r, pl.ds(mine, piece)], y_in[u, k, side])
            go(to_x(u, k))
        if 0 <= j - 1 < len(steps):
            u, k = steps[j - 1]
            to_x(u, k).wait_recv()
            r = level[k] * 2 + x
            d[u, r, pl.ds(part, 2 * piece)] = add(d[u, r, pl.ds(part, 2 * piece)], x_in[u, k])
            if k:
                go(to_z(u, k))
        if j >= 3 and (j - 3) % 4 == 2 and (j - 3) // 4 < units:
            u = (j - 3) // 4
            for k in (1, 3, 2):
                to_z(u, k).wait_recv()
            total[u] = add(d[u, row, pl.ds(part, 2 * piece)], z_in[u, 0], z_in[u, 1], z_in[u, 2])
            go(to_y_again(u))
        if j >= 4 and (j - 4) % 4 == 2 and (j - 4) // 4 < units:
            u = (j - 4) // 4
            to_y_again(u).wait_recv()
            here, there = y * piece, (1 - y) * piece
            here, there = pl.multiple_of(here, piece), pl.multiple_of(there, piece)
            grad[u, c, pl.ds(mine, piece)] = total[u, pl.ds(here, piece)]
            grad[u, c, pl.ds(theirs, piece)] = y2_in[u, pl.ds(there, piece)]
            grad[u, c, pl.ds(piece, piece)] = add(
                total[u, pl.ds(there, piece)], y2_in[u, pl.ds(here, piece)]
            )
            go(to_core(u))
        if j >= 5 and (j - 5) % 4 == 2 and (j - 5) // 4 < units:
            u = (j - 5) // 4
            to_core(u).wait_recv()
            copy = pltpu.make_async_copy(grad.at[u], out.at[u], store.at[u])
            copy.start()
            outs.append(copy)
    for copy in sent:
        copy.wait_send()
    for copy in outs:
        copy.wait()


def reduce_units(blocks, number):
    units = len(blocks)
    rows, width = blocks[0].shape
    n = rows // 8
    sems = pltpu.SemaphoreType.DMA

    def space(*shape):
        return pltpu.VMEM(shape + (width,), bf16)

    return pl.pallas_call(
        reduce_kernel,
        out_shape=jax.ShapeDtypeStruct((units, 2, n, width), bf16),
        in_specs=[ANY],
        out_specs=ANY,
        scratch_shapes=[
            space(units, 8, n),
            space(units, 4, 2, n // 3),
            space(units, 4, 2 * n // 3),
            space(units, 3, 2 * n // 3),
            space(units, 2 * n // 3),
            space(units, 2 * n // 3),
            space(units, 2, n),
            sems((units,)),
        ]
        + [sems((units, 4))] * 4
        + [sems((units, 3))] * 2
        + [sems((units,))] * 5,
        compiler_params=pltpu.CompilerParams(
            collective_id=number, has_side_effects=True, vmem_limit_bytes=48 << 20
        ),
        name=f"reduce_{number}",
    )(jnp.stack(blocks).reshape(units, 8, n, width))


def reduce_fast(early, hidden_one, attended, hidden_two, activated, back_feed, back_before):
    x, y, z, c = place()
    width = hidden_one.shape[1]

    def pick(first, second, which):
        return jnp.where(which == 0, first, second)

    act = activated.T.reshape(8, 4, width // 8, activated.shape[0])
    feed_far = over_core(back_feed)
    blocks = []
    for unit in range(2):
        mine, there = (
            lax.dynamic_index_in_dim(act, 2 * unit + which, 1, False).reshape(width, -1)
            for which in (c, 1 - c)
        )
        far = over_core(there)
        blocks.append((dot(mine, back_feed) + dot(far, feed_far)).astype(bf16))
    two_far = over_core(hidden_two)
    for unit in range(2):
        first, second = (
            back_before[:, (2 * unit + j) * width : (2 * unit + j + 1) * width] for j in range(2)
        )
        far = over_core(pick(second, first, c))
        blocks.append(
            (outer(hidden_two, pick(first, second, c)) + outer(two_far, far)).astype(bf16)
        )
    big = reduce_units(blocks, 1).astype(f32)
    one_far, att_far = over_core(hidden_one), over_core(attended)

    def late(back_query, back_key, back_value, back_project):
        far = over_core(pick(back_project, back_key, c))
        left, left_far = pick(hidden_one, attended, c), pick(one_far, att_far, c)
        first = (outer(left, pick(back_key, back_project, c)) + outer(left_far, far)).astype(bf16)
        far = over_core(pick(back_value, back_query, c))
        second = (
            outer(hidden_one, pick(back_query, back_value, c)) + outer(one_far, far)
        ).astype(bf16)
        small = reduce_units([first, second], 2).astype(f32)
        con = big[0:2].reshape(-1, width)
        exp = jnp.concatenate([big[2, 0], big[2, 1], big[3, 0], big[3, 1]], axis=1)
        att = jnp.concatenate([small[1, 0], small[0, 0], small[1, 1]], axis=1)
        return att, small[0, 1], exp, con

    return late


def reduce_plain(early, hidden_one, attended, hidden_two, activated, back_feed, back_before):
    def total(left, right):
        part = lax.psum_scatter(
            outer(left, right).astype(bf16), "rows", scatter_dimension=0, tiled=True
        )
        return lax.psum(part.astype(f32), "seg")

    con = total(activated, back_feed)
    exp = total(hidden_two, back_before)

    def late(back_query, back_key, back_value, back_project):
        att = total(hidden_one, jnp.concatenate([back_query, back_key, back_value], axis=1))
        return att, total(attended, back_project), exp, con

    return late


def on_device(
    fast,
    tokens,
    condition,
    segment_ids,
    cotangent,
    modulation_master,
    modulation_first,
    modulation_second,
    attention_master,
    attention_first,
    attention_second,
    projection_master,
    projection_first,
    projection_second,
    expand_master,
    expand_first,
    expand_second,
    contract_master,
    contract_first,
    contract_second,
    bias_master,
    bias_first,
    bias_second,
):
    width = tokens.shape[1]
    hidden = expand_master.shape[1]
    shard = modulation_master.shape[0]
    n_seg = condition.shape[1]
    row = lax.axis_index("rows")
    segments = segment_ids[0]
    onehot = (segments[:, None] == jnp.arange(n_seg, dtype=jnp.int32)[None, :]).astype(f32)
    starts = jnp.sum(
        segments[:, None] < jnp.arange(n_seg + 1, dtype=jnp.int32)[None, :], axis=0, dtype=jnp.int32
    )
    tokens_wide = tokens.astype(f32)
    upstream = cotangent.astype(f32)

    cond_silu = jax.nn.silu(condition[0].astype(f32)).astype(bf16)
    gather = gather_fast if fast else gather_plain
    w_att, w_proj, w_exp, w_con, modulation, biases = gather(
        attention_master,
        projection_master,
        expand_master,
        contract_master,
        cond_silu,
        bias_master.astype(bf16),
        modulation_master.astype(bf16),
    )
    biases = biases.astype(f32)
    query_bias, value_bias, projection_bias = (
        biases[j * width : (j + 1) * width] for j in range(3)
    )
    expand_bias = biases[3 * width : 3 * width + hidden]
    contract_bias = biases[3 * width + hidden : 4 * width + hidden]
    modulation = modulation + biases[4 * width + hidden :]

    per_token = jnp.dot(onehot, modulation, precision=highest)
    shift_one, scale_one, gate_one, shift_two, scale_two, gate_two = jnp.split(per_token, 6, axis=1)
    normed_one, inverse_one = layer_norm(tokens_wide)
    hidden_one = (normed_one * (1.0 + scale_one) + shift_one).astype(bf16)
    query = (dot(hidden_one, w_att[0]) + query_bias).astype(bf16)
    key = dot(hidden_one, w_att[1]).astype(bf16)
    value = (dot(hidden_one, w_att[2]) + value_bias).astype(bf16)
    attended, *slabs = attend(starts, query, key, value)
    projected = dot(attended, w_proj) + projection_bias
    middle = tokens_wide + gate_one * projected
    normed_two, inverse_two = layer_norm(middle)
    hidden_two = (normed_two * (1.0 + scale_two) + shift_two).astype(bf16)
    before = (
        jnp.concatenate([dot(hidden_two, part) for part in w_exp], axis=1) + expand_bias
    )
    activated = jax.nn.gelu(before, approximate=True).astype(bf16)
    feedforward = dot(activated, w_con) + contract_bias
    output = middle + gate_two * feedforward

    back_gate_two = upstream * feedforward
    back_feed = (upstream * gate_two).astype(bf16)
    back_active = back_dot(back_feed, w_con)
    gelu_pull = jax.vjp(partial(jax.nn.gelu, approximate=True), before)[1]
    back_before = gelu_pull(back_active)[0].astype(bf16)
    reduce = reduce_fast if fast else reduce_plain
    late = reduce(None, hidden_one, attended, hidden_two, activated, back_feed, back_before)
    back_hidden_two = sum(
        back_dot(back_before[:, j * width : (j + 1) * width], w_exp[j]) for j in range(4)
    )
    back_middle = upstream + norm_back(back_hidden_two * (1.0 + scale_two), normed_two, inverse_two)
    back_gate_one = back_middle * projected
    back_project = (back_middle * gate_one).astype(bf16)
    back_attend = back_dot(back_project, w_proj).astype(bf16)
    back_query, back_key, back_value = attend_back(starts, *slabs, back_attend)
    grad_att, grad_proj, grad_exp, grad_con = late(back_query, back_key, back_value, back_project)
    back_hidden_one = (
        back_dot(back_query, w_att[0]) + back_dot(back_key, w_att[1]) + back_dot(back_value, w_att[2])
    )
    back_tokens = back_middle + norm_back(
        back_hidden_one * (1.0 + scale_one), normed_one, inverse_one
    )
    back_modulation = jnp.concatenate(
        [
            outer(onehot, part, highest)
            for part in (
                back_hidden_one,
                back_hidden_one * normed_one,
                back_gate_one,
                back_hidden_two,
                back_hidden_two * normed_two,
                back_gate_two,
            )
        ],
        axis=1,
    )
    columns = jnp.concatenate(
        [
            jnp.sum(part.astype(f32), axis=0)
            for part in (back_query, back_value, back_project, back_before, back_feed)
        ]
    )
    payload = jnp.concatenate([back_modulation, columns.reshape(n_seg, -1)], axis=1)
    everyone = lax.all_gather(payload, ("rows", "seg"), axis=0, tiled=True)
    cond_all = lax.all_gather(cond_silu, ("rows", "seg"), axis=0, tiled=True)
    mod_all = everyone[:, : 6 * width]
    cond_rows = lax.dynamic_slice_in_dim(cond_all, row * shard, shard, axis=1)
    grad_mod = outer(cond_rows.astype(f32), mod_all, highest)
    devices = everyone.shape[0] // n_seg
    rest = jnp.sum(everyone[:, 6 * width :].reshape(devices, -1), axis=0)
    grad_bias = lax.dynamic_slice_in_dim(
        jnp.concatenate([rest, jnp.sum(mod_all, axis=0)]),
        row * bias_master.shape[0],
        bias_master.shape[0],
    )
    results = [
        adam_update(*operands)
        for operands in (
            (grad_mod, modulation_master, modulation_first, modulation_second),
            (grad_att, attention_master, attention_first, attention_second),
            (grad_proj, projection_master, projection_first, projection_second),
            (grad_exp, expand_master, expand_first, expand_second),
            (grad_con, contract_master, contract_first, contract_second),
            (grad_bias, bias_master, bias_first, bias_second),
        )
    ]
    flat = tuple((item for result in results for item in result))
    return (output.astype(bf16), back_tokens.astype(bf16)) + flat


def solution(mesh):
    both = ("rows", "seg")
    fast = mesh.shape["rows"] == 8 and mesh.shape["seg"] == 4
    token, matrix, vector = P(both, None), P("rows", None), P("rows")
    in_specs = (token, P(both, None, None), token, token) + (matrix,) * 15 + (vector,) * 3
    out_specs = (token, token) + (matrix,) * 15 + (vector,) * 3
    return jax.shard_map(
        partial(on_device, fast),
        mesh=mesh,
        in_specs=in_specs,
        out_specs=out_specs,
        check_vma=False,
    )
```

```python
from functools import partial

import jax
import jax.numpy as jnp
from jax import lax
from jax.experimental import pallas as pl
from jax.experimental.pallas import tpu as pltpu
from jax.sharding import PartitionSpec as P

HEAD_DIM = 72
STEP = 10
SPAN = 256
EXP_SCALE = HEAD_DIM**-0.5 * 1.4426950408889634

bf16 = jnp.bfloat16
f32 = jnp.float32
highest = lax.Precision.HIGHEST
beta_first = 0.9
beta_second = 0.999
learning = 0.06
weight_decay = 0.1
adam_epsilon = 1e-08
norm_epsilon = 1e-06

ROW_X = [(z * 2 + x, z * 2 + 1 - x) for z in range(4) for x in range(2)]
ROW_Z = [
    [(z * 2 + x, (z + k) % 4 * 2 + x) for z in range(4) for x in range(2)] for k in range(4)
]
SEG_Y = [(y * 2 + c, (1 - y) * 2 + c) for y in range(2) for c in range(2)]
SEG_C = [(y * 2 + c, y * 2 + 1 - c) for y in range(2) for c in range(2)]


def over_x(v):
    return lax.ppermute(v, "rows", ROW_X)


def over_z(v, k):
    return lax.ppermute(v, "rows", ROW_Z[k])


def over_y(v):
    return lax.ppermute(v, "seg", SEG_Y)


def over_core(v):
    return lax.ppermute(v, "seg", SEG_C)


def place():
    row = lax.axis_index("rows")
    seg = lax.axis_index("seg")
    return row % 2, seg // 2, row // 2, seg % 2


def layer_norm(values):
    center = values - jnp.mean(values, axis=-1, keepdims=True)
    inverse = lax.rsqrt(jnp.mean(center * center, axis=-1, keepdims=True) + norm_epsilon)
    return (center * inverse, inverse)


def norm_back(upstream, normed, inverse):
    return inverse * (
        upstream
        - jnp.mean(upstream, axis=-1, keepdims=True)
        - normed * jnp.mean(upstream * normed, axis=-1, keepdims=True)
    )


def outer(left, right, precision=None):
    return lax.dot_general(
        left,
        right,
        (((0,), (0,)), ((), ())),
        precision=precision,
        preferred_element_type=f32,
    )


def dot(left, right):
    return jnp.dot(left, right, preferred_element_type=f32)


def back_dot(left, right):
    return lax.dot_general(left, right, (((1,), (1,)), ((), ())), preferred_element_type=f32)


def spread_rows(starts, source, s):
    rows = source.shape[0]
    row = lax.broadcasted_iota(jnp.int32, (SPAN, rows), 0) + starts[s]
    col = lax.broadcasted_iota(jnp.int32, (SPAN, rows), 1)
    pick = jnp.where((col == row) & (row < starts[s + 1]), 1.0, 0.0).astype(bf16)
    return dot(pick, source[...])

def spread(starts, source, out):
    def one(s,_):
        out[s]=spread_rows(starts,source,s).astype(bf16)
        return 0
    lax.fori_loop(0,out.shape[0],one,0)

def unspread(starts, slabs, out):
    n=slabs.shape[0]; rows=out.shape[0]
    def one(i,_):
        row=lax.broadcasted_iota(jnp.int32,(SPAN,1),0)+i*SPAN
        home=row
        for s in range(1,n):
            home=home+jnp.where(row>=starts[s],SPAN-(starts[s]-starts[s-1]),0)
        pick=(lax.broadcasted_iota(jnp.int32,(SPAN,n*SPAN),1)==home).astype(bf16)
        out[pl.ds(pl.multiple_of(i*SPAN,SPAN),SPAN),:]=dot(pick,slabs[...].reshape(n*SPAN,slabs.shape[2])).astype(bf16)
        return 0
    lax.fori_loop(0,rows//SPAN,one,0)

def attend_slab(starts, s, qs, ks, vs, os, heads):
    length = starts[s + 1] - starts[s]
    outside = jnp.where(lax.broadcasted_iota(jnp.int32, (SPAN, 1), 0) < length, 0.0, -1e30)
    for h in heads:
        cols = slice(h * HEAD_DIM, (h + 1) * HEAD_DIM)
        score = back_dot(ks[s, :, cols], qs[s, :, cols]) + outside
        power = jnp.exp2((score - jnp.max(score, axis=0, keepdims=True)) * EXP_SCALE)
        soft = (power * (1.0 / jnp.sum(power, axis=0, keepdims=True))).astype(bf16)
        os[s, :, cols] = outer(soft, vs[s, :, cols]).astype(bf16)


def attend_kernel(starts, q, k, v, out, qs, ks, vs, os):
    for src, dst in ((q, qs), (k, ks), (v, vs)):
        spread(starts, src, dst)

    def seg(s, carry):
        attend_slab(starts, s, qs, ks, vs, os, range(qs.shape[2] // HEAD_DIM))
        return carry

    lax.fori_loop(0, qs.shape[0], seg, 0)
    unspread(starts, os, out)

def back_kernel(starts, qs, ks, vs, up, dq, dk, dv, ups, dqs, dks, dvs):
    spread(starts,up,ups)
    n=qs.shape[0]; scale=HEAD_DIM**-0.5
    def seg(s,_):
        length=starts[s+1]-starts[s]
        outside=jnp.where(lax.broadcasted_iota(jnp.int32,(SPAN,1),0)<length,0.0,-1e30)
        for h in range(qs.shape[2]//HEAD_DIM):
            cols=slice(h*HEAD_DIM,(h+1)*HEAD_DIM)
            query,key,value,upstream=qs[s,:,cols],ks[s,:,cols],vs[s,:,cols],ups[s,:,cols]
            score=back_dot(key,query)+outside
            power=jnp.exp2((score-jnp.max(score,axis=0,keepdims=True))*EXP_SCALE)
            soft=power*(1.0/jnp.sum(power,axis=0,keepdims=True))
            back_soft=back_dot(value,upstream)
            mean=jnp.sum(back_soft*soft,axis=0,keepdims=True)
            back_score=(soft*(back_soft-mean)).astype(bf16)
            dvs[s,:,cols]=dot(soft.astype(bf16),upstream).astype(bf16)
            dks[s,:,cols]=(dot(back_score,query)*scale).astype(bf16)
            dqs[s,:,cols]=(outer(back_score,key)*scale).astype(bf16)
        return 0
    lax.fori_loop(0,n,seg,0)
    for slabs,out in ((dqs,dq),(dks,dk),(dvs,dv)): unspread(starts,slabs,out)

VM = pl.BlockSpec(memory_space=pltpu.VMEM)
SM = pl.BlockSpec(memory_space=pltpu.SMEM)
ANY = pl.BlockSpec(memory_space=pl.ANY)
def attend(starts,q,k,v):
    n=starts.shape[0]-1; rows,width=q.shape
    slab=jax.ShapeDtypeStruct((n,SPAN,width),bf16)
    return pl.pallas_call(attend_kernel,out_shape=(jax.ShapeDtypeStruct(q.shape,bf16),slab,slab,slab),
        in_specs=[SM,VM,VM,VM],out_specs=(VM,)*4,
        scratch_shapes=[pltpu.VMEM((n,SPAN,width),bf16)],
        compiler_params=pltpu.CompilerParams(vmem_limit_bytes=56<<20),
        cost_estimate=pl.CostEstimate(flops=2*2*16*n*SPAN*SPAN*128,bytes_accessed=rows*width*14,transcendentals=16*n*SPAN*SPAN),name="attend")(starts,q,k,v)
def attend_back(starts,qs,ks,vs,up):
    n=starts.shape[0]-1; rows,width=up.shape
    slab=pltpu.VMEM((n,SPAN,width),bf16); o=jax.ShapeDtypeStruct(up.shape,bf16)
    return pl.pallas_call(back_kernel,out_shape=(o,o,o),
        in_specs=[SM,VM,VM,VM,VM],out_specs=(VM,)*3,
        scratch_shapes=[slab]*4,
        compiler_params=pltpu.CompilerParams(vmem_limit_bytes=56<<20),
        cost_estimate=pl.CostEstimate(flops=5*2*16*n*SPAN*SPAN*128,bytes_accessed=rows*width*14,transcendentals=16*n*SPAN*SPAN),name="attend_back")(starts,qs,ks,vs,up)


def adam_update(gradient, master, first, second):
    first_new = beta_first * first + (1.0 - beta_first) * gradient
    second_new = beta_second * second + (1.0 - beta_second) * gradient * gradient
    first_hat = first_new / (1.0 - beta_first**STEP)
    second_hat = second_new / (1.0 - beta_second**STEP)
    master_new = master - learning * (
        first_hat / (jnp.sqrt(second_hat) + adam_epsilon) + weight_decay * master
    )
    return (master_new, first_new, second_new)


def gelu(v):
    return 0.5 * v * (1.0 + jnp.tanh(0.7978845608028654 * (v + 0.044715 * (v * v * v))))


def remote(src, dst, send, recv, device):
    return pltpu.make_async_remote_copy(
        src_ref=src,
        dst_ref=dst,
        send_sem=send,
        recv_sem=recv,
        device_id=device,
        device_id_type=pl.DeviceIdType.MESH,
    )


def greet(peers):
    barrier = pltpu.get_barrier_semaphore()
    for peer in peers:
        pl.semaphore_signal(
            barrier, inc=1, device_id=peer, device_id_type=pl.DeviceIdType.MESH
        )
    pl.semaphore_wait(barrier, len(peers))


def layer_rows(values):
    center = values - jnp.mean(values, axis=-1, keepdims=True)
    return center * lax.rsqrt(jnp.mean(center * center, axis=-1, keepdims=True) + norm_epsilon)


def forward_kernel(
    own, cond, bias, w_mod, starts, seg_ids, tokens, *refs
):
    w_out, rest = refs[:8], refs[8:]
    w_con_out, modulation, h1_out, slab_out, att_out, proj_out, mid_out, h2_out = rest[:8]
    before_out, act_out, ff_out, y_out = rest[8:12]
    w, w_con, conds, bias_in, bias_all, parts, x_parts, z_parts = rest[12:20]
    slabs, padded, wide, hidden = rest[20:24]
    small_s, small_r, part_s, part_r = rest[24:28]
    z_s, z_r, x_s, x_r, y_s, y_r, c_s, c_r, load_sem, out_sem, save_sem = rest[28:]
    row, seg = lax.axis_index("rows"), lax.axis_index("seg")
    x, z = row % 2, row // 2
    y, c = seg // 2, seg % 2
    n, width = own.shape[1:]
    count = tokens.shape[0]
    units = ((0, 2), (1, 3), (4, 5), (6, 7), (8, 9), (10, 11))
    piece = n // 3
    part = pl.multiple_of(y * piece, piece)
    third = pl.multiple_of(y * 2 * piece, piece)
    far = [lax.rem(z + 4 - k, 4) for k in range(4)]

    def block_of(u):
        return units[u][0] + c * (units[u][1] - units[u][0])

    def slot(u, r, rows):
        if u < 4:
            return w.at[block_of(u), r, rows]
        return w_con.at[r, block_of(u) - 8, rows]

    loads = []
    for u in range(6):
        copy = pltpu.make_async_copy(
            own.at[block_of(u), pl.ds(part, 2 * piece)],
            slot(u, row, pl.ds(part, 2 * piece)),
            load_sem.at[u],
        )
        copy.start()
        loads.append(copy)
    z_peers = [(lax.rem(z + k, 4) * 2 + x, seg) for k in (1, 2, 3)]
    x_peer, y_peer, c_peer = (row + 1 - 2 * x, seg), (row, seg + 2 - 4 * y), (row, seg + 1 - 2 * c)
    cross_peers = [(lax.rem(z + k, 4) * 2 + 1 - x, seg) for k in (1, 2, 3)]
    row_peers = z_peers + cross_peers + [x_peer]
    greet(row_peers + [y_peer, c_peer])
    sent = []

    def go(copy):
        copy.start()
        sent.append(copy)

    small = []
    for i, peer in enumerate(row_peers):
        small.append(remote(cond.at[peer[0]], conds.at[row], small_s.at[i], small_r.at[i], peer))
        small.append(remote(bias, bias_in.at[row], small_s.at[7 + i], small_r.at[7 + i], peer))
    for copy in small:
        go(copy)
    conds[row] = cond[row]
    bias_in[row] = bias[...]

    def to_x():
        return remote(parts.at[:, 1 - x], x_parts, part_s.at[0], part_r.at[0], x_peer)

    def to_z(k):
        src = parts.at[lax.rem(z + k, 4), x]
        return remote(src, z_parts.at[k - 1], part_s.at[k], part_r.at[k], z_peers[k - 1])

    def multiply():
        for copy in small:
            copy.wait_recv()
        left = conds[...].reshape(-1, conds.shape[2])[:, :n].astype(bf16)
        half = w_mod.shape[1] // 2
        upper = lax.broadcasted_iota(jnp.int32, (left.shape[0], 1), 0) % 8 < 4
        for start in range(0, half, width):
            both = jnp.where(
                upper,
                dot(left, w_mod[:, start : start + width]),
                dot(left, w_mod[:, half + start : half + start + width]),
            )
            parts[:, :, :, start : start + width] = both.reshape(4, 2, 8, width)
        go(to_x())
        bias_all[...] = jnp.zeros_like(bias_all)
        for r in range(8):
            rows = slice(16 * max(r - 1, 0), 16 * max(r - 1, 0) + 32)
            bias_all[rows] = bias_all[rows] + bias_in[r].astype(f32)

    def sum_x():
        to_x().wait_recv()
        for level in range(4):
            parts[level, x] = parts[level, x] + x_parts[level]
        for k in (1, 3, 2):
            go(to_z(k))

    def sum_z():
        for k in (1, 3, 2):
            to_z(k).wait_recv()
        total = parts[z, x] + z_parts[0] + z_parts[1] + z_parts[2]
        first = 3 + w_expand // width + 1
        for part_no in range(3):
            cols = slice(part_no * width, (part_no + 1) * width)
            upper = lax.broadcasted_iota(jnp.int32, (8, 1), 0) < 4
            modulation[:, cols] = total[:, cols] + jnp.where(
                upper, bias_row(first + part_no), bias_row(first + 3 + part_no)
            )

    w_expand = 4 * width

    def bias_row(number):
        tall = width // 128
        return jnp.concatenate(
            [bias_all[number * tall + i : number * tall + i + 1, :] for i in range(tall)], axis=1
        )

    def along_z(u, k):
        ref = slot(u, row, pl.ds(part, 2 * piece))
        return remote(ref, ref, z_s.at[u, k - 1], z_r.at[u, k - 1], z_peers[k - 1])

    def along_x(u, k):
        ref = slot(u, far[k] * 2 + x, pl.ds(part, 2 * piece))
        return remote(ref, ref, x_s.at[u, k], x_r.at[u, k], x_peer)

    def along_y(u, k):
        ref = slot(u, pl.ds(far[k] * 2, 2), pl.ds(third, piece))
        return remote(ref, ref, y_s.at[u, k], y_r.at[u, k], y_peer)

    def across(u, k):
        ref = slot(u, pl.ds(far[k] * 2, 2), slice(None))
        return remote(ref, ref, c_s.at[u, k], c_r.at[u, k], c_peer)

    steps = [(u, k) for u in range(6) for k in (0, 1, 3, 2)]
    outs, kept = [], {}

    def keep(name, number, src, dst, sem):
        kept[name, number] = save(src, dst, save_sem.at[sem])

    def finish(name, number=None):
        kept.pop((name, number)).wait()

    def save(src, dst, sem):
        copy = pltpu.make_async_copy(src, dst, sem)
        copy.start()
        return copy

    def step(j):
        if j < len(steps):
            u, k = steps[j]
            if k == 0:
                for later in [0, 1] if u == 0 else [u + 1]:
                    if later < 6:
                        loads[later].wait()
                        for hop in (1, 3, 2):
                            go(along_z(later, hop))
            else:
                along_z(u, k).wait_recv()
            go(along_x(u, k))
        if 0 <= j - 1 < len(steps):
            along_x(*steps[j - 1]).wait_recv()
            go(along_y(*steps[j - 1]))
        if 0 <= j - 2 < len(steps):
            along_y(*steps[j - 2]).wait_recv()
            go(across(*steps[j - 2]))
        if 0 <= j - 3 < len(steps):
            u, k = steps[j - 3]
            across(u, k).wait_recv()
            if k == 2:
                if u < 4:
                    for b in units[u]:
                        outs.append(save(w.at[b], w_out[b], out_sem.at[b]))
                elif u == 5:
                    outs.append(save(w_con, w_con_out, out_sem.at[8]))


    def of_segment(rows, number):
        ids = seg_ids[rows, :]
        base, col = number // 3 * 4, number % 3 * width
        result = jnp.zeros((ids.shape[0], width), f32)
        for s in range(4):
            line = modulation[base + s : base + s + 1, col : col + width]
            result = jnp.where(ids == s, line, result)
        return result

    def tiles(size, body):
        def one(i, carry):
            body(pl.ds(pl.multiple_of(i * size, size), size))
            return carry

        lax.fori_loop(0, count // size, one, 0)

    def matrix(b):
        return w[b].reshape(8 * n, width)

    def norm_one():
        def body(rows):
            normed = layer_rows(tokens[rows, :].astype(f32))
            padded[rows, :] = (
                normed * (1.0 + of_segment(rows, 1)) + of_segment(rows, 0)
            ).astype(bf16)

        tiles(128, body)
        keep("h1", None, padded, h1_out, 0)

    def spread_hidden():
        def one(s, carry):
            slabs[3, s] = spread_rows(starts, padded, s).astype(bf16)
            return carry

        lax.fori_loop(0, 4, one, 0)

    def project(which):
        def one(s, carry):
            result = dot(slabs[3, s], matrix(which))
            if which != 1:
                result = result + bias_row(which // 2)
            slabs[which, s] = result.astype(bf16)
            return carry

        lax.fori_loop(0, 4, one, 0)
        keep("slab", which, slabs.at[which], slab_out.at[which], 1 + which)

    def attend_heads(first, last):
        def one(s, carry):
            attend_slab(
                starts, s, slabs.at[0], slabs.at[1], slabs.at[2], slabs.at[3], range(first, last)
            )
            return carry

        lax.fori_loop(0, 4, one, 0)

    def gather_back():
        finish("h1")
        unspread(starts, slabs.at[3], padded)
        keep("attended", None, padded, att_out, 4)

    def add_projected():
        def body(rows):
            projected = dot(padded[rows, :], matrix(3)) + bias_row(2)
            wide[1, rows, :] = projected
            middle = tokens[rows, :].astype(f32) + of_segment(rows, 2) * projected
            wide[0, rows, :] = middle

        tiles(256, body)
        keep("wide", None, wide.at[1], proj_out, 5)
        keep("middle", None, wide.at[0], mid_out, 6)

    def norm_two():
        def body(rows):
            normed = layer_rows(wide[0, rows, :])
            hidden[rows, :] = (
                normed * (1.0 + of_segment(rows, 4)) + of_segment(rows, 3)
            ).astype(bf16)

        tiles(128, body)
        keep("h2", None, hidden, h2_out, 7)

    def expand_block(j):
        finish("wide")
        if j < 3:
            finish("slab", j)

        def body(i, carry):
            rows = pl.ds(pl.multiple_of(i * SPAN, SPAN), SPAN)
            before = dot(hidden[rows, :], matrix(4 + j)) + bias_row(3 + j)
            wide[1, rows, :] = before
            slabs[j, i] = gelu(before).astype(bf16)
            return carry

        lax.fori_loop(0, count // SPAN, body, 0)
        keep("wide", None, wide.at[1], before_out.at[j], 8 + j)
        keep("act", j, slabs.at[j, pl.ds(0, 3)], act_out.at[:, :, pl.ds(j * width, width)], 12 + j)

    def contract():
        finish("wide")
        finish("attended")

        def body(i, carry):
            rows = pl.ds(pl.multiple_of(i * SPAN, SPAN), SPAN)
            result = dot(slabs[0, i], w_con[0:2].reshape(8 * n, width))
            for q in range(1, 4):
                result = result + dot(slabs[q, i], w_con[2 * q : 2 * q + 2].reshape(8 * n, width))
            result = result + bias_row(7)
            wide[1, rows, :] = result
            padded[rows, :] = (wide[0, rows, :] + of_segment(rows, 5) * result).astype(bf16)
            return carry

        lax.fori_loop(0, count // SPAN, body, 0)
        keep("wide", None, wide.at[1], ff_out, 16)
        keep("out", None, padded, y_out, 17)

    plan = [0, multiply, 1, 2, sum_x, 3, 4, sum_z, 5, norm_one, 6, spread_hidden, 7]
    plan += [partial(project, 0), 8, partial(project, 2), 9, 10, partial(project, 1), 11]
    for first in range(0, 16, 2):
        plan += [partial(attend_heads, first, first + 2)] + ([12 + first // 4] if first % 4 else [])
    plan += [gather_back, 16, add_projected, norm_two, 17]
    plan += [partial(expand_block, 0), 18, partial(expand_block, 1), 19]
    plan += [partial(expand_block, 2), 20, partial(expand_block, 3), 21, 22, 23, 24, 25, 26]
    for item in plan + [contract]:
        if isinstance(item, int):
            step(item)
        else:
            item()
    for copy in sent:
        copy.wait_send()
    for copy in outs + list(kept.values()):
        copy.wait()


def forward_fast(own_parts, cond_silu, bias_low, mod_low, starts, segments, tokens):
    attention, projection, expand, contract = own_parts
    width = projection.shape[1]
    n = attention.shape[0]
    count = tokens.shape[0]
    blocks = [attention[:, j * width : (j + 1) * width] for j in range(3)] + [projection]
    blocks += [expand[:, j * width : (j + 1) * width] for j in range(4)]
    blocks += [contract[j * n : (j + 1) * n] for j in range(4)]
    own = jnp.stack([block.astype(bf16) for block in blocks])
    n_seg = cond_silu.shape[0]
    cond = cond_silu.astype(f32).reshape(n_seg, 8, n).transpose(1, 0, 2)
    cond = jnp.pad(jnp.concatenate([cond, cond], axis=1), ((0, 0), (0, 0), (0, 256 - n)))
    row = lax.axis_index("rows")
    window = 128 * 16 * jnp.maximum(row - 1, 0)
    bias = lax.dynamic_update_slice(
        jnp.zeros(4096, bf16), bias_low, (row * bias_low.shape[0] - window,)
    ).reshape(32, 128)
    sems = pltpu.SemaphoreType.DMA

    def shape(dtype, *dims):
        return jax.ShapeDtypeStruct(dims, dtype)

    outs = pl.pallas_call(
        forward_kernel,
        out_shape=(shape(bf16, 8, n, width),) * 8
        + (
            shape(bf16, 8, 4, n, width),
            shape(f32, 8, 3 * width),
            shape(bf16, count, width),
            shape(bf16, 3, 4, SPAN, width),
            shape(bf16, count, width),
            shape(f32, count, width),
            shape(f32, count, width),
            shape(bf16, count, width),
            shape(f32, 4, count, width),
            shape(bf16, count // SPAN, SPAN, 4 * width),
            shape(f32, count, width),
            shape(bf16, count, width),
        ),
        in_specs=[ANY, VM, VM, VM, SM, VM, VM],
        out_specs=(ANY,) * 9 + (VM,) + (ANY,) * 10,
        scratch_shapes=[
            pltpu.VMEM((8, 8, n, width), bf16),
            pltpu.VMEM((8, 4, n, width), bf16),
            pltpu.VMEM((8, 8, 256), f32),
            pltpu.VMEM((8, 32, 128), bf16),
            pltpu.VMEM((128, 128), f32),
            pltpu.VMEM((4, 2, 8, 3 * width), f32),
            pltpu.VMEM((4, 8, 3 * width), f32),
            pltpu.VMEM((3, 8, 3 * width), f32),
            pltpu.VMEM((4, 4, SPAN, width), bf16),
            pltpu.VMEM((count, width), bf16),
            pltpu.VMEM((2, count, width), f32),
            pltpu.VMEM((count, width), bf16),
            sems((14,)),
            sems((14,)),
            sems((4,)),
            sems((4,)),
        ]
        + [sems((6, 3))] * 2
        + [sems((6, 4))] * 6
        + [sems((6,)), sems((9,)), sems((18,))],
        compiler_params=pltpu.CompilerParams(
            collective_id=0, has_side_effects=True, vmem_limit_bytes=60 << 20
        ),
        name="forward",
    )(own, cond, bias, mod_low, starts, segments[:, None], tokens)
    w = [block.reshape(8 * n, width) for block in outs[:8]]
    modulation = jnp.concatenate([outs[9][:n_seg], outs[9][n_seg:]], axis=1)
    weights = (tuple(w[:3]), w[3], tuple(w[4:]), outs[8].reshape(32 * n, width))
    h1, slabs, attended, projected, middle, h2, before, act, feedforward, output = outs[10:]
    saved = (
        modulation,
        h1,
        (slabs[0], slabs[1], slabs[2]),
        attended,
        projected,
        middle,
        h2,
        [before[j] for j in range(4)],
        act.reshape(count, 4 * width),
        feedforward,
    )
    return output, saved, weights


def of_tokens(onehot, modulation, width):
    rows = sum(onehot[:, s : s + 1] * modulation[s] for s in range(onehot.shape[1]))
    return [rows[:, j * width : (j + 1) * width] for j in range(6)]


def forward_plain(own_parts, cond_silu, bias_low, mod_low, starts, segments, tokens):
    def whole(part):
        return lax.all_gather(part.astype(bf16), "rows", axis=0, tiled=True)

    attention, projection, expand, contract = own_parts
    width = projection.shape[1]
    att, w_proj, exp, w_con = map(whole, own_parts)
    w_att = tuple(att[:, j * width : (j + 1) * width] for j in range(3))
    w_exp = tuple(exp[:, j * width : (j + 1) * width] for j in range(4))
    shard = mod_low.shape[0]
    cond = lax.all_gather(cond_silu, "rows", axis=0, tiled=True)
    cond = lax.dynamic_slice_in_dim(cond, lax.axis_index("rows") * shard, shard, axis=1)
    modulation = lax.psum_scatter(dot(cond, mod_low), "rows", scatter_dimension=0, tiled=True)
    biases = whole(bias_low).astype(f32)
    bias = [biases[j * width : (j + 1) * width] for j in range(14)]
    modulation = modulation + biases[8 * width :]
    onehot = (segments[:, None] == jnp.arange(cond_silu.shape[0])[None, :]).astype(f32)
    shift_one, scale_one, gate_one, shift_two, scale_two, gate_two = of_tokens(
        onehot, modulation, width
    )
    wide = tokens.astype(f32)
    hidden_one = (layer_norm(wide)[0] * (1.0 + scale_one) + shift_one).astype(bf16)
    query = (dot(hidden_one, w_att[0]) + bias[0]).astype(bf16)
    key = dot(hidden_one, w_att[1]).astype(bf16)
    value = (dot(hidden_one, w_att[2]) + bias[1]).astype(bf16)
    attended, *slabs = attend(starts, query, key, value)
    projected = dot(attended, w_proj) + bias[2]
    middle = wide + gate_one * projected
    hidden_two = (layer_norm(middle)[0] * (1.0 + scale_two) + shift_two).astype(bf16)
    before = [dot(hidden_two, part) + bias[3 + j] for j, part in enumerate(w_exp)]
    activated = jnp.concatenate([gelu(part).astype(bf16) for part in before], axis=1)
    feedforward = dot(activated, w_con) + bias[7]
    output = (middle + gate_two * feedforward).astype(bf16)
    saved = (
        modulation,
        hidden_one,
        slabs,
        attended,
        projected,
        middle,
        hidden_two,
        before,
        activated,
        feedforward,
    )
    return output, saved, (w_att, w_proj, w_exp, w_con)


def reduce_kernel(
    blocks, out, d, y_in, x_in, z_in, total, y2_in, grad, load, y_s, y_r, x_s, x_r, z_s, z_r, y2_s, y2_r, c_s, c_r, store
):
    row, seg = lax.axis_index("rows"), lax.axis_index("seg")
    x, z = row % 2, row // 2
    y, c = seg // 2, seg % 2
    units, _, n, width = blocks.shape
    piece = n // 3
    part = pl.multiple_of(y * piece, piece)
    mine = pl.multiple_of(y * 2 * piece, piece)
    theirs = pl.multiple_of((1 - y) * 2 * piece, piece)
    level = [lax.rem(z + k, 4) for k in range(4)]
    z_peers = [(level[k] * 2 + x, seg) for k in range(4)]
    x_peer, y_peer, c_peer = (row + 1 - 2 * x, seg), (row, seg + 2 - 4 * y), (row, seg + 1 - 2 * c)
    loads = []
    for u in range(units):
        copy = pltpu.make_async_copy(blocks.at[u], d.at[u], load.at[u])
        copy.start()
        loads.append(copy)
    greet(z_peers[1:] + [x_peer, y_peer, c_peer])
    sent = []

    def add(*terms):
        result = terms[0].astype(f32)
        for term in terms[1:]:
            result = result + term.astype(f32)
        return result.astype(bf16)

    def to_y(u, k):
        src = d.at[u, pl.ds(level[k] * 2, 2), pl.ds(theirs, piece)]
        return remote(src, y_in.at[u, k], y_s.at[u, k], y_r.at[u, k], y_peer)

    def to_x(u, k):
        src = d.at[u, level[k] * 2 + 1 - x, pl.ds(part, 2 * piece)]
        return remote(src, x_in.at[u, k], x_s.at[u, k], x_r.at[u, k], x_peer)

    def to_z(u, k):
        src = d.at[u, level[k] * 2 + x, pl.ds(part, 2 * piece)]
        return remote(src, z_in.at[u, k - 1], z_s.at[u, k - 1], z_r.at[u, k - 1], z_peers[k])

    def to_y_again(u):
        return remote(total.at[u], y2_in.at[u], y2_s.at[u], y2_r.at[u], y_peer)

    def to_core(u):
        ref = grad.at[u, c]
        return remote(ref, ref, c_s.at[u], c_r.at[u], c_peer)

    def go(copy):
        copy.start()
        sent.append(copy)

    steps = [(u, k) for u in range(units) for k in (1, 3, 2, 0)]
    ahead = 5
    outs = []

    def first(j):
        u, k = steps[j]
        if k == 1:
            loads[u].wait()
        go(to_y(u, k))

    for j in range(ahead):
        first(j)
    for j in range(len(steps) + 8):
        if j + ahead < len(steps):
            first(j + ahead)
        if j < len(steps):
            u, k = steps[j]
            to_y(u, k).wait_recv()
            for side in range(2):
                r = level[k] * 2 + side
                d[u, r, pl.ds(mine, piece)] = add(d[u, r, pl.ds(mine, piece)], y_in[u, k, side])
            go(to_x(u, k))
        if 0 <= j - 1 < len(steps):
            u, k = steps[j - 1]
            to_x(u, k).wait_recv()
            r = level[k] * 2 + x
            d[u, r, pl.ds(part, 2 * piece)] = add(d[u, r, pl.ds(part, 2 * piece)], x_in[u, k])
            if k:
                go(to_z(u, k))
        if j >= 3 and (j - 3) % 4 == 2 and (j - 3) // 4 < units:
            u = (j - 3) // 4
            for k in (1, 3, 2):
                to_z(u, k).wait_recv()
            total[u] = add(d[u, row, pl.ds(part, 2 * piece)], z_in[u, 0], z_in[u, 1], z_in[u, 2])
            go(to_y_again(u))
        if j >= 4 and (j - 4) % 4 == 2 and (j - 4) // 4 < units:
            u = (j - 4) // 4
            to_y_again(u).wait_recv()
            here, there = y * piece, (1 - y) * piece
            here, there = pl.multiple_of(here, piece), pl.multiple_of(there, piece)
            grad[u, c, pl.ds(mine, piece)] = total[u, pl.ds(here, piece)]
            grad[u, c, pl.ds(theirs, piece)] = y2_in[u, pl.ds(there, piece)]
            grad[u, c, pl.ds(piece, piece)] = add(
                total[u, pl.ds(there, piece)], y2_in[u, pl.ds(here, piece)]
            )
            go(to_core(u))
        if j >= 5 and (j - 5) % 4 == 2 and (j - 5) // 4 < units:
            u = (j - 5) // 4
            to_core(u).wait_recv()
            copy = pltpu.make_async_copy(grad.at[u], out.at[u], store.at[u])
            copy.start()
            outs.append(copy)
    for copy in sent:
        copy.wait_send()
    for copy in outs:
        copy.wait()


def reduce_units(blocks, number):
    units = len(blocks)
    rows, width = blocks[0].shape
    n = rows // 8
    sems = pltpu.SemaphoreType.DMA

    def space(*shape):
        return pltpu.VMEM(shape + (width,), bf16)

    return pl.pallas_call(
        reduce_kernel,
        out_shape=jax.ShapeDtypeStruct((units, 2, n, width), bf16),
        in_specs=[ANY],
        out_specs=ANY,
        scratch_shapes=[
            space(units, 8, n),
            space(units, 4, 2, n // 3),
            space(units, 4, 2 * n // 3),
            space(units, 3, 2 * n // 3),
            space(units, 2 * n // 3),
            space(units, 2 * n // 3),
            space(units, 2, n),
            sems((units,)),
        ]
        + [sems((units, 4))] * 4
        + [sems((units, 3))] * 2
        + [sems((units,))] * 5,
        compiler_params=pltpu.CompilerParams(
            collective_id=number, has_side_effects=True, vmem_limit_bytes=48 << 20
        ),
        name=f"reduce_{number}",
    )(jnp.stack(blocks).reshape(units, 8, n, width))


def reduce_fast(early, hidden_one, attended, hidden_two, activated, back_feed, back_before):
    x, y, z, c = place()
    width = hidden_one.shape[1]

    def pick(first, second, which):
        return jnp.where(which == 0, first, second)

    act = activated.T.reshape(8, 4, width // 8, activated.shape[0])
    feed_far = over_core(back_feed)
    blocks = []
    for unit in range(2):
        mine, there = (
            lax.dynamic_index_in_dim(act, 2 * unit + which, 1, False).reshape(width, -1)
            for which in (c, 1 - c)
        )
        far = over_core(there)
        blocks.append((dot(mine, back_feed) + dot(far, feed_far)).astype(bf16))
    two_far = over_core(hidden_two)
    for unit in range(2):
        first, second = (
            back_before[:, (2 * unit + j) * width : (2 * unit + j + 1) * width] for j in range(2)
        )
        far = over_core(pick(second, first, c))
        blocks.append(
            (outer(hidden_two, pick(first, second, c)) + outer(two_far, far)).astype(bf16)
        )
    big = reduce_units(blocks, 1).astype(f32)
    one_far, att_far = over_core(hidden_one), over_core(attended)

    def late(back_query, back_key, back_value, back_project):
        far = over_core(pick(back_project, back_key, c))
        left, left_far = pick(hidden_one, attended, c), pick(one_far, att_far, c)
        first = (outer(left, pick(back_key, back_project, c)) + outer(left_far, far)).astype(bf16)
        far = over_core(pick(back_value, back_query, c))
        second = (
            outer(hidden_one, pick(back_query, back_value, c)) + outer(one_far, far)
        ).astype(bf16)
        small = reduce_units([first, second], 2).astype(f32)
        con = big[0:2].reshape(-1, width)
        exp = jnp.concatenate([big[2, 0], big[2, 1], big[3, 0], big[3, 1]], axis=1)
        att = jnp.concatenate([small[1, 0], small[0, 0], small[1, 1]], axis=1)
        return att, small[0, 1], exp, con

    return late


def reduce_plain(early, hidden_one, attended, hidden_two, activated, back_feed, back_before):
    def total(left, right):
        part = lax.psum_scatter(
            outer(left, right).astype(bf16), "rows", scatter_dimension=0, tiled=True
        )
        return lax.psum(part.astype(f32), "seg")

    con = total(activated, back_feed)
    exp = total(hidden_two, back_before)

    def late(back_query, back_key, back_value, back_project):
        att = total(hidden_one, jnp.concatenate([back_query, back_key, back_value], axis=1))
        return att, total(attended, back_project), exp, con

    return late


def on_device(
    fast,
    tokens,
    condition,
    segment_ids,
    cotangent,
    modulation_master,
    modulation_first,
    modulation_second,
    attention_master,
    attention_first,
    attention_second,
    projection_master,
    projection_first,
    projection_second,
    expand_master,
    expand_first,
    expand_second,
    contract_master,
    contract_first,
    contract_second,
    bias_master,
    bias_first,
    bias_second,
):
    width = tokens.shape[1]
    hidden = expand_master.shape[1]
    shard = modulation_master.shape[0]
    n_seg = condition.shape[1]
    row = lax.axis_index("rows")
    segments = segment_ids[0]
    onehot = (segments[:, None] == jnp.arange(n_seg, dtype=jnp.int32)[None, :]).astype(f32)
    starts = jnp.sum(
        segments[:, None] < jnp.arange(n_seg + 1, dtype=jnp.int32)[None, :], axis=0, dtype=jnp.int32
    )
    tokens_wide = tokens.astype(f32)
    upstream = cotangent.astype(f32)

    cond_silu = jax.nn.silu(condition[0].astype(f32)).astype(bf16)
    forward = forward_fast if fast else forward_plain
    output, saved, (w_att, w_proj, w_exp, w_con) = forward(
        (attention_master, projection_master, expand_master, contract_master),
        cond_silu,
        bias_master.astype(bf16),
        modulation_master.astype(bf16),
        starts,
        segments,
        tokens,
    )
    (
        modulation,
        hidden_one,
        slabs,
        attended,
        projected,
        middle,
        hidden_two,
        before,
        activated,
        feedforward,
    ) = saved
    shift_one, scale_one, gate_one, shift_two, scale_two, gate_two = of_tokens(
        onehot, modulation, width
    )
    normed_one, inverse_one = layer_norm(tokens_wide)
    normed_two, inverse_two = layer_norm(middle)

    back_gate_two = upstream * feedforward
    back_feed = (upstream * gate_two).astype(bf16)
    back_before = []
    for j, part in enumerate(before):
        back_active = back_dot(back_feed, w_con[j * width : (j + 1) * width])
        back_before.append(jax.vjp(gelu, part)[1](back_active)[0].astype(bf16))
    back_before = jnp.concatenate(back_before, axis=1)
    reduce = reduce_fast if fast else reduce_plain
    late = reduce(None, hidden_one, attended, hidden_two, activated, back_feed, back_before)
    back_hidden_two = sum(
        back_dot(back_before[:, j * width : (j + 1) * width], w_exp[j]) for j in range(4)
    )
    back_middle = upstream + norm_back(back_hidden_two * (1.0 + scale_two), normed_two, inverse_two)
    back_gate_one = back_middle * projected
    back_project = (back_middle * gate_one).astype(bf16)
    back_attend = back_dot(back_project, w_proj).astype(bf16)
    back_query, back_key, back_value = attend_back(starts, *slabs, back_attend)
    grad_att, grad_proj, grad_exp, grad_con = late(back_query, back_key, back_value, back_project)
    back_hidden_one = (
        back_dot(back_query, w_att[0]) + back_dot(back_key, w_att[1]) + back_dot(back_value, w_att[2])
    )
    back_tokens = back_middle + norm_back(
        back_hidden_one * (1.0 + scale_one), normed_one, inverse_one
    )
    back_modulation = jnp.concatenate(
        [
            outer(onehot, part, highest)
            for part in (
                back_hidden_one,
                back_hidden_one * normed_one,
                back_gate_one,
                back_hidden_two,
                back_hidden_two * normed_two,
                back_gate_two,
            )
        ],
        axis=1,
    )
    columns = jnp.concatenate(
        [
            jnp.sum(part.astype(f32), axis=0)
            for part in (back_query, back_value, back_project, back_before, back_feed)
        ]
    )
    payload = jnp.concatenate(
        [back_modulation, columns.reshape(n_seg, -1), cond_silu.astype(f32)], axis=1
    )
    everyone = lax.all_gather(payload, ("rows", "seg"), axis=0, tiled=True)
    mod_all = everyone[:, : 6 * width]
    cond_rows = lax.dynamic_slice_in_dim(
        everyone, everyone.shape[1] - width + row * shard, shard, axis=1
    )
    grad_mod = outer(cond_rows, mod_all, highest)
    devices = everyone.shape[0] // n_seg
    rest = jnp.sum(everyone[:, 6 * width : -width].reshape(devices, -1), axis=0)
    grad_bias = lax.dynamic_slice_in_dim(
        jnp.concatenate([rest, jnp.sum(mod_all, axis=0)]),
        row * bias_master.shape[0],
        bias_master.shape[0],
    )
    results = [
        adam_update(*operands)
        for operands in (
            (grad_mod, modulation_master, modulation_first, modulation_second),
            (grad_att, attention_master, attention_first, attention_second),
            (grad_proj, projection_master, projection_first, projection_second),
            (grad_exp, expand_master, expand_first, expand_second),
            (grad_con, contract_master, contract_first, contract_second),
            (grad_bias, bias_master, bias_first, bias_second),
        )
    ]
    flat = tuple((item for result in results for item in result))
    return (output, back_tokens.astype(bf16)) + flat


def solution(mesh):
    both = ("rows", "seg")
    fast = mesh.shape["rows"] == 8 and mesh.shape["seg"] == 4
    token, matrix, vector = P(both, None), P("rows", None), P("rows")
    in_specs = (token, P(both, None, None), token, token) + (matrix,) * 15 + (vector,) * 3
    out_specs = (token, token) + (matrix,) * 15 + (vector,) * 3
    return jax.shard_map(
        partial(on_device, fast),
        mesh=mesh,
        in_specs=in_specs,
        out_specs=out_specs,
        check_vma=False,
    )
```

```python
from functools import partial

import jax
import jax.numpy as jnp
from jax import lax
from jax.experimental import pallas as pl
from jax.experimental.pallas import tpu as pltpu
from jax.sharding import PartitionSpec as P

HEAD_DIM = 72
STEP = 10
SPAN = 256
EXP_SCALE = HEAD_DIM**-0.5 * 1.4426950408889634

bf16 = jnp.bfloat16
f32 = jnp.float32
highest = lax.Precision.HIGHEST
beta_first = 0.9
beta_second = 0.999
learning = 0.06
weight_decay = 0.1
adam_epsilon = 1e-08
norm_epsilon = 1e-06

ROW_X = [(z * 2 + x, z * 2 + 1 - x) for z in range(4) for x in range(2)]
ROW_Z = [
    [(z * 2 + x, (z + k) % 4 * 2 + x) for z in range(4) for x in range(2)] for k in range(4)
]
SEG_Y = [(y * 2 + c, (1 - y) * 2 + c) for y in range(2) for c in range(2)]
SEG_C = [(y * 2 + c, y * 2 + 1 - c) for y in range(2) for c in range(2)]


def over_x(v):
    return lax.ppermute(v, "rows", ROW_X)


def over_z(v, k):
    return lax.ppermute(v, "rows", ROW_Z[k])


def over_y(v):
    return lax.ppermute(v, "seg", SEG_Y)


def over_core(v):
    return lax.ppermute(v, "seg", SEG_C)


def place():
    row = lax.axis_index("rows")
    seg = lax.axis_index("seg")
    return row % 2, seg // 2, row // 2, seg % 2


def layer_norm(values):
    center = values - jnp.mean(values, axis=-1, keepdims=True)
    inverse = lax.rsqrt(jnp.mean(center * center, axis=-1, keepdims=True) + norm_epsilon)
    return (center * inverse, inverse)


def norm_back(upstream, normed, inverse):
    return inverse * (
        upstream
        - jnp.mean(upstream, axis=-1, keepdims=True)
        - normed * jnp.mean(upstream * normed, axis=-1, keepdims=True)
    )


def outer(left, right, precision=None):
    return lax.dot_general(
        left,
        right,
        (((0,), (0,)), ((), ())),
        precision=precision,
        preferred_element_type=f32,
    )


def dot(left, right):
    return jnp.dot(left, right, preferred_element_type=f32)


def back_dot(left, right):
    return lax.dot_general(left, right, (((1,), (1,)), ((), ())), preferred_element_type=f32)


def spread_rows(starts, source, s):
    rows = source.shape[0]
    row = lax.broadcasted_iota(jnp.int32, (SPAN, rows), 0) + starts[s]
    col = lax.broadcasted_iota(jnp.int32, (SPAN, rows), 1)
    pick = jnp.where((col == row) & (row < starts[s + 1]), 1.0, 0.0).astype(bf16)
    return dot(pick, source[...])

def spread(starts, source, out):
    def one(s,_):
        out[s]=spread_rows(starts,source,s).astype(bf16)
        return 0
    lax.fori_loop(0,out.shape[0],one,0)

def home_rows(starts, i, flat, n):
    row = lax.broadcasted_iota(jnp.int32, (SPAN, 1), 0) + i * SPAN
    home = row
    for s in range(1, n):
        home = home + jnp.where(row >= starts[s], SPAN - (starts[s] - starts[s - 1]), 0)
    pick = jnp.where(lax.broadcasted_iota(jnp.int32, (SPAN, n * SPAN), 1) == home, 1.0, 0.0)
    return dot(pick.astype(bf16), flat)


def unspread(starts, slabs, out):
    n, _, width = slabs.shape

    def one(i, carry):
        place = pl.ds(pl.multiple_of(i * SPAN, SPAN), SPAN)
        flat = slabs[...].reshape(n * SPAN, width)
        out[place, :] = home_rows(starts, i, flat, n).astype(bf16)
        return carry

    lax.fori_loop(0, out.shape[0] // SPAN, one, 0)


def attend_slab(starts, s, qs, ks, vs, os, heads):
    length = starts[s + 1] - starts[s]
    outside = jnp.where(lax.broadcasted_iota(jnp.int32, (SPAN, 1), 0) < length, 0.0, -1e30)
    for h in heads:
        cols = slice(h * HEAD_DIM, (h + 1) * HEAD_DIM)
        score = back_dot(ks[s, :, cols], qs[s, :, cols]) + outside
        power = jnp.exp2((score - jnp.max(score, axis=0, keepdims=True)) * EXP_SCALE)
        soft = (power * (1.0 / jnp.sum(power, axis=0, keepdims=True))).astype(bf16)
        os[s, :, cols] = outer(soft, vs[s, :, cols]).astype(bf16)


def attend_kernel(starts, q, k, v, out, qs, ks, vs, os):
    for src, dst in ((q, qs), (k, ks), (v, vs)):
        spread(starts, src, dst)

    def seg(s, carry):
        attend_slab(starts, s, qs, ks, vs, os, range(qs.shape[2] // HEAD_DIM))
        return carry

    lax.fori_loop(0, qs.shape[0], seg, 0)
    unspread(starts, os, out)

def back_slab(starts, s, qs, ks, vs, ups, dqs, dks, dvs, heads):
    scale = HEAD_DIM**-0.5
    length = starts[s + 1] - starts[s]
    outside = jnp.where(lax.broadcasted_iota(jnp.int32, (SPAN, 1), 0) < length, 0.0, -1e30)
    for h in heads:
        cols = slice(h * HEAD_DIM, (h + 1) * HEAD_DIM)
        query, key, value, upstream = (part[s, :, cols] for part in (qs, ks, vs, ups))
        score = back_dot(key, query) + outside
        power = jnp.exp2((score - jnp.max(score, axis=0, keepdims=True)) * EXP_SCALE)
        soft = power * (1.0 / jnp.sum(power, axis=0, keepdims=True))
        back_soft = back_dot(value, upstream)
        mean = jnp.sum(back_soft * soft, axis=0, keepdims=True)
        back_score = (soft * (back_soft - mean)).astype(bf16)
        dvs[s, :, cols] = dot(soft.astype(bf16), upstream).astype(bf16)
        dks[s, :, cols] = (dot(back_score, query) * scale).astype(bf16)
        dqs[s, :, cols] = (outer(back_score, key) * scale).astype(bf16)


class Slab:
    def __init__(self, ref, slot, rows):
        self.ref, self.slot, self.rows = ref, slot, rows

    def __getitem__(self, index):
        return self.ref[self.slot, self.rows, index[2]]

    def __setitem__(self, index, value):
        self.ref[self.slot, self.rows, index[2]] = value


def back_slab_flat(starts, s, rows, qs, ks, vs, space, heads):
    dqs, dks, dvs, ups = (Slab(space, slot, rows) for slot in range(4))
    back_slab(starts, s, qs, ks, vs, ups, dqs, dks, dvs, heads)


def back_kernel(starts, qs, ks, vs, up, dq, dk, dv, ups, dqs, dks, dvs):
    spread(starts, up, ups)

    def seg(s, carry):
        back_slab(
            starts, s, qs, ks, vs, ups, dqs, dks, dvs, range(qs.shape[2] // HEAD_DIM)
        )
        return carry

    lax.fori_loop(0, qs.shape[0], seg, 0)
    for slabs, out in ((dqs, dq), (dks, dk), (dvs, dv)):
        unspread(starts, slabs, out)


VM = pl.BlockSpec(memory_space=pltpu.VMEM)
SM = pl.BlockSpec(memory_space=pltpu.SMEM)
ANY = pl.BlockSpec(memory_space=pl.ANY)
def attend(starts,q,k,v):
    n=starts.shape[0]-1; rows,width=q.shape
    slab=jax.ShapeDtypeStruct((n,SPAN,width),bf16)
    return pl.pallas_call(attend_kernel,out_shape=(jax.ShapeDtypeStruct(q.shape,bf16),slab,slab,slab),
        in_specs=[SM,VM,VM,VM],out_specs=(VM,)*4,
        scratch_shapes=[pltpu.VMEM((n,SPAN,width),bf16)],
        compiler_params=pltpu.CompilerParams(vmem_limit_bytes=56<<20),
        cost_estimate=pl.CostEstimate(flops=2*2*16*n*SPAN*SPAN*128,bytes_accessed=rows*width*14,transcendentals=16*n*SPAN*SPAN),name="attend")(starts,q,k,v)
def attend_back(starts,qs,ks,vs,up):
    n=starts.shape[0]-1; rows,width=up.shape
    slab=pltpu.VMEM((n,SPAN,width),bf16); o=jax.ShapeDtypeStruct(up.shape,bf16)
    return pl.pallas_call(back_kernel,out_shape=(o,o,o),
        in_specs=[SM,VM,VM,VM,VM],out_specs=(VM,)*3,
        scratch_shapes=[slab]*4,
        compiler_params=pltpu.CompilerParams(vmem_limit_bytes=56<<20),
        cost_estimate=pl.CostEstimate(flops=5*2*16*n*SPAN*SPAN*128,bytes_accessed=rows*width*14,transcendentals=16*n*SPAN*SPAN),name="attend_back")(starts,qs,ks,vs,up)


def adam_update(gradient, master, first, second):
    first_new = beta_first * first + (1.0 - beta_first) * gradient
    second_new = beta_second * second + (1.0 - beta_second) * gradient * gradient
    first_hat = first_new / (1.0 - beta_first**STEP)
    second_hat = second_new / (1.0 - beta_second**STEP)
    master_new = master - learning * (
        first_hat / (jnp.sqrt(second_hat) + adam_epsilon) + weight_decay * master
    )
    return (master_new, first_new, second_new)


def gelu(v):
    return 0.5 * v * (1.0 + jnp.tanh(0.7978845608028654 * (v + 0.044715 * (v * v * v))))


def remote(src, dst, send, recv, device):
    return pltpu.make_async_remote_copy(
        src_ref=src,
        dst_ref=dst,
        send_sem=send,
        recv_sem=recv,
        device_id=device,
        device_id_type=pl.DeviceIdType.MESH,
    )


def greet(peers):
    barrier = pltpu.get_barrier_semaphore()
    for peer in peers:
        pl.semaphore_signal(
            barrier, inc=1, device_id=peer, device_id_type=pl.DeviceIdType.MESH
        )
    pl.semaphore_wait(barrier, len(peers))


def layer_rows(values):
    center = values - jnp.mean(values, axis=-1, keepdims=True)
    return center * lax.rsqrt(jnp.mean(center * center, axis=-1, keepdims=True) + norm_epsilon)


def forward_kernel(
    att_low, proj_low, exp_low, con_low, cond, bias, w_mod, starts, seg_ids, tokens, *refs
):
    w_out, con_out, slab_out, before_out = refs[:8], refs[8:12], refs[12:15], refs[15:19]
    modulation, pair_out, proj_out, mid_out, h2_out, act_out, ff_out, y_out = refs[19:27]
    rest = refs[27:]
    w, w_con, conds, bias_in, bias_all, parts, x_parts, z_parts = rest[:8]
    slabs, padded, wide, hidden, turned = rest[8:13]
    small_s, small_r, part_s, part_r = rest[13:17]
    z_s, z_r, x_s, x_r, y_s, y_r, c_s, c_r, load_sem, out_sem, save_sem = rest[17:]
    row, seg = lax.axis_index("rows"), lax.axis_index("seg")
    x, z = row % 2, row // 2
    y, c = seg // 2, seg % 2
    n, width = proj_low.shape
    count = tokens.shape[0]
    units = ((0, 2), (1, 3), (4, 5), (6, 7), (8, 9), (10, 11))
    piece = n // 3
    part = pl.multiple_of(y * piece, piece)
    third = pl.multiple_of(y * 2 * piece, piece)
    far = [lax.rem(z + 4 - k, 4) for k in range(4)]

    def block_of(u):
        return units[u][0] + c * (units[u][1] - units[u][0])

    def slot(u, r, rows):
        if u < 4:
            return w.at[block_of(u), r, rows]
        return w_con.at[r, block_of(u) - 8, rows]

    def columns(number):
        return pl.ds(pl.multiple_of(number * width, width), width)

    mine = pl.ds(part, 2 * piece)
    own = (
        att_low.at[mine, columns(2 * c)],
        None,
        exp_low.at[mine, columns(c)],
        exp_low.at[mine, columns(2 + c)],
        con_low.at[pl.ds(pl.multiple_of(c * n + part, 16), 2 * piece)],
        con_low.at[pl.ds(pl.multiple_of((2 + c) * n + part, 16), 2 * piece)],
    )
    loads = []
    for u in range(6):
        dst = slot(u, row, mine)
        if u != 1:
            copy = pltpu.make_async_copy(own[u], dst, load_sem.at[u])
            copy.start()
        else:
            two = (att_low.at[mine, columns(1)], proj_low.at[mine])
            for core in range(2):

                @pl.when(c == core)
                def _():
                    pltpu.make_async_copy(two[core], dst, load_sem.at[u]).start()

            copy = pltpu.make_async_copy(two[1], dst, load_sem.at[u])
        loads.append(copy)
    z_peers = [(lax.rem(z + k, 4) * 2 + x, seg) for k in (1, 2, 3)]
    x_peer, y_peer, c_peer = (row + 1 - 2 * x, seg), (row, seg + 2 - 4 * y), (row, seg + 1 - 2 * c)
    cross_peers = [(lax.rem(z + k, 4) * 2 + 1 - x, seg) for k in (1, 2, 3)]
    row_peers = z_peers + cross_peers + [x_peer]
    greet(row_peers + [y_peer, c_peer])
    sent = []

    def go(copy):
        copy.start()
        sent.append(copy)

    small = []
    for i, peer in enumerate(row_peers):
        small.append(remote(cond.at[peer[0]], conds.at[row], small_s.at[i], small_r.at[i], peer))
        small.append(remote(bias, bias_in.at[row], small_s.at[7 + i], small_r.at[7 + i], peer))
    for copy in small:
        go(copy)
    conds[row] = cond[row]
    bias_in[row] = bias[...]

    def to_x():
        return remote(parts.at[:, 1 - x], x_parts, part_s.at[0], part_r.at[0], x_peer)

    def to_z(k):
        src = parts.at[lax.rem(z + k, 4), x]
        return remote(src, z_parts.at[k - 1], part_s.at[k], part_r.at[k], z_peers[k - 1])

    def multiply():
        for copy in small:
            copy.wait_recv()
        left = conds[...].reshape(-1, conds.shape[2])[:, :n].astype(bf16)
        half = w_mod.shape[1] // 2
        upper = lax.broadcasted_iota(jnp.int32, (left.shape[0], 1), 0) % 8 < 4
        for start in range(0, half, width):
            both = jnp.where(
                upper,
                dot(left, w_mod[:, start : start + width]),
                dot(left, w_mod[:, half + start : half + start + width]),
            )
            parts[:, :, :, start : start + width] = both.reshape(4, 2, 8, width)
        go(to_x())
        bias_all[...] = jnp.zeros_like(bias_all)
        for r in range(8):
            rows = slice(16 * max(r - 1, 0), 16 * max(r - 1, 0) + 32)
            bias_all[rows] = bias_all[rows] + bias_in[r].astype(f32)

    def sum_x():
        to_x().wait_recv()
        for level in range(4):
            parts[level, x] = parts[level, x] + x_parts[level]
        for k in (1, 3, 2):
            go(to_z(k))

    def sum_z():
        for k in (1, 3, 2):
            to_z(k).wait_recv()
        total = parts[z, x] + z_parts[0] + z_parts[1] + z_parts[2]
        first = 3 + w_expand // width + 1
        for part_no in range(3):
            cols = slice(part_no * width, (part_no + 1) * width)
            upper = lax.broadcasted_iota(jnp.int32, (8, 1), 0) < 4
            modulation[:, cols] = total[:, cols] + jnp.where(
                upper, bias_row(first + part_no), bias_row(first + 3 + part_no)
            )

    w_expand = 4 * width

    def bias_row(number):
        tall = width // 128
        return jnp.concatenate(
            [bias_all[number * tall + i : number * tall + i + 1, :] for i in range(tall)], axis=1
        )

    def along_z(u, k):
        ref = slot(u, row, pl.ds(part, 2 * piece))
        return remote(ref, ref, z_s.at[u, k - 1], z_r.at[u, k - 1], z_peers[k - 1])

    def along_x(u, k):
        ref = slot(u, far[k] * 2 + x, pl.ds(part, 2 * piece))
        return remote(ref, ref, x_s.at[u, k], x_r.at[u, k], x_peer)

    def along_y(u, k):
        ref = slot(u, pl.ds(far[k] * 2, 2), pl.ds(third, piece))
        return remote(ref, ref, y_s.at[u, k], y_r.at[u, k], y_peer)

    def across(u, k):
        ref = slot(u, pl.ds(far[k] * 2, 2), slice(None))
        return remote(ref, ref, c_s.at[u, k], c_r.at[u, k], c_peer)

    steps = [(u, k) for u in range(6) for k in (0, 1, 3, 2)]
    outs, kept = [], {}

    def keep(name, number, src, dst, sem):
        kept[name, number] = save(src, dst, save_sem.at[sem])

    def finish(name, number=None):
        kept.pop((name, number)).wait()

    def save(src, dst, sem):
        copy = pltpu.make_async_copy(src, dst, sem)
        copy.start()
        return copy

    def step(j):
        if j < len(steps):
            u, k = steps[j]
            if k == 0:
                for later in [0, 1] if u == 0 else [u + 1]:
                    if later < 6:
                        loads[later].wait()
                        for hop in (1, 3, 2):
                            go(along_z(later, hop))
            else:
                along_z(u, k).wait_recv()
            go(along_x(u, k))
        if 0 <= j - 1 < len(steps):
            along_x(*steps[j - 1]).wait_recv()
            go(along_y(*steps[j - 1]))
        if 0 <= j - 2 < len(steps):
            along_y(*steps[j - 2]).wait_recv()
            go(across(*steps[j - 2]))
        if 0 <= j - 3 < len(steps):
            u, k = steps[j - 3]
            across(u, k).wait_recv()
            if k == 2:
                if u < 4:
                    for b in units[u]:
                        outs.append(save(w.at[b], w_out[b], out_sem.at[b]))
                elif u == 5:
                    for q in range(4):
                        outs.append(save(w_con.at[pl.ds(2 * q, 2)], con_out[q], out_sem.at[8 + q]))


    def of_segment(rows, number):
        ids = seg_ids[rows, :]
        base, col = number // 3 * 4, number % 3 * width
        result = jnp.zeros((ids.shape[0], width), f32)
        for s in range(4):
            line = modulation[base + s : base + s + 1, col : col + width]
            result = jnp.where(ids == s, line, result)
        return result

    def tiles(size, body):
        def one(i, carry):
            body(pl.ds(pl.multiple_of(i * size, size), size))
            return carry

        lax.fori_loop(0, count // size, one, 0)

    def matrix(b):
        return w[b].reshape(8 * n, width)

    def turn(source, out, sem):
        if ("turned", None) in kept:
            finish("turned")

        def body(i, carry):
            rows = pl.ds(pl.multiple_of(i * SPAN, SPAN), SPAN)
            turned[:, rows] = source[rows, :].T
            return carry

        lax.fori_loop(0, count // SPAN, body, 0)
        keep("turned", None, turned, out, sem)

    def norm_one():
        def body(rows):
            normed = layer_rows(tokens[rows, :].astype(f32))
            padded[rows, :] = (
                normed * (1.0 + of_segment(rows, 1)) + of_segment(rows, 0)
            ).astype(bf16)

        tiles(128, body)
        turn(padded, pair_out.at[0], 0)

    def spread_hidden():
        def one(s, carry):
            slabs[3, s] = spread_rows(starts, padded, s).astype(bf16)
            return carry

        lax.fori_loop(0, 4, one, 0)

    def project(which):
        def one(s, carry):
            result = dot(slabs[3, s], matrix(which))
            if which != 1:
                result = result + bias_row(which // 2)
            slabs[which, s] = result.astype(bf16)
            return carry

        lax.fori_loop(0, 4, one, 0)
        keep("slab", which, slabs.at[which], slab_out[which], 1 + which)

    def attend_heads(first, last):
        def one(s, carry):
            attend_slab(
                starts, s, slabs.at[0], slabs.at[1], slabs.at[2], slabs.at[3], range(first, last)
            )
            return carry

        lax.fori_loop(0, 4, one, 0)

    def gather_back():
        unspread(starts, slabs.at[3], padded)
        turn(padded, pair_out.at[1], 4)

    def add_projected():
        def body(rows):
            projected = dot(padded[rows, :], matrix(3)) + bias_row(2)
            wide[1, rows, :] = projected
            middle = tokens[rows, :].astype(f32) + of_segment(rows, 2) * projected
            wide[0, rows, :] = middle

        tiles(256, body)
        keep("wide", None, wide.at[1], proj_out, 5)
        keep("middle", None, wide.at[0], mid_out, 6)

    def norm_two():
        def body(rows):
            normed = layer_rows(wide[0, rows, :])
            hidden[rows, :] = (
                normed * (1.0 + of_segment(rows, 4)) + of_segment(rows, 3)
            ).astype(bf16)

        tiles(128, body)
        turn(hidden, h2_out, 7)

    def expand_block(j):
        finish("wide")
        finish("turned")
        if j < 3:
            finish("slab", j)

        def body(i, carry):
            rows = pl.ds(pl.multiple_of(i * SPAN, SPAN), SPAN)
            before = dot(hidden[rows, :], matrix(4 + j)) + bias_row(3 + j)
            wide[1, rows, :] = before
            low = gelu(before).astype(bf16)
            slabs[j, i] = low
            turned[:, rows] = low.T
            return carry

        lax.fori_loop(0, count // SPAN, body, 0)
        keep("wide", None, wide.at[1], before_out[j], 8 + j)
        keep("turned", None, turned, act_out.at[j], 12 + j)

    def contract():
        finish("wide")

        def body(i, carry):
            rows = pl.ds(pl.multiple_of(i * SPAN, SPAN), SPAN)
            result = dot(slabs[0, i], w_con[0:2].reshape(8 * n, width))
            for q in range(1, 4):
                result = result + dot(slabs[q, i], w_con[2 * q : 2 * q + 2].reshape(8 * n, width))
            result = result + bias_row(7)
            wide[1, rows, :] = result
            padded[rows, :] = (wide[0, rows, :] + of_segment(rows, 5) * result).astype(bf16)
            return carry

        lax.fori_loop(0, count // SPAN, body, 0)
        keep("wide", None, wide.at[1], ff_out, 16)
        keep("out", None, padded, y_out, 17)

    plan = [0, multiply, 1, 2, sum_x, 3, 4, sum_z, 5, norm_one, 6, spread_hidden, 7]
    plan += [partial(project, 0), 8, partial(project, 2), 9, 10, partial(project, 1), 11]
    for first in range(0, 16, 2):
        plan += [partial(attend_heads, first, first + 2)] + ([12 + first // 4] if first % 4 else [])
    plan += [gather_back, 16, add_projected, norm_two, 17]
    plan += [partial(expand_block, 0), 18, partial(expand_block, 1), 19]
    plan += [partial(expand_block, 2), 20, partial(expand_block, 3), 21, 22, 23, 24, 25, 26]
    for item in plan + [contract]:
        if isinstance(item, int):
            step(item)
        else:
            item()
    for copy in sent:
        copy.wait_send()
    for copy in outs + list(kept.values()):
        copy.wait()


def forward_fast(own_parts, cond_silu, bias_low, mod_low, starts, segments, tokens):
    attention, projection, expand, contract = own_parts
    width = projection.shape[1]
    n = attention.shape[0]
    count = tokens.shape[0]
    low = [part.astype(bf16) for part in own_parts]
    n_seg = cond_silu.shape[0]
    cond = cond_silu.astype(f32).reshape(n_seg, 8, n).transpose(1, 0, 2)
    cond = jnp.pad(jnp.concatenate([cond, cond], axis=1), ((0, 0), (0, 0), (0, 256 - n)))
    row = lax.axis_index("rows")
    window = 128 * 16 * jnp.maximum(row - 1, 0)
    bias = lax.dynamic_update_slice(
        jnp.zeros(4096, bf16), bias_low, (row * bias_low.shape[0] - window,)
    ).reshape(32, 128)
    sems = pltpu.SemaphoreType.DMA

    def shape(dtype, *dims):
        return jax.ShapeDtypeStruct(dims, dtype)

    outs = pl.pallas_call(
        forward_kernel,
        out_shape=(shape(bf16, 8, n, width),) * 8
        + (shape(bf16, 2, 4, n, width),) * 4
        + (shape(bf16, 4, SPAN, width),) * 3
        + (shape(f32, count, width),) * 4
        + (
            shape(f32, 8, 3 * width),
            shape(bf16, 2, width, count),
            shape(f32, count, width),
            shape(f32, count, width),
            shape(bf16, width, count),
            shape(bf16, 4, width, count),
            shape(f32, count, width),
            shape(bf16, count, width),
        ),
        in_specs=[ANY] * 4 + [VM, VM, VM, SM, VM, VM],
        out_specs=(ANY,) * 19 + (VM,) + (ANY,) * 7,
        scratch_shapes=[
            pltpu.VMEM((8, 8, n, width), bf16),
            pltpu.VMEM((8, 4, n, width), bf16),
            pltpu.VMEM((8, 8, 256), f32),
            pltpu.VMEM((8, 32, 128), bf16),
            pltpu.VMEM((128, 128), f32),
            pltpu.VMEM((4, 2, 8, 3 * width), f32),
            pltpu.VMEM((4, 8, 3 * width), f32),
            pltpu.VMEM((3, 8, 3 * width), f32),
            pltpu.VMEM((4, 4, SPAN, width), bf16),
            pltpu.VMEM((count, width), bf16),
            pltpu.VMEM((2, count, width), f32),
            pltpu.VMEM((count, width), bf16),
            pltpu.VMEM((width, count), bf16),
            sems((14,)),
            sems((14,)),
            sems((4,)),
            sems((4,)),
        ]
        + [sems((6, 3))] * 2
        + [sems((6, 4))] * 6
        + [sems((6,)), sems((12,)), sems((18,))],
        compiler_params=pltpu.CompilerParams(
            collective_id=0, has_side_effects=True, vmem_limit_bytes=60 << 20
        ),
        name="forward",
    )(*low, cond, bias, mod_low, starts, segments[:, None], tokens)
    w = [block.reshape(8 * n, width) for block in outs[:8]]
    con = [block.reshape(8 * n, width) for block in outs[8:12]]
    modulation = jnp.concatenate([outs[19][:n_seg], outs[19][n_seg:]], axis=1)
    weights = (tuple(w[:3]), w[3], tuple(w[4:]), con)
    pair, projected, middle, h2, act, feedforward, output = outs[20:]
    lefts = (
        pair.reshape(2, 8, n, count),
        h2.reshape(8, n, count),
        act.reshape(8, 4, n, count),
    )
    saved = (modulation, outs[12:15], projected, middle, outs[15:19], feedforward, lefts)
    return output, saved, weights


def of_tokens(onehot, modulation, width):
    rows = sum(onehot[:, s : s + 1] * modulation[s] for s in range(onehot.shape[1]))
    return [rows[:, j * width : (j + 1) * width] for j in range(6)]


def forward_plain(own_parts, cond_silu, bias_low, mod_low, starts, segments, tokens):
    def whole(part):
        return lax.all_gather(part.astype(bf16), "rows", axis=0, tiled=True)

    attention, projection, expand, contract = own_parts
    width = projection.shape[1]
    att, w_proj, exp, w_con = map(whole, own_parts)
    w_att = tuple(att[:, j * width : (j + 1) * width] for j in range(3))
    w_exp = tuple(exp[:, j * width : (j + 1) * width] for j in range(4))
    shard = mod_low.shape[0]
    cond = lax.all_gather(cond_silu, "rows", axis=0, tiled=True)
    cond = lax.dynamic_slice_in_dim(cond, lax.axis_index("rows") * shard, shard, axis=1)
    modulation = lax.psum_scatter(dot(cond, mod_low), "rows", scatter_dimension=0, tiled=True)
    biases = whole(bias_low).astype(f32)
    bias = [biases[j * width : (j + 1) * width] for j in range(14)]
    modulation = modulation + biases[8 * width :]
    onehot = (segments[:, None] == jnp.arange(cond_silu.shape[0])[None, :]).astype(f32)
    shift_one, scale_one, gate_one, shift_two, scale_two, gate_two = of_tokens(
        onehot, modulation, width
    )
    wide = tokens.astype(f32)
    hidden_one = (layer_norm(wide)[0] * (1.0 + scale_one) + shift_one).astype(bf16)
    query = (dot(hidden_one, w_att[0]) + bias[0]).astype(bf16)
    key = dot(hidden_one, w_att[1]).astype(bf16)
    value = (dot(hidden_one, w_att[2]) + bias[1]).astype(bf16)
    attended, *slabs = attend(starts, query, key, value)
    projected = dot(attended, w_proj) + bias[2]
    middle = wide + gate_one * projected
    hidden_two = (layer_norm(middle)[0] * (1.0 + scale_two) + shift_two).astype(bf16)
    before = [dot(hidden_two, part) + bias[3 + j] for j, part in enumerate(w_exp)]
    activated = jnp.concatenate([gelu(part).astype(bf16) for part in before], axis=1)
    feedforward = dot(activated, w_con) + bias[7]
    output = (middle + gate_two * feedforward).astype(bf16)
    w_con = [w_con[j * width : (j + 1) * width] for j in range(4)]
    lefts = (hidden_one, attended, hidden_two, activated)
    saved = (modulation, slabs, projected, middle, before, feedforward, lefts)
    return output, saved, (w_att, w_proj, w_exp, w_con)


class Reduce:
    def __init__(self, out, refs, units):
        self.out = out
        self.d, self.y_in, self.x_in, self.z_in, self.total, self.y2_in, self.grad = refs[:7]
        self.y_s, self.y_r, self.x_s, self.x_r, self.z_s, self.z_r = refs[7:13]
        self.y2_s, self.y2_r, self.c_s, self.c_r, self.store = refs[13:]
        row, seg = lax.axis_index("rows"), lax.axis_index("seg")
        self.row, self.x, self.z = row, row % 2, row // 2
        self.y, self.c = seg // 2, seg % 2
        self.units = units
        self.slots, _, n, self.width = self.d.shape
        self.piece = piece = n // 3
        self.part = pl.multiple_of(self.y * piece, piece)
        self.mine = pl.multiple_of(self.y * 2 * piece, piece)
        self.theirs = pl.multiple_of((1 - self.y) * 2 * piece, piece)
        self.level = [lax.rem(self.z + k, 4) for k in range(4)]
        self.z_peers = [(self.level[k] * 2 + self.x, seg) for k in range(4)]
        self.x_peer = (row + 1 - 2 * self.x, seg)
        self.y_peer = (row, seg + 2 - 4 * self.y)
        self.c_peer = (row, seg + 1 - 2 * self.c)
        self.sent, self.outs = {u: [] for u in range(units)}, []
        self.steps = [(u, k) for u in range(self.units) for k in (1, 3, 2, 0)]
        self.count = len(self.steps) + 8

    def greet(self):
        greet(self.z_peers[1:] + [self.x_peer, self.y_peer, self.c_peer])

    def go(self, u, copy):
        copy.start()
        self.sent[u].append(copy)

    def drain(self, u):
        for copy in self.sent.pop(u, ()):
            copy.wait_send()

    def add(self, *terms):
        result = terms[0].astype(f32)
        for term in terms[1:]:
            result = result + term.astype(f32)
        return result.astype(bf16)


    def to_y(self, u, k):
        i = u % self.slots
        src = self.d.at[i, pl.ds(self.level[k] * 2, 2), pl.ds(self.theirs, self.piece)]
        return remote(src, self.y_in.at[i, k], self.y_s.at[u, k], self.y_r.at[u, k], self.y_peer)

    def to_x(self, u, k):
        i = u % self.slots
        src = self.d.at[i, self.level[k] * 2 + 1 - self.x, pl.ds(self.part, 2 * self.piece)]
        return remote(src, self.x_in.at[i, k], self.x_s.at[u, k], self.x_r.at[u, k], self.x_peer)

    def to_z(self, u, k):
        i = u % self.slots
        src = self.d.at[i, self.level[k] * 2 + self.x, pl.ds(self.part, 2 * self.piece)]
        return remote(
            src, self.z_in.at[i, k - 1], self.z_s.at[u, k - 1], self.z_r.at[u, k - 1], self.z_peers[k]
        )

    def to_y_again(self, u):
        i = u % self.slots
        return remote(
            self.total.at[i], self.y2_in.at[i], self.y2_s.at[u], self.y2_r.at[u], self.y_peer
        )

    def to_core(self, u):
        ref = self.grad.at[u, self.c]
        return remote(ref, ref, self.c_s.at[u], self.c_r.at[u], self.c_peer)

    def begin(self, u):
        for k in (1, 3, 2, 0):
            self.go(u, self.to_y(u, k))

    def step(self, j):
        d, piece = self.d, self.piece
        mine, part = pl.ds(self.mine, piece), pl.ds(self.part, 2 * piece)
        if j < len(self.steps):
            u, k = self.steps[j]
            i = u % self.slots
            self.to_y(u, k).wait_recv()
            for side in range(2):
                r = self.level[k] * 2 + side
                d[i, r, mine] = self.add(d[i, r, mine], self.y_in[i, k, side])
            self.go(u, self.to_x(u, k))
        if 0 <= j - 1 < len(self.steps):
            u, k = self.steps[j - 1]
            i = u % self.slots
            self.to_x(u, k).wait_recv()
            r = self.level[k] * 2 + self.x
            d[i, r, part] = self.add(d[i, r, part], self.x_in[i, k])
            if k:
                self.go(u, self.to_z(u, k))
        if j >= 5 and (j - 5) % 4 == 0 and (j - 5) // 4 < self.units:
            u = (j - 5) // 4
            i = u % self.slots
            for k in (1, 3, 2):
                self.to_z(u, k).wait_recv()
            z_in = self.z_in
            self.total[i] = self.add(d[i, self.row, part], z_in[i, 0], z_in[i, 1], z_in[i, 2])
            self.go(u, self.to_y_again(u))
        if j >= 6 and (j - 6) % 4 == 0 and (j - 6) // 4 < self.units:
            u = (j - 6) // 4
            i = u % self.slots
            self.to_y_again(u).wait_recv()
            total, y2_in, grad, c = self.total, self.y2_in, self.grad, self.c
            here = pl.ds(pl.multiple_of(self.y * piece, piece), piece)
            there = pl.ds(pl.multiple_of((1 - self.y) * piece, piece), piece)
            grad[u, c, mine] = total[i, here]
            grad[u, c, pl.ds(self.theirs, piece)] = y2_in[i, there]
            grad[u, c, pl.ds(piece, piece)] = self.add(total[i, there], y2_in[i, here])
            self.go(u, self.to_core(u))
        if j >= 7 and (j - 7) % 4 == 0 and (j - 7) // 4 < self.units:
            u = (j - 7) // 4
            self.to_core(u).wait_recv()
            copy = pltpu.make_async_copy(self.grad.at[u], self.out.at[u], self.store.at[u])
            copy.start()
            self.outs.append(copy)

    def finish(self):
        for u in range(self.units):
            self.drain(u)
        for copy in self.outs:
            copy.wait()

    @staticmethod
    def scratch(units, slots, n, width):
        sems = pltpu.SemaphoreType.DMA

        def space(*shape):
            return pltpu.VMEM(shape + (width,), bf16)

        return (
            [
                space(slots, 8, n),
                space(slots, 4, 2, n // 3),
                space(slots, 4, 2 * n // 3),
                space(slots, 3, 2 * n // 3),
                space(slots, 2 * n // 3),
                space(slots, 2 * n // 3),
                space(units, 2, n),
            ]
            + [sems((units, 4))] * 4
            + [sems((units, 3))] * 2
            + [sems((units,))] * 5
        )


def multiply_pair(out, lefts, rights):
    n, width = out.shape[1:]

    def one(i, carry):
        rows = pl.ds(2 * i, 2)
        total = 0.0
        for left, right in zip(lefts, rights):
            total = total + dot(left[rows].reshape(2 * n, left.shape[2]), right[...])
        out[rows] = total.astype(bf16).reshape(2, n, width)
        return carry

    lax.fori_loop(0, 4, one, 0)


def reduce_kernel(
    act, feed, hidden, b0, b1, b2, b3, pair, project, starts, qs, ks, vs, up, out, qv, dk, left, right,
    near, far_s, far_r, save_sem, free, *refs
):
    red = Reduce(out, refs, 6)
    c, count = red.c, up.shape[0]
    rows = pl.ds(0, count)

    def near_copy(index, src, dst):
        return pltpu.make_async_copy(src, dst, near.at[index])

    def far_copy(index, src, dst):
        return remote(src, dst, far_s.at[index], far_r.at[index], red.c_peer)

    def lefts(i):
        return left.at[2 * i], left.at[2 * i + 1]

    def rights(i):
        return right.at[2 * i, rows], right.at[2 * i + 1, rows]

    fixed = [
        (act.at[:, c], act.at[:, 1 - c], lefts(0)),
        (feed, feed, rights(0)),
        (act.at[:, 2 + c], act.at[:, 3 - c], lefts(1)),
        (hidden, hidden, lefts(2)),
    ]
    pulls = [
        ((near_copy(i, here, dst[0]),) * 2, (far_copy(i, there, dst[1]),) * 2)
        for i, (here, there, dst) in enumerate(fixed)
    ]
    for i, two in ((4, (b0, b1)), (5, (b2, b3))):
        dst = rights(i - 3)
        pulls.append(
            (
                tuple(near_copy(i, two[core], dst[0]) for core in range(2)),
                tuple(far_copy(i, two[1 - core], dst[1]) for core in range(2)),
            )
        )
    late_far = right.at[0, rows], right.at[1, rows]
    pulls.append(((near_copy(6, pair.at[c], left.at[0]),) * 2, (far_copy(6, pair.at[1 - c], left.at[1]),) * 2))
    pulls.append(((near_copy(7, pair.at[0], left.at[2]),) * 2, (far_copy(7, pair.at[0], left.at[3]),) * 2))
    pulls.append(
        (
            (None, near_copy(8, project, right.at[2, rows])),
            (far_copy(8, project, late_far[0]), far_copy(8, right.at[3, rows], late_far[0])),
        )
    )
    pulls.append(
        ((None, None), (far_copy(9, right.at[5 - c, rows], late_far[1]),) * 2)
    )

    def start(index, side):
        two = pulls[index][side]
        if two[0] is two[1]:
            if two[0] is not None:
                two[0].start()
            return
        for core in range(2):
            if two[core] is not None:

                @pl.when(c == core)
                def _():
                    two[core].start()

    def arrive(index):
        two, far = pulls[index]
        if two[0] is None and two[1] is not None:

            @pl.when(c == 1)
            def _():
                two[1].wait()
        elif two[0] is not None:
            two[0].wait()
        far[0].wait()

    def block(u):
        for index in ((0, 1), (2,), (3, 4), (5,))[u]:
            arrive(index)
        for index in ((2, 3, 4), (5,), (), ())[u]:
            start(index, 1)
        multiply_pair(red.d.at[u], lefts(min(u, 2)), rights(max(u - 1, 0)))
        red.begin(u)

    def late_pulls():
        pl.semaphore_signal(
            free, inc=1, device_id=red.c_peer, device_id_type=pl.DeviceIdType.MESH
        )
        for index in (6, 7, 8):
            start(index, 0)
        pl.semaphore_wait(free, 1)
        for index in (6, 8, 7, 9):
            start(index, 1)

    def late_block(u):
        for index in ((6, 8), (7, 9))[u - 4]:
            arrive(index)
        red.drain(u - 4)
        own = right.at[3 - c, rows] if u == 4 else right.at[4 + c, rows]
        multiply_pair(red.d.at[u - 4], lefts(u - 4), (own, late_far[u - 4]))
        red.begin(u)

    def spread_up():
        def one(s, carry):
            place = pl.ds(pl.multiple_of(s * SPAN, SPAN), SPAN)
            right[3, place, :] = spread_rows(starts, up, s).astype(bf16)
            return carry

        lax.fori_loop(0, 4, one, 0)

    def heads(first, last):
        def one(s, carry):
            place = pl.ds(pl.multiple_of(s * SPAN, SPAN), SPAN)
            back_slab_flat(starts, s, place, qs, ks, vs, right, range(first, last))
            return carry

        lax.fori_loop(0, 4, one, 0)

    kept = []

    def collect(which, slot, dst):
        def one(i, carry):
            place = pl.ds(pl.multiple_of(i * SPAN, SPAN), SPAN)
            right[slot, place, :] = home_rows(starts, i, right[which], 4).astype(bf16)
            return carry

        lax.fori_loop(0, count // SPAN, one, 0)
        copy = pltpu.make_async_copy(right.at[slot, rows], dst, save_sem.at[which])
        copy.start()
        kept.append(copy)

    for index in (0, 1, 2, 3, 4, 5):
        start(index, 0)
    red.greet()
    for index in (0, 1):
        start(index, 1)
    plan = [partial(block, 0), partial(block, 1), 0, partial(block, 2), 1, partial(block, 3), 2]
    plan += [spread_up, 3]
    for first in range(0, 16, 2):
        plan += [partial(heads, first, first + 2), 4 + first // 2]
    plan += [partial(collect, 0, 4, qv.at[0]), partial(collect, 2, 5, qv.at[1]), 12]
    plan += [partial(collect, 1, 3, dk), late_pulls, 13, 14, partial(late_block, 4), 15]
    plan += [partial(late_block, 5)] + list(range(16, red.count))
    for item in plan:
        if isinstance(item, int):
            red.step(item)
        else:
            item()
    red.finish()
    for copy in kept:
        copy.wait()


def reduce_all(lefts, feed, befores, project, starts, slabs, up):
    pair, hidden, act = lefts
    n = act.shape[2]
    count, width = feed.shape
    sems = pltpu.SemaphoreType.DMA
    return pl.pallas_call(
        reduce_kernel,
        out_shape=(
            jax.ShapeDtypeStruct((6, 2, n, width), bf16),
            jax.ShapeDtypeStruct((2, count, width), bf16),
            jax.ShapeDtypeStruct((count, width), bf16),
        ),
        in_specs=[ANY] * 9 + [SM] + [VM] * 4,
        out_specs=(ANY,) * 3,
        scratch_shapes=[
            pltpu.VMEM((6, 8, n, count), bf16),
            pltpu.VMEM((6, 4 * SPAN, width), bf16),
            sems((9,)),
            sems((10,)),
            sems((10,)),
            sems((3,)),
            pltpu.SemaphoreType.REGULAR,
        ]
        + Reduce.scratch(6, 4, n, width),
        compiler_params=pltpu.CompilerParams(
            collective_id=1, has_side_effects=True, vmem_limit_bytes=60 << 20
        ),
        name="reduce",
    )(act, feed, hidden, *befores, pair, project, starts, *slabs, up)


def reduce_fast(lefts, feed, befores, starts, slabs, up, back_project):
    width = feed.shape[1]
    sums, qv, back_key = reduce_all(lefts, feed, befores, back_project, starts, slabs, up)

    def late():
        con = sums[0:2].reshape(-1, width)
        exp = jnp.concatenate([sums[2, 0], sums[2, 1], sums[3, 0], sums[3, 1]], axis=1)
        att = jnp.concatenate([sums[5, 0], sums[4, 0], sums[5, 1]], axis=1)
        return tuple(part.astype(f32) for part in (att, sums[4, 1], exp, con))

    return (qv[0], back_key, qv[1]), late


def reduce_plain(lefts, feed, befores, starts, slabs, up, back_project):
    hidden_one, attended, hidden_two, activated = lefts
    back_query, back_key, back_value = attend_back(starts, *slabs, up)

    def total(left, right):
        part = lax.psum_scatter(
            outer(left, right).astype(bf16), "rows", scatter_dimension=0, tiled=True
        )
        return lax.psum(part.astype(f32), "seg")

    def late():
        att = total(hidden_one, jnp.concatenate([back_query, back_key, back_value], axis=1))
        exp = total(hidden_two, jnp.concatenate(befores, axis=1))
        return att, total(attended, back_project), exp, total(activated, feed)

    return (back_query, back_key, back_value), late


def on_device(
    fast,
    tokens,
    condition,
    segment_ids,
    cotangent,
    modulation_master,
    modulation_first,
    modulation_second,
    attention_master,
    attention_first,
    attention_second,
    projection_master,
    projection_first,
    projection_second,
    expand_master,
    expand_first,
    expand_second,
    contract_master,
    contract_first,
    contract_second,
    bias_master,
    bias_first,
    bias_second,
):
    width = tokens.shape[1]
    hidden = expand_master.shape[1]
    shard = modulation_master.shape[0]
    n_seg = condition.shape[1]
    row = lax.axis_index("rows")
    segments = segment_ids[0]
    onehot = (segments[:, None] == jnp.arange(n_seg, dtype=jnp.int32)[None, :]).astype(f32)
    starts = jnp.sum(
        segments[:, None] < jnp.arange(n_seg + 1, dtype=jnp.int32)[None, :], axis=0, dtype=jnp.int32
    )
    tokens_wide = tokens.astype(f32)
    upstream = cotangent.astype(f32)

    cond_silu = jax.nn.silu(condition[0].astype(f32)).astype(bf16)
    forward = forward_fast if fast else forward_plain
    output, saved, (w_att, w_proj, w_exp, w_con) = forward(
        (attention_master, projection_master, expand_master, contract_master),
        cond_silu,
        bias_master.astype(bf16),
        modulation_master.astype(bf16),
        starts,
        segments,
        tokens,
    )
    modulation, slabs, projected, middle, before, feedforward, lefts = saved
    shift_one, scale_one, gate_one, shift_two, scale_two, gate_two = of_tokens(
        onehot, modulation, width
    )
    normed_one, inverse_one = layer_norm(tokens_wide)
    normed_two, inverse_two = layer_norm(middle)

    back_gate_two = upstream * feedforward
    back_feed = (upstream * gate_two).astype(bf16)
    back_before = []
    for j, part in enumerate(before):
        back_active = back_dot(back_feed, w_con[j])
        back_before.append(jax.vjp(gelu, part)[1](back_active)[0].astype(bf16))
    back_hidden_two = sum(back_dot(back_before[j], w_exp[j]) for j in range(4))
    back_middle = upstream + norm_back(back_hidden_two * (1.0 + scale_two), normed_two, inverse_two)
    back_gate_one = back_middle * projected
    back_project = (back_middle * gate_one).astype(bf16)
    back_attend = back_dot(back_project, w_proj).astype(bf16)
    reduce = reduce_fast if fast else reduce_plain
    (back_query, back_key, back_value), late = reduce(
        lefts, back_feed, back_before, starts, slabs, back_attend, back_project
    )
    back_hidden_one = (
        back_dot(back_query, w_att[0]) + back_dot(back_key, w_att[1]) + back_dot(back_value, w_att[2])
    )
    back_tokens = back_middle + norm_back(
        back_hidden_one * (1.0 + scale_one), normed_one, inverse_one
    )
    back_modulation = [
        outer(onehot, part, highest)
        for part in (
            back_hidden_one,
            back_hidden_one * normed_one,
            back_gate_one,
            back_hidden_two,
            back_hidden_two * normed_two,
            back_gate_two,
        )
    ]
    columns = [
        jnp.sum(part.astype(f32), axis=0, keepdims=True)
        for part in (back_query, back_value, back_project, *back_before, back_feed)
    ]
    payload = jnp.concatenate(back_modulation + [cond_silu.astype(f32)] + columns, axis=0)
    everyone = lax.all_gather(payload, ("rows", "seg"), axis=0)
    grad_att, grad_proj, grad_exp, grad_con = late()
    mods = [
        everyone[:, j * n_seg : (j + 1) * n_seg].reshape(-1, width) for j in range(6)
    ]
    cond_rows = lax.dynamic_slice_in_dim(
        everyone[:, 6 * n_seg : 7 * n_seg].reshape(-1, width), row * shard, shard, axis=1
    )
    grad_mod = outer(cond_rows, jnp.concatenate(mods, axis=1), highest)
    rest = jnp.sum(everyone[:, 7 * n_seg :], axis=0).reshape(-1)
    grad_bias = lax.dynamic_slice_in_dim(
        jnp.concatenate([rest] + [jnp.sum(part, axis=0) for part in mods]),
        row * bias_master.shape[0],
        bias_master.shape[0],
    )
    results = [
        adam_update(*operands)
        for operands in (
            (grad_mod, modulation_master, modulation_first, modulation_second),
            (grad_att, attention_master, attention_first, attention_second),
            (grad_proj, projection_master, projection_first, projection_second),
            (grad_exp, expand_master, expand_first, expand_second),
            (grad_con, contract_master, contract_first, contract_second),
            (grad_bias, bias_master, bias_first, bias_second),
        )
    ]
    flat = tuple((item for result in results for item in result))
    return (output, back_tokens.astype(bf16)) + flat


def solution(mesh):
    both = ("rows", "seg")
    fast = mesh.shape["rows"] == 8 and mesh.shape["seg"] == 4
    token, matrix, vector = P(both, None), P("rows", None), P("rows")
    in_specs = (token, P(both, None, None), token, token) + (matrix,) * 15 + (vector,) * 3
    out_specs = (token, token) + (matrix,) * 15 + (vector,) * 3
    return jax.shard_map(
        partial(on_device, fast),
        mesh=mesh,
        in_specs=in_specs,
        out_specs=out_specs,
        check_vma=False,
    )
```

```python
from functools import partial

import jax
import jax.numpy as jnp
from jax import lax
from jax.experimental import pallas as pl
from jax.experimental.pallas import tpu as pltpu
from jax.sharding import PartitionSpec as P

HEAD_DIM = 72
STEP = 10
SPAN = 256
EXP_SCALE = HEAD_DIM**-0.5 * 1.4426950408889634

bf16 = jnp.bfloat16
f32 = jnp.float32
highest = lax.Precision.HIGHEST
beta_first = 0.9
beta_second = 0.999
learning = 0.06
weight_decay = 0.1
adam_epsilon = 1e-08
norm_epsilon = 1e-06

ROW_X = [(z * 2 + x, z * 2 + 1 - x) for z in range(4) for x in range(2)]
ROW_Z = [
    [(z * 2 + x, (z + k) % 4 * 2 + x) for z in range(4) for x in range(2)] for k in range(4)
]
SEG_Y = [(y * 2 + c, (1 - y) * 2 + c) for y in range(2) for c in range(2)]
SEG_C = [(y * 2 + c, y * 2 + 1 - c) for y in range(2) for c in range(2)]


def over_x(v):
    return lax.ppermute(v, "rows", ROW_X)


def over_z(v, k):
    return lax.ppermute(v, "rows", ROW_Z[k])


def over_y(v):
    return lax.ppermute(v, "seg", SEG_Y)


def over_core(v):
    return lax.ppermute(v, "seg", SEG_C)


def place():
    row = lax.axis_index("rows")
    seg = lax.axis_index("seg")
    return row % 2, seg // 2, row // 2, seg % 2


def layer_norm(values):
    center = values - jnp.mean(values, axis=-1, keepdims=True)
    inverse = lax.rsqrt(jnp.mean(center * center, axis=-1, keepdims=True) + norm_epsilon)
    return (center * inverse, inverse)


def norm_back(upstream, normed, inverse):
    return inverse * (
        upstream
        - jnp.mean(upstream, axis=-1, keepdims=True)
        - normed * jnp.mean(upstream * normed, axis=-1, keepdims=True)
    )


def outer(left, right, precision=None):
    return lax.dot_general(
        left,
        right,
        (((0,), (0,)), ((), ())),
        precision=precision,
        preferred_element_type=f32,
    )


def dot(left, right):
    return jnp.dot(left, right, preferred_element_type=f32)


def back_dot(left, right):
    return lax.dot_general(left, right, (((1,), (1,)), ((), ())), preferred_element_type=f32)


def spread_rows(starts, source, s):
    rows = source.shape[0]
    row = lax.broadcasted_iota(jnp.int32, (SPAN, rows), 0) + starts[s]
    col = lax.broadcasted_iota(jnp.int32, (SPAN, rows), 1)
    pick = jnp.where((col == row) & (row < starts[s + 1]), 1.0, 0.0).astype(bf16)
    return dot(pick, source[...])

def spread(starts, source, out):
    def one(s,_):
        out[s]=spread_rows(starts,source,s).astype(bf16)
        return 0
    lax.fori_loop(0,out.shape[0],one,0)

def home_rows(starts, i, flat, n):
    row = lax.broadcasted_iota(jnp.int32, (SPAN, 1), 0) + i * SPAN
    home = row
    for s in range(1, n):
        home = home + jnp.where(row >= starts[s], SPAN - (starts[s] - starts[s - 1]), 0)
    pick = jnp.where(lax.broadcasted_iota(jnp.int32, (SPAN, n * SPAN), 1) == home, 1.0, 0.0)
    return dot(pick.astype(bf16), flat)


def unspread(starts, slabs, out):
    n, _, width = slabs.shape

    def one(i, carry):
        place = pl.ds(pl.multiple_of(i * SPAN, SPAN), SPAN)
        flat = slabs[...].reshape(n * SPAN, width)
        out[place, :] = home_rows(starts, i, flat, n).astype(bf16)
        return carry

    lax.fori_loop(0, out.shape[0] // SPAN, one, 0)


def attend_slab(starts, s, qs, ks, vs, os, heads):
    length = starts[s + 1] - starts[s]
    outside = jnp.where(lax.broadcasted_iota(jnp.int32, (SPAN, 1), 0) < length, 0.0, -1e30)
    for h in heads:
        cols = slice(h * HEAD_DIM, (h + 1) * HEAD_DIM)
        score = back_dot(ks[s, :, cols], qs[s, :, cols]) + outside
        power = jnp.exp2((score - jnp.max(score, axis=0, keepdims=True)) * EXP_SCALE)
        soft = (power * (1.0 / jnp.sum(power, axis=0, keepdims=True))).astype(bf16)
        os[s, :, cols] = outer(soft, vs[s, :, cols]).astype(bf16)


def attend_kernel(starts, q, k, v, out, qs, ks, vs, os):
    for src, dst in ((q, qs), (k, ks), (v, vs)):
        spread(starts, src, dst)

    def seg(s, carry):
        attend_slab(starts, s, qs, ks, vs, os, range(qs.shape[2] // HEAD_DIM))
        return carry

    lax.fori_loop(0, qs.shape[0], seg, 0)
    unspread(starts, os, out)

def back_slab(starts, s, qs, ks, vs, ups, dqs, dks, dvs, heads):
    scale = HEAD_DIM**-0.5
    length = starts[s + 1] - starts[s]
    outside = jnp.where(lax.broadcasted_iota(jnp.int32, (SPAN, 1), 0) < length, 0.0, -1e30)
    for h in heads:
        cols = slice(h * HEAD_DIM, (h + 1) * HEAD_DIM)
        query, key, value, upstream = (part[s, :, cols] for part in (qs, ks, vs, ups))
        score = back_dot(key, query) + outside
        power = jnp.exp2((score - jnp.max(score, axis=0, keepdims=True)) * EXP_SCALE)
        soft = power * (1.0 / jnp.sum(power, axis=0, keepdims=True))
        back_soft = back_dot(value, upstream)
        mean = jnp.sum(back_soft * soft, axis=0, keepdims=True)
        back_score = (soft * (back_soft - mean)).astype(bf16)
        dvs[s, :, cols] = dot(soft.astype(bf16), upstream).astype(bf16)
        dks[s, :, cols] = (dot(back_score, query) * scale).astype(bf16)
        dqs[s, :, cols] = (outer(back_score, key) * scale).astype(bf16)


class Slab:
    def __init__(self, ref, slot, rows):
        self.ref, self.slot, self.rows = ref, slot, rows

    def __getitem__(self, index):
        return self.ref[self.slot, self.rows, index[2]]

    def __setitem__(self, index, value):
        self.ref[self.slot, self.rows, index[2]] = value


def back_slab_flat(starts, s, rows, qs, ks, vs, space, heads):
    dqs, dks, dvs, ups = (Slab(space, slot, rows) for slot in range(4))
    back_slab(starts, s, qs, ks, vs, ups, dqs, dks, dvs, heads)


def back_kernel(starts, qs, ks, vs, up, dq, dk, dv, ups, dqs, dks, dvs):
    spread(starts, up, ups)

    def seg(s, carry):
        back_slab(
            starts, s, qs, ks, vs, ups, dqs, dks, dvs, range(qs.shape[2] // HEAD_DIM)
        )
        return carry

    lax.fori_loop(0, qs.shape[0], seg, 0)
    for slabs, out in ((dqs, dq), (dks, dk), (dvs, dv)):
        unspread(starts, slabs, out)


VM = pl.BlockSpec(memory_space=pltpu.VMEM)
SM = pl.BlockSpec(memory_space=pltpu.SMEM)
ANY = pl.BlockSpec(memory_space=pl.ANY)
def attend(starts,q,k,v):
    n=starts.shape[0]-1; rows,width=q.shape
    slab=jax.ShapeDtypeStruct((n,SPAN,width),bf16)
    return pl.pallas_call(attend_kernel,out_shape=(jax.ShapeDtypeStruct(q.shape,bf16),slab,slab,slab),
        in_specs=[SM,VM,VM,VM],out_specs=(VM,)*4,
        scratch_shapes=[pltpu.VMEM((n,SPAN,width),bf16)],
        compiler_params=pltpu.CompilerParams(vmem_limit_bytes=56<<20),
        cost_estimate=pl.CostEstimate(flops=2*2*16*n*SPAN*SPAN*128,bytes_accessed=rows*width*14,transcendentals=16*n*SPAN*SPAN),name="attend")(starts,q,k,v)
def attend_back(starts,qs,ks,vs,up):
    n=starts.shape[0]-1; rows,width=up.shape
    slab=pltpu.VMEM((n,SPAN,width),bf16); o=jax.ShapeDtypeStruct(up.shape,bf16)
    return pl.pallas_call(back_kernel,out_shape=(o,o,o),
        in_specs=[SM,VM,VM,VM,VM],out_specs=(VM,)*3,
        scratch_shapes=[slab]*4,
        compiler_params=pltpu.CompilerParams(vmem_limit_bytes=56<<20),
        cost_estimate=pl.CostEstimate(flops=5*2*16*n*SPAN*SPAN*128,bytes_accessed=rows*width*14,transcendentals=16*n*SPAN*SPAN),name="attend_back")(starts,qs,ks,vs,up)


def adam_update(gradient, master, first, second):
    first_new = beta_first * first + (1.0 - beta_first) * gradient
    second_new = beta_second * second + (1.0 - beta_second) * gradient * gradient
    first_hat = first_new / (1.0 - beta_first**STEP)
    second_hat = second_new / (1.0 - beta_second**STEP)
    master_new = master - learning * (
        first_hat / (jnp.sqrt(second_hat) + adam_epsilon) + weight_decay * master
    )
    return (master_new, first_new, second_new)


def gelu(v):
    return 0.5 * v * (1.0 + jnp.tanh(0.7978845608028654 * (v + 0.044715 * (v * v * v))))


def remote(src, dst, send, recv, device):
    return pltpu.make_async_remote_copy(
        src_ref=src,
        dst_ref=dst,
        send_sem=send,
        recv_sem=recv,
        device_id=device,
        device_id_type=pl.DeviceIdType.MESH,
    )


def greet(peers):
    barrier = pltpu.get_barrier_semaphore()
    for peer in peers:
        pl.semaphore_signal(
            barrier, inc=1, device_id=peer, device_id_type=pl.DeviceIdType.MESH
        )
    pl.semaphore_wait(barrier, len(peers))


def layer_rows(values):
    center = values - jnp.mean(values, axis=-1, keepdims=True)
    return center * lax.rsqrt(jnp.mean(center * center, axis=-1, keepdims=True) + norm_epsilon)


def forward_kernel(
    att_low, proj_low, exp_low, con_low, cond, bias, w_mod, starts, seg_ids, tokens, *refs
):
    w_out, con_out, slab_out, before_out = refs[:8], refs[8:12], refs[12:15], refs[15:19]
    modulation, pair_out, proj_out, mid_out, h2_out, act_out, ff_out, y_out = refs[19:27]
    rest = refs[27:]
    w, w_con, conds, bias_in, bias_all, parts, x_parts, z_parts = rest[:8]
    slabs, padded, wide, hidden, turned = rest[8:13]
    small_s, small_r, part_s, part_r = rest[13:17]
    z_s, z_r, x_s, x_r, y_s, y_r, c_s, c_r, load_sem, out_sem, save_sem = rest[17:]
    row, seg = lax.axis_index("rows"), lax.axis_index("seg")
    x, z = row % 2, row // 2
    y, c = seg // 2, seg % 2
    n, width = proj_low.shape
    count = tokens.shape[0]
    units = ((0, 2), (1, 3), (4, 5), (6, 7), (8, 9), (10, 11))
    piece = n // 3
    part = pl.multiple_of(y * piece, piece)
    third = pl.multiple_of(y * 2 * piece, piece)
    far = [lax.rem(z + 4 - k, 4) for k in range(4)]

    def block_of(u):
        return units[u][0] + c * (units[u][1] - units[u][0])

    def slot(u, r, rows):
        if u < 4:
            return w.at[block_of(u), r, rows]
        return w_con.at[r, block_of(u) - 8, rows]

    def columns(number):
        return pl.ds(pl.multiple_of(number * width, width), width)

    mine = pl.ds(part, 2 * piece)
    own = (
        att_low.at[mine, columns(2 * c)],
        None,
        exp_low.at[mine, columns(c)],
        exp_low.at[mine, columns(2 + c)],
        con_low.at[pl.ds(pl.multiple_of(c * n + part, 16), 2 * piece)],
        con_low.at[pl.ds(pl.multiple_of((2 + c) * n + part, 16), 2 * piece)],
    )
    loads = []
    for u in range(6):
        dst = slot(u, row, mine)
        if u != 1:
            copy = pltpu.make_async_copy(own[u], dst, load_sem.at[u])
            copy.start()
        else:
            two = (att_low.at[mine, columns(1)], proj_low.at[mine])
            for core in range(2):

                @pl.when(c == core)
                def _():
                    pltpu.make_async_copy(two[core], dst, load_sem.at[u]).start()

            copy = pltpu.make_async_copy(two[1], dst, load_sem.at[u])
        loads.append(copy)
    z_peers = [(lax.rem(z + k, 4) * 2 + x, seg) for k in (1, 2, 3)]
    x_peer, y_peer, c_peer = (row + 1 - 2 * x, seg), (row, seg + 2 - 4 * y), (row, seg + 1 - 2 * c)
    cross_peers = [(lax.rem(z + k, 4) * 2 + 1 - x, seg) for k in (1, 2, 3)]
    row_peers = z_peers + cross_peers + [x_peer]
    greet(row_peers + [y_peer, c_peer])
    sent = []

    def go(copy):
        copy.start()
        sent.append(copy)

    small = []
    for i, peer in enumerate(row_peers):
        small.append(remote(cond.at[peer[0]], conds.at[row], small_s.at[i], small_r.at[i], peer))
        small.append(remote(bias, bias_in.at[row], small_s.at[7 + i], small_r.at[7 + i], peer))
    for copy in small:
        go(copy)
    conds[row] = cond[row]
    bias_in[row] = bias[...]

    def to_x():
        return remote(parts.at[:, 1 - x], x_parts, part_s.at[0], part_r.at[0], x_peer)

    def to_z(k):
        src = parts.at[lax.rem(z + k, 4), x]
        return remote(src, z_parts.at[k - 1], part_s.at[k], part_r.at[k], z_peers[k - 1])

    def multiply():
        for copy in small:
            copy.wait_recv()
        left = conds[...].reshape(-1, conds.shape[2])[:, :n].astype(bf16)
        half = w_mod.shape[1] // 2
        upper = lax.broadcasted_iota(jnp.int32, (left.shape[0], 1), 0) % 8 < 4
        for start in range(0, half, width):
            both = jnp.where(
                upper,
                dot(left, w_mod[:, start : start + width]),
                dot(left, w_mod[:, half + start : half + start + width]),
            )
            parts[:, :, :, start : start + width] = both.reshape(4, 2, 8, width)
        go(to_x())
        bias_all[...] = jnp.zeros_like(bias_all)
        for r in range(8):
            rows = slice(16 * max(r - 1, 0), 16 * max(r - 1, 0) + 32)
            bias_all[rows] = bias_all[rows] + bias_in[r].astype(f32)

    def sum_x():
        to_x().wait_recv()
        for level in range(4):
            parts[level, x] = parts[level, x] + x_parts[level]
        for k in (1, 3, 2):
            go(to_z(k))

    def sum_z():
        for k in (1, 3, 2):
            to_z(k).wait_recv()
        total = parts[z, x] + z_parts[0] + z_parts[1] + z_parts[2]
        first = 3 + w_expand // width + 1
        for part_no in range(3):
            cols = slice(part_no * width, (part_no + 1) * width)
            upper = lax.broadcasted_iota(jnp.int32, (8, 1), 0) < 4
            modulation[:, cols] = total[:, cols] + jnp.where(
                upper, bias_row(first + part_no), bias_row(first + 3 + part_no)
            )

    w_expand = 4 * width

    def bias_row(number):
        tall = width // 128
        return jnp.concatenate(
            [bias_all[number * tall + i : number * tall + i + 1, :] for i in range(tall)], axis=1
        )

    def along_z(u, k):
        ref = slot(u, row, pl.ds(part, 2 * piece))
        return remote(ref, ref, z_s.at[u, k - 1], z_r.at[u, k - 1], z_peers[k - 1])

    def along_x(u, k):
        ref = slot(u, far[k] * 2 + x, pl.ds(part, 2 * piece))
        return remote(ref, ref, x_s.at[u, k], x_r.at[u, k], x_peer)

    def along_y(u, k):
        ref = slot(u, pl.ds(far[k] * 2, 2), pl.ds(third, piece))
        return remote(ref, ref, y_s.at[u, k], y_r.at[u, k], y_peer)

    def across(u, k):
        ref = slot(u, pl.ds(far[k] * 2, 2), slice(None))
        return remote(ref, ref, c_s.at[u, k], c_r.at[u, k], c_peer)

    steps = [(u, k) for u in range(6) for k in (0, 1, 3, 2)]
    outs, kept = [], {}

    def keep(name, number, src, dst, sem):
        kept[name, number] = save(src, dst, save_sem.at[sem])

    def finish(name, number=None):
        kept.pop((name, number)).wait()

    def save(src, dst, sem):
        copy = pltpu.make_async_copy(src, dst, sem)
        copy.start()
        return copy

    def step(j):
        if j < len(steps):
            u, k = steps[j]
            if j == 0:
                loads[0].wait()
                for hop in (1, 3, 2):
                    go(along_z(0, hop))
            if k:
                along_z(u, k).wait_recv()
            go(along_x(u, k))
            if u < 5 and j % 4 < 3:
                if k == 0:
                    loads[u + 1].wait()
                go(along_z(u + 1, (1, 3, 2)[j % 4]))
        if 0 <= j - 1 < len(steps):
            along_x(*steps[j - 1]).wait_recv()
            go(along_y(*steps[j - 1]))
        if 0 <= j - 2 < len(steps):
            along_y(*steps[j - 2]).wait_recv()
            go(across(*steps[j - 2]))
        if 0 <= j - 3 < len(steps):
            u, k = steps[j - 3]
            across(u, k).wait_recv()
            if k == 2:
                if u < 4:
                    for b in units[u]:
                        outs.append(save(w.at[b], w_out[b], out_sem.at[b]))
                elif u == 5:
                    for q in range(4):
                        outs.append(save(w_con.at[pl.ds(2 * q, 2)], con_out[q], out_sem.at[8 + q]))


    def of_segment(rows, number):
        ids = seg_ids[rows, :]
        base, col = number // 3 * 4, number % 3 * width
        result = jnp.zeros((ids.shape[0], width), f32)
        for s in range(4):
            line = modulation[base + s : base + s + 1, col : col + width]
            result = jnp.where(ids == s, line, result)
        return result

    def tiles(size, body):
        def one(i, carry):
            body(pl.ds(pl.multiple_of(i * size, size), size))
            return carry

        lax.fori_loop(0, count // size, one, 0)

    def matrix(b):
        return w[b].reshape(8 * n, width)

    def turn(source, out, sem):
        if ("turned", None) in kept:
            finish("turned")

        def body(i, carry):
            rows = pl.ds(pl.multiple_of(i * SPAN, SPAN), SPAN)
            turned[:, rows] = source[rows, :].T
            return carry

        lax.fori_loop(0, count // SPAN, body, 0)
        keep("turned", None, turned, out, sem)

    def norm_one():
        def body(rows):
            normed = layer_rows(tokens[rows, :].astype(f32))
            padded[rows, :] = (
                normed * (1.0 + of_segment(rows, 1)) + of_segment(rows, 0)
            ).astype(bf16)

        tiles(128, body)
        turn(padded, pair_out.at[0], 0)

    def spread_hidden():
        def one(s, carry):
            slabs[3, s] = spread_rows(starts, padded, s).astype(bf16)
            return carry

        lax.fori_loop(0, 4, one, 0)

    def project(which):
        def one(s, carry):
            result = dot(slabs[3, s], matrix(which))
            if which != 1:
                result = result + bias_row(which // 2)
            slabs[which, s] = result.astype(bf16)
            return carry

        lax.fori_loop(0, 4, one, 0)
        keep("slab", which, slabs.at[which], slab_out[which], 1 + which)

    def attend_heads(first, last):
        def one(s, carry):
            attend_slab(
                starts, s, slabs.at[0], slabs.at[1], slabs.at[2], slabs.at[3], range(first, last)
            )
            return carry

        lax.fori_loop(0, 4, one, 0)

    def gather_back():
        unspread(starts, slabs.at[3], padded)
        turn(padded, pair_out.at[1], 4)

    def add_projected():
        def body(rows):
            projected = dot(padded[rows, :], matrix(3)) + bias_row(2)
            wide[1, rows, :] = projected
            middle = tokens[rows, :].astype(f32) + of_segment(rows, 2) * projected
            wide[0, rows, :] = middle

        tiles(256, body)
        keep("wide", None, wide.at[1], proj_out, 5)
        keep("middle", None, wide.at[0], mid_out, 6)

    def norm_two():
        def body(rows):
            normed = layer_rows(wide[0, rows, :])
            hidden[rows, :] = (
                normed * (1.0 + of_segment(rows, 4)) + of_segment(rows, 3)
            ).astype(bf16)

        tiles(128, body)
        turn(hidden, h2_out, 7)

    def expand_block(j):
        finish("wide")
        finish("turned")
        if j < 3:
            finish("slab", j)

        def body(i, carry):
            rows = pl.ds(pl.multiple_of(i * SPAN, SPAN), SPAN)
            before = dot(hidden[rows, :], matrix(4 + j)) + bias_row(3 + j)
            wide[1, rows, :] = before
            low = gelu(before).astype(bf16)
            slabs[j, i] = low
            turned[:, rows] = low.T
            return carry

        lax.fori_loop(0, count // SPAN, body, 0)
        keep("wide", None, wide.at[1], before_out[j], 8 + j)
        keep("turned", None, turned, act_out.at[j], 12 + j)

    def contract():
        finish("wide")

        def body(i, carry):
            rows = pl.ds(pl.multiple_of(i * SPAN, SPAN), SPAN)
            result = dot(slabs[0, i], w_con[0:2].reshape(8 * n, width))
            for q in range(1, 4):
                result = result + dot(slabs[q, i], w_con[2 * q : 2 * q + 2].reshape(8 * n, width))
            result = result + bias_row(7)
            wide[1, rows, :] = result
            padded[rows, :] = (wide[0, rows, :] + of_segment(rows, 5) * result).astype(bf16)
            return carry

        lax.fori_loop(0, count // SPAN, body, 0)
        keep("wide", None, wide.at[1], ff_out, 16)
        keep("out", None, padded, y_out, 17)

    plan = [0, multiply, 1, 2, sum_x, 3, 4, sum_z, 5, norm_one, 6, spread_hidden, 7]
    plan += [partial(project, 0), 8, partial(project, 2), 9, 10, partial(project, 1), 11]
    for first in range(0, 16, 2):
        plan += [partial(attend_heads, first, first + 2)] + ([12 + first // 4] if first % 4 else [])
    plan += [gather_back, 16, add_projected, norm_two, 17]
    plan += [partial(expand_block, 0), 18, partial(expand_block, 1), 19]
    plan += [partial(expand_block, 2), 20, partial(expand_block, 3), 21, 22, 23, 24, 25, 26]
    for item in plan + [contract]:
        if isinstance(item, int):
            step(item)
        else:
            item()
    for copy in sent:
        copy.wait_send()
    for copy in outs + list(kept.values()):
        copy.wait()


def forward_fast(own_parts, cond_silu, bias_low, mod_low, starts, segments, tokens):
    attention, projection, expand, contract = own_parts
    width = projection.shape[1]
    n = attention.shape[0]
    count = tokens.shape[0]
    low = [part.astype(bf16) for part in own_parts]
    n_seg = cond_silu.shape[0]
    cond = cond_silu.astype(f32).reshape(n_seg, 8, n).transpose(1, 0, 2)
    cond = jnp.pad(jnp.concatenate([cond, cond], axis=1), ((0, 0), (0, 0), (0, 256 - n)))
    row = lax.axis_index("rows")
    window = 128 * 16 * jnp.maximum(row - 1, 0)
    bias = lax.dynamic_update_slice(
        jnp.zeros(4096, bf16), bias_low, (row * bias_low.shape[0] - window,)
    ).reshape(32, 128)
    sems = pltpu.SemaphoreType.DMA

    def shape(dtype, *dims):
        return jax.ShapeDtypeStruct(dims, dtype)

    outs = pl.pallas_call(
        forward_kernel,
        out_shape=(shape(bf16, 8, n, width),) * 8
        + (shape(bf16, 2, 4, n, width),) * 4
        + (shape(bf16, 4, SPAN, width),) * 3
        + (shape(f32, count, width),) * 4
        + (
            shape(f32, 8, 3 * width),
            shape(bf16, 2, width, count),
            shape(f32, count, width),
            shape(f32, count, width),
            shape(bf16, width, count),
            shape(bf16, 4, width, count),
            shape(f32, count, width),
            shape(bf16, count, width),
        ),
        in_specs=[ANY] * 4 + [VM, VM, VM, SM, VM, VM],
        out_specs=(ANY,) * 19 + (VM,) + (ANY,) * 7,
        scratch_shapes=[
            pltpu.VMEM((8, 8, n, width), bf16),
            pltpu.VMEM((8, 4, n, width), bf16),
            pltpu.VMEM((8, 8, 256), f32),
            pltpu.VMEM((8, 32, 128), bf16),
            pltpu.VMEM((128, 128), f32),
            pltpu.VMEM((4, 2, 8, 3 * width), f32),
            pltpu.VMEM((4, 8, 3 * width), f32),
            pltpu.VMEM((3, 8, 3 * width), f32),
            pltpu.VMEM((4, 4, SPAN, width), bf16),
            pltpu.VMEM((count, width), bf16),
            pltpu.VMEM((2, count, width), f32),
            pltpu.VMEM((count, width), bf16),
            pltpu.VMEM((width, count), bf16),
            sems((14,)),
            sems((14,)),
            sems((4,)),
            sems((4,)),
        ]
        + [sems((6, 3))] * 2
        + [sems((6, 4))] * 6
        + [sems((6,)), sems((12,)), sems((18,))],
        compiler_params=pltpu.CompilerParams(
            collective_id=0, has_side_effects=True, vmem_limit_bytes=60 << 20
        ),
        name="forward",
    )(*low, cond, bias, mod_low, starts, segments[:, None], tokens)
    w = [block.reshape(8 * n, width) for block in outs[:8]]
    con = [block.reshape(8 * n, width) for block in outs[8:12]]
    modulation = jnp.concatenate([outs[19][:n_seg], outs[19][n_seg:]], axis=1)
    weights = (tuple(w[:3]), w[3], tuple(w[4:]), con)
    pair, projected, middle, h2, act, feedforward, output = outs[20:]
    lefts = (
        pair.reshape(2, 8, n, count),
        h2.reshape(8, n, count),
        act.reshape(8, 4, n, count),
    )
    saved = (modulation, outs[12:15], projected, middle, outs[15:19], feedforward, lefts)
    return output, saved, weights


def of_tokens(onehot, modulation, width):
    rows = sum(onehot[:, s : s + 1] * modulation[s] for s in range(onehot.shape[1]))
    return [rows[:, j * width : (j + 1) * width] for j in range(6)]


def forward_plain(own_parts, cond_silu, bias_low, mod_low, starts, segments, tokens):
    def whole(part):
        return lax.all_gather(part.astype(bf16), "rows", axis=0, tiled=True)

    attention, projection, expand, contract = own_parts
    width = projection.shape[1]
    att, w_proj, exp, w_con = map(whole, own_parts)
    w_att = tuple(att[:, j * width : (j + 1) * width] for j in range(3))
    w_exp = tuple(exp[:, j * width : (j + 1) * width] for j in range(4))
    shard = mod_low.shape[0]
    cond = lax.all_gather(cond_silu, "rows", axis=0, tiled=True)
    cond = lax.dynamic_slice_in_dim(cond, lax.axis_index("rows") * shard, shard, axis=1)
    modulation = lax.psum_scatter(dot(cond, mod_low), "rows", scatter_dimension=0, tiled=True)
    biases = whole(bias_low).astype(f32)
    bias = [biases[j * width : (j + 1) * width] for j in range(14)]
    modulation = modulation + biases[8 * width :]
    onehot = (segments[:, None] == jnp.arange(cond_silu.shape[0])[None, :]).astype(f32)
    shift_one, scale_one, gate_one, shift_two, scale_two, gate_two = of_tokens(
        onehot, modulation, width
    )
    wide = tokens.astype(f32)
    hidden_one = (layer_norm(wide)[0] * (1.0 + scale_one) + shift_one).astype(bf16)
    query = (dot(hidden_one, w_att[0]) + bias[0]).astype(bf16)
    key = dot(hidden_one, w_att[1]).astype(bf16)
    value = (dot(hidden_one, w_att[2]) + bias[1]).astype(bf16)
    attended, *slabs = attend(starts, query, key, value)
    projected = dot(attended, w_proj) + bias[2]
    middle = wide + gate_one * projected
    hidden_two = (layer_norm(middle)[0] * (1.0 + scale_two) + shift_two).astype(bf16)
    before = [dot(hidden_two, part) + bias[3 + j] for j, part in enumerate(w_exp)]
    activated = jnp.concatenate([gelu(part).astype(bf16) for part in before], axis=1)
    feedforward = dot(activated, w_con) + bias[7]
    output = (middle + gate_two * feedforward).astype(bf16)
    w_con = [w_con[j * width : (j + 1) * width] for j in range(4)]
    lefts = (hidden_one, attended, hidden_two, activated)
    saved = (modulation, slabs, projected, middle, before, feedforward, lefts)
    return output, saved, (w_att, w_proj, w_exp, w_con)


AHEAD = 2


def gather_last(value):
    value = jnp.stack([value] + [over_z(value, k) for k in (1, 2, 3)])
    for over in (over_x, over_y, over_core):
        value = jnp.concatenate([value, over(value)])
    return value


class Reduce:
    def __init__(self, out, refs, units):
        self.out = out
        self.d, self.y_in, self.x_in, self.z_in, self.total, self.y2_in, self.grad = refs[:7]
        self.y_s, self.y_r, self.x_s, self.x_r, self.z_s, self.z_r = refs[7:13]
        self.y2_s, self.y2_r, self.c_s, self.c_r, self.store = refs[13:]
        row, seg = lax.axis_index("rows"), lax.axis_index("seg")
        self.row, self.x, self.z = row, row % 2, row // 2
        self.y, self.c = seg // 2, seg % 2
        self.units = units
        self.slots, _, n, self.width = self.d.shape
        self.piece = piece = n // 3
        self.part = pl.multiple_of(self.y * piece, piece)
        self.mine = pl.multiple_of(self.y * 2 * piece, piece)
        self.theirs = pl.multiple_of((1 - self.y) * 2 * piece, piece)
        self.level = [lax.rem(self.z + k, 4) for k in range(4)]
        self.z_peers = [(self.level[k] * 2 + self.x, seg) for k in range(4)]
        self.x_peer = (row + 1 - 2 * self.x, seg)
        self.y_peer = (row, seg + 2 - 4 * self.y)
        self.c_peer = (row, seg + 1 - 2 * self.c)
        self.sent, self.outs = {u: [] for u in range(units)}, []
        self.ready, self.next_y = -1, 0
        self.steps = [(u, k) for u in range(self.units) for k in (1, 3, 2, 0)]
        self.count = len(self.steps) + 8

    def greet(self):
        greet(self.z_peers[1:] + [self.x_peer, self.y_peer, self.c_peer])

    def go(self, u, copy):
        copy.start()
        self.sent[u].append(copy)

    def drain(self, u):
        for copy in self.sent.pop(u, ()):
            copy.wait_send()

    def add(self, *terms):
        result = terms[0].astype(f32)
        for term in terms[1:]:
            result = result + term.astype(f32)
        return result.astype(bf16)


    def to_y(self, u, k):
        i = u % self.slots
        src = self.d.at[i, pl.ds(self.level[k] * 2, 2), pl.ds(self.theirs, self.piece)]
        return remote(src, self.y_in.at[i, k], self.y_s.at[u, k], self.y_r.at[u, k], self.y_peer)

    def to_x(self, u, k):
        i = u % self.slots
        src = self.d.at[i, self.level[k] * 2 + 1 - self.x, pl.ds(self.part, 2 * self.piece)]
        return remote(src, self.x_in.at[i, k], self.x_s.at[u, k], self.x_r.at[u, k], self.x_peer)

    def to_z(self, u, k):
        i = u % self.slots
        src = self.d.at[i, self.level[k] * 2 + self.x, pl.ds(self.part, 2 * self.piece)]
        return remote(
            src, self.z_in.at[i, k - 1], self.z_s.at[u, k - 1], self.z_r.at[u, k - 1], self.z_peers[k]
        )

    def to_y_again(self, u):
        i = u % self.slots
        return remote(
            self.total.at[i], self.y2_in.at[i], self.y2_s.at[u], self.y2_r.at[u], self.y_peer
        )

    def to_core(self, u):
        ref = self.grad.at[u, self.c]
        return remote(ref, ref, self.c_s.at[u], self.c_r.at[u], self.c_peer)

    def begin(self, u):
        self.ready = u

    def pump(self, limit):
        while self.next_y < min(limit, len(self.steps)) and self.steps[self.next_y][0] <= self.ready:
            u, k = self.steps[self.next_y]
            self.go(u, self.to_y(u, k))
            self.next_y += 1

    def step(self, j):
        self.pump(j + 1 + AHEAD)
        d, piece = self.d, self.piece
        mine, part = pl.ds(self.mine, piece), pl.ds(self.part, 2 * piece)
        if j < len(self.steps):
            u, k = self.steps[j]
            i = u % self.slots
            self.to_y(u, k).wait_recv()
            for side in range(2):
                r = self.level[k] * 2 + side
                d[i, r, mine] = self.add(d[i, r, mine], self.y_in[i, k, side])
            self.go(u, self.to_x(u, k))
        if 0 <= j - 1 < len(self.steps):
            u, k = self.steps[j - 1]
            i = u % self.slots
            self.to_x(u, k).wait_recv()
            r = self.level[k] * 2 + self.x
            d[i, r, part] = self.add(d[i, r, part], self.x_in[i, k])
            if k:
                self.go(u, self.to_z(u, k))
        if j >= 5 and (j - 5) % 4 == 0 and (j - 5) // 4 < self.units:
            u = (j - 5) // 4
            i = u % self.slots
            for k in (1, 3, 2):
                self.to_z(u, k).wait_recv()
            z_in = self.z_in
            self.total[i] = self.add(d[i, self.row, part], z_in[i, 0], z_in[i, 1], z_in[i, 2])
            self.go(u, self.to_y_again(u))
        if j >= 6 and (j - 6) % 4 == 0 and (j - 6) // 4 < self.units:
            u = (j - 6) // 4
            i = u % self.slots
            self.to_y_again(u).wait_recv()
            total, y2_in, grad, c = self.total, self.y2_in, self.grad, self.c
            here = pl.ds(pl.multiple_of(self.y * piece, piece), piece)
            there = pl.ds(pl.multiple_of((1 - self.y) * piece, piece), piece)
            grad[u, c, mine] = total[i, here]
            grad[u, c, pl.ds(self.theirs, piece)] = y2_in[i, there]
            grad[u, c, pl.ds(piece, piece)] = self.add(total[i, there], y2_in[i, here])
            self.go(u, self.to_core(u))
        if j >= 7 and (j - 7) % 4 == 0 and (j - 7) // 4 < self.units:
            u = (j - 7) // 4
            self.to_core(u).wait_recv()
            copy = pltpu.make_async_copy(self.grad.at[u], self.out.at[u], self.store.at[u])
            copy.start()
            self.outs.append(copy)

    def finish(self):
        for u in range(self.units):
            self.drain(u)
        for copy in self.outs:
            copy.wait()

    @staticmethod
    def scratch(units, slots, n, width):
        sems = pltpu.SemaphoreType.DMA

        def space(*shape):
            return pltpu.VMEM(shape + (width,), bf16)

        return (
            [
                space(slots, 8, n),
                space(slots, 4, 2, n // 3),
                space(slots, 4, 2 * n // 3),
                space(slots, 3, 2 * n // 3),
                space(slots, 2 * n // 3),
                space(slots, 2 * n // 3),
                space(units, 2, n),
            ]
            + [sems((units, 4))] * 4
            + [sems((units, 3))] * 2
            + [sems((units,))] * 5
        )


def multiply_pair(out, lefts, rights):
    n, width = out.shape[1:]

    def one(i, carry):
        rows = pl.ds(2 * i, 2)
        total = 0.0
        for left, right in zip(lefts, rights):
            total = total + dot(left[rows].reshape(2 * n, left.shape[2]), right[...])
        out[rows] = total.astype(bf16).reshape(2, n, width)
        return carry

    lax.fori_loop(0, 4, one, 0)


def reduce_kernel(
    act, feed, hidden, b0, b1, b2, b3, pair, project, starts, qs, ks, vs, up, out, qv, dk, left, right,
    near, far_s, far_r, save_sem, free, *refs
):
    red = Reduce(out, refs, 6)
    c, count = red.c, up.shape[0]
    rows = pl.ds(0, count)

    def near_copy(index, src, dst):
        return pltpu.make_async_copy(src, dst, near.at[index])

    def far_copy(index, src, dst):
        return remote(src, dst, far_s.at[index], far_r.at[index], red.c_peer)

    def lefts(i):
        return left.at[2 * i], left.at[2 * i + 1]

    def rights(i):
        return right.at[2 * i, rows], right.at[2 * i + 1, rows]

    fixed = [
        (act.at[:, c], act.at[:, 1 - c], lefts(0)),
        (feed, feed, rights(0)),
        (act.at[:, 2 + c], act.at[:, 3 - c], lefts(1)),
        (hidden, hidden, lefts(2)),
    ]
    pulls = [
        ((near_copy(i, here, dst[0]),) * 2, (far_copy(i, there, dst[1]),) * 2)
        for i, (here, there, dst) in enumerate(fixed)
    ]
    for i, two in ((4, (b0, b1)), (5, (b2, b3))):
        dst = rights(i - 3)
        pulls.append(
            (
                tuple(near_copy(i, two[core], dst[0]) for core in range(2)),
                tuple(far_copy(i, two[1 - core], dst[1]) for core in range(2)),
            )
        )
    late_far = right.at[0, rows], right.at[1, rows]
    pulls.append(((near_copy(6, pair.at[c], left.at[0]),) * 2, (far_copy(6, pair.at[1 - c], left.at[1]),) * 2))
    pulls.append(((near_copy(7, pair.at[0], left.at[2]),) * 2, (far_copy(7, pair.at[0], left.at[3]),) * 2))
    pulls.append(
        (
            (None, near_copy(8, project, right.at[2, rows])),
            (far_copy(8, project, late_far[0]), far_copy(8, right.at[3, rows], late_far[0])),
        )
    )
    pulls.append(
        ((None, None), (far_copy(9, right.at[5 - c, rows], late_far[1]),) * 2)
    )

    def start(index, side):
        two = pulls[index][side]
        if two[0] is two[1]:
            if two[0] is not None:
                two[0].start()
            return
        for core in range(2):
            if two[core] is not None:

                @pl.when(c == core)
                def _():
                    two[core].start()

    def arrive(index):
        two, far = pulls[index]
        if two[0] is None and two[1] is not None:

            @pl.when(c == 1)
            def _():
                two[1].wait()
        elif two[0] is not None:
            two[0].wait()
        far[0].wait()

    def block(u):
        for index in ((0, 1), (2,), (3, 4), (5,))[u]:
            arrive(index)
        for index in ((2, 3, 4), (5,), (), ())[u]:
            start(index, 1)
        multiply_pair(red.d.at[u], lefts(min(u, 2)), rights(max(u - 1, 0)))
        red.begin(u)
        if u == 0:
            red.pump(AHEAD)

    def late_pulls():
        pl.semaphore_signal(
            free, inc=1, device_id=red.c_peer, device_id_type=pl.DeviceIdType.MESH
        )
        for index in (6, 7, 8):
            start(index, 0)
        pl.semaphore_wait(free, 1)
        for index in (6, 8, 7, 9):
            start(index, 1)

    def late_block(u):
        for index in ((6, 8), (7, 9))[u - 4]:
            arrive(index)
        red.drain(u - 4)
        own = right.at[3 - c, rows] if u == 4 else right.at[4 + c, rows]
        multiply_pair(red.d.at[u - 4], lefts(u - 4), (own, late_far[u - 4]))
        red.begin(u)

    def spread_up():
        def one(s, carry):
            place = pl.ds(pl.multiple_of(s * SPAN, SPAN), SPAN)
            right[3, place, :] = spread_rows(starts, up, s).astype(bf16)
            return carry

        lax.fori_loop(0, 4, one, 0)

    def heads(first, last):
        def one(s, carry):
            place = pl.ds(pl.multiple_of(s * SPAN, SPAN), SPAN)
            back_slab_flat(starts, s, place, qs, ks, vs, right, range(first, last))
            return carry

        lax.fori_loop(0, 4, one, 0)

    kept = []

    def collect(which, slot, dst):
        def one(i, carry):
            place = pl.ds(pl.multiple_of(i * SPAN, SPAN), SPAN)
            right[slot, place, :] = home_rows(starts, i, right[which], 4).astype(bf16)
            return carry

        lax.fori_loop(0, count // SPAN, one, 0)
        copy = pltpu.make_async_copy(right.at[slot, rows], dst, save_sem.at[which])
        copy.start()
        kept.append(copy)

    for index in (0, 1, 2, 3, 4, 5):
        start(index, 0)
    red.greet()
    for index in (0, 1):
        start(index, 1)
    plan = [partial(block, 0), partial(block, 1), 0, partial(block, 2), 1, partial(block, 3), 2]
    plan += [spread_up, 3]
    for first in range(0, 16, 2):
        plan += [partial(heads, first, first + 2), 4 + first // 2]
    plan += [partial(collect, 0, 4, qv.at[0]), partial(collect, 2, 5, qv.at[1]), 12]
    plan += [partial(collect, 1, 3, dk), late_pulls, 13, 14, partial(late_block, 4), 15]
    plan += [partial(late_block, 5)] + list(range(16, red.count))
    for item in plan:
        if isinstance(item, int):
            red.step(item)
        else:
            item()
    red.finish()
    for copy in kept:
        copy.wait()


def reduce_all(lefts, feed, befores, project, starts, slabs, up):
    pair, hidden, act = lefts
    n = act.shape[2]
    count, width = feed.shape
    sems = pltpu.SemaphoreType.DMA
    return pl.pallas_call(
        reduce_kernel,
        out_shape=(
            jax.ShapeDtypeStruct((6, 2, n, width), bf16),
            jax.ShapeDtypeStruct((2, count, width), bf16),
            jax.ShapeDtypeStruct((count, width), bf16),
        ),
        in_specs=[ANY] * 9 + [SM] + [VM] * 4,
        out_specs=(ANY,) * 3,
        scratch_shapes=[
            pltpu.VMEM((6, 8, n, count), bf16),
            pltpu.VMEM((6, 4 * SPAN, width), bf16),
            sems((9,)),
            sems((10,)),
            sems((10,)),
            sems((3,)),
            pltpu.SemaphoreType.REGULAR,
        ]
        + Reduce.scratch(6, 4, n, width),
        compiler_params=pltpu.CompilerParams(
            collective_id=1, has_side_effects=True, vmem_limit_bytes=60 << 20
        ),
        cost_estimate=pl.CostEstimate(
            flops=180_000_000_000, bytes_accessed=60_000_000, transcendentals=0
        ),
        name="reduce",
    )(act, feed, hidden, *befores, pair, project, starts, *slabs, up)


def reduce_fast(lefts, feed, befores, starts, slabs, up, back_project):
    width = feed.shape[1]
    sums, qv, back_key = reduce_all(lefts, feed, befores, back_project, starts, slabs, up)

    def late():
        con = sums[0:2].reshape(-1, width)
        exp = jnp.concatenate([sums[2, 0], sums[2, 1], sums[3, 0], sums[3, 1]], axis=1)
        att = jnp.concatenate([sums[5, 0], sums[4, 0], sums[5, 1]], axis=1)
        return tuple(part.astype(f32) for part in (att, sums[4, 1], exp, con))

    return (qv[0], back_key, qv[1]), late


def reduce_plain(lefts, feed, befores, starts, slabs, up, back_project):
    hidden_one, attended, hidden_two, activated = lefts
    back_query, back_key, back_value = attend_back(starts, *slabs, up)

    def total(left, right):
        part = lax.psum_scatter(
            outer(left, right).astype(bf16), "rows", scatter_dimension=0, tiled=True
        )
        return lax.psum(part.astype(f32), "seg")

    def late():
        att = total(hidden_one, jnp.concatenate([back_query, back_key, back_value], axis=1))
        exp = total(hidden_two, jnp.concatenate(befores, axis=1))
        return att, total(attended, back_project), exp, total(activated, feed)

    return (back_query, back_key, back_value), late


def on_device(
    fast,
    tokens,
    condition,
    segment_ids,
    cotangent,
    modulation_master,
    modulation_first,
    modulation_second,
    attention_master,
    attention_first,
    attention_second,
    projection_master,
    projection_first,
    projection_second,
    expand_master,
    expand_first,
    expand_second,
    contract_master,
    contract_first,
    contract_second,
    bias_master,
    bias_first,
    bias_second,
):
    width = tokens.shape[1]
    hidden = expand_master.shape[1]
    shard = modulation_master.shape[0]
    n_seg = condition.shape[1]
    row = lax.axis_index("rows")
    segments = segment_ids[0]
    onehot = (segments[:, None] == jnp.arange(n_seg, dtype=jnp.int32)[None, :]).astype(f32)
    starts = jnp.sum(
        segments[:, None] < jnp.arange(n_seg + 1, dtype=jnp.int32)[None, :], axis=0, dtype=jnp.int32
    )
    tokens_wide = tokens.astype(f32)
    upstream = cotangent.astype(f32)

    cond_silu = jax.nn.silu(condition[0].astype(f32)).astype(bf16)
    forward = forward_fast if fast else forward_plain
    output, saved, (w_att, w_proj, w_exp, w_con) = forward(
        (attention_master, projection_master, expand_master, contract_master),
        cond_silu,
        bias_master.astype(bf16),
        modulation_master.astype(bf16),
        starts,
        segments,
        tokens,
    )
    modulation, slabs, projected, middle, before, feedforward, lefts = saved
    shift_one, scale_one, gate_one, shift_two, scale_two, gate_two = of_tokens(
        onehot, modulation, width
    )
    normed_one, inverse_one = layer_norm(tokens_wide)
    normed_two, inverse_two = layer_norm(middle)

    back_gate_two = upstream * feedforward
    back_feed = (upstream * gate_two).astype(bf16)
    back_before = []
    for j, part in enumerate(before):
        back_active = back_dot(back_feed, w_con[j])
        back_before.append(jax.vjp(gelu, part)[1](back_active)[0].astype(bf16))
    back_hidden_two = sum(back_dot(back_before[j], w_exp[j]) for j in range(4))
    back_middle = upstream + norm_back(back_hidden_two * (1.0 + scale_two), normed_two, inverse_two)
    back_gate_one = back_middle * projected
    back_project = (back_middle * gate_one).astype(bf16)
    back_attend = back_dot(back_project, w_proj).astype(bf16)
    def segment_sums(*parts):
        return [outer(onehot, part, highest) for part in parts]

    def column_sums(*parts):
        return [jnp.sum(part.astype(f32), axis=0, keepdims=True) for part in parts]

    early = jnp.concatenate(
        segment_sums(
            back_gate_one, back_hidden_two, back_hidden_two * normed_two, back_gate_two
        )
        + [cond_silu.astype(f32)]
        + column_sums(back_project, *back_before, back_feed),
        axis=0,
    )
    back_attend, early = lax.optimization_barrier((back_attend, early))
    early = lax.all_gather(early.astype(bf16), ("rows", "seg"), axis=0)
    reduce = reduce_fast if fast else reduce_plain
    (back_query, back_key, back_value), late = reduce(
        lefts, back_feed, back_before, starts, slabs, back_attend, back_project
    )
    back_hidden_one = (
        back_dot(back_query, w_att[0]) + back_dot(back_key, w_att[1]) + back_dot(back_value, w_att[2])
    )
    back_tokens = back_middle + norm_back(
        back_hidden_one * (1.0 + scale_one), normed_one, inverse_one
    )
    last = segment_sums(back_hidden_one, back_hidden_one * normed_one)
    last = last + [cond_silu.astype(f32)] + column_sums(back_query, back_value)
    last = jnp.concatenate(last, axis=0)
    last = jnp.pad(last, ((0, -last.shape[0] % 16), (0, 0))).astype(bf16)
    last, early = lax.optimization_barrier((last, early))
    if fast:
        last = gather_last(last)
    else:
        last = lax.all_gather(last, ("rows", "seg"), axis=0)
    grad_att, grad_proj, grad_exp, grad_con = late()

    def part_of(rows, number):
        return rows[:, number * n_seg : (number + 1) * n_seg].reshape(-1, width)

    def mod_gradient(conds, parts):
        conds = lax.dynamic_slice_in_dim(conds, row * shard, shard, axis=1)
        return outer(conds, jnp.concatenate(parts, axis=1))

    mods = [part_of(last, j) for j in range(2)], [part_of(early, j) for j in range(4)]
    grad_mod = jnp.concatenate(
        [mod_gradient(part_of(last, 2), mods[0]), mod_gradient(part_of(early, 4), mods[1])], axis=1
    )
    totals = [last[:, 3 * n_seg : 3 * n_seg + 2], early[:, 5 * n_seg :]]
    totals = [jnp.sum(part.astype(f32), axis=0) for part in totals]
    totals += [
        jnp.sum(part.astype(f32), axis=0, keepdims=True) for part in mods[0] + mods[1]
    ]
    grad_bias = lax.dynamic_slice_in_dim(
        jnp.concatenate(totals, axis=0).reshape(-1),
        row * bias_master.shape[0],
        bias_master.shape[0],
    )
    results = [
        adam_update(*operands)
        for operands in (
            (grad_mod, modulation_master, modulation_first, modulation_second),
            (grad_att, attention_master, attention_first, attention_second),
            (grad_proj, projection_master, projection_first, projection_second),
            (grad_exp, expand_master, expand_first, expand_second),
            (grad_con, contract_master, contract_first, contract_second),
            (grad_bias, bias_master, bias_first, bias_second),
        )
    ]
    flat = tuple((item for result in results for item in result))
    return (output, back_tokens.astype(bf16)) + flat


def solution(mesh):
    both = ("rows", "seg")
    fast = mesh.shape["rows"] == 8 and mesh.shape["seg"] == 4
    token, matrix, vector = P(both, None), P("rows", None), P("rows")
    in_specs = (token, P(both, None, None), token, token) + (matrix,) * 15 + (vector,) * 3
    out_specs = (token, token) + (matrix,) * 15 + (vector,) * 3
    return jax.shard_map(
        partial(on_device, fast),
        mesh=mesh,
        in_specs=in_specs,
        out_specs=out_specs,
        check_vma=False,
    )
```

```python
from functools import partial

import jax
import jax.numpy as jnp
from jax import lax
from jax.experimental import pallas as pl
from jax.experimental.pallas import tpu as pltpu
from jax.sharding import PartitionSpec as P

HEAD_DIM = 72
STEP = 10
SPAN = 256
EXP_SCALE = HEAD_DIM**-0.5 * 1.4426950408889634

bf16 = jnp.bfloat16
f32 = jnp.float32
highest = lax.Precision.HIGHEST
beta_first = 0.9
beta_second = 0.999
learning = 0.06
weight_decay = 0.1
adam_epsilon = 1e-08
norm_epsilon = 1e-06

ROW_X = [(z * 2 + x, z * 2 + 1 - x) for z in range(4) for x in range(2)]
ROW_Z = [
    [(z * 2 + x, (z + k) % 4 * 2 + x) for z in range(4) for x in range(2)] for k in range(4)
]
SEG_Y = [(y * 2 + c, (1 - y) * 2 + c) for y in range(2) for c in range(2)]
SEG_C = [(y * 2 + c, y * 2 + 1 - c) for y in range(2) for c in range(2)]


def over_x(v):
    return lax.ppermute(v, "rows", ROW_X)


def over_z(v, k):
    return lax.ppermute(v, "rows", ROW_Z[k])


def over_y(v):
    return lax.ppermute(v, "seg", SEG_Y)


def over_core(v):
    return lax.ppermute(v, "seg", SEG_C)


def place():
    row = lax.axis_index("rows")
    seg = lax.axis_index("seg")
    return row % 2, seg // 2, row // 2, seg % 2


def layer_norm(values):
    center = values - jnp.mean(values, axis=-1, keepdims=True)
    inverse = lax.rsqrt(jnp.mean(center * center, axis=-1, keepdims=True) + norm_epsilon)
    return (center * inverse, inverse)


def norm_back(upstream, normed, inverse):
    return inverse * (
        upstream
        - jnp.mean(upstream, axis=-1, keepdims=True)
        - normed * jnp.mean(upstream * normed, axis=-1, keepdims=True)
    )


def outer(left, right, precision=None):
    return lax.dot_general(
        left,
        right,
        (((0,), (0,)), ((), ())),
        precision=precision,
        preferred_element_type=f32,
    )


def dot(left, right):
    return jnp.dot(left, right, preferred_element_type=f32)


def back_dot(left, right):
    return lax.dot_general(left, right, (((1,), (1,)), ((), ())), preferred_element_type=f32)


def spread_rows(starts, source, s):
    rows = source.shape[0]
    row = lax.broadcasted_iota(jnp.int32, (SPAN, rows), 0) + starts[s]
    col = lax.broadcasted_iota(jnp.int32, (SPAN, rows), 1)
    pick = jnp.where((col == row) & (row < starts[s + 1]), 1.0, 0.0).astype(bf16)
    return dot(pick, source[...])

def spread(starts, source, out):
    def one(s,_):
        out[s]=spread_rows(starts,source,s).astype(bf16)
        return 0
    lax.fori_loop(0,out.shape[0],one,0)

def home_rows(starts, i, flat, n):
    row = lax.broadcasted_iota(jnp.int32, (SPAN, 1), 0) + i * SPAN
    home = row
    for s in range(1, n):
        home = home + jnp.where(row >= starts[s], SPAN - (starts[s] - starts[s - 1]), 0)
    pick = jnp.where(lax.broadcasted_iota(jnp.int32, (SPAN, n * SPAN), 1) == home, 1.0, 0.0)
    return dot(pick.astype(bf16), flat)


def unspread(starts, slabs, out):
    n, _, width = slabs.shape

    def one(i, carry):
        place = pl.ds(pl.multiple_of(i * SPAN, SPAN), SPAN)
        flat = slabs[...].reshape(n * SPAN, width)
        out[place, :] = home_rows(starts, i, flat, n).astype(bf16)
        return carry

    lax.fori_loop(0, out.shape[0] // SPAN, one, 0)


def attend_slab(starts, s, qs, ks, vs, os, heads):
    length = starts[s + 1] - starts[s]
    outside = jnp.where(lax.broadcasted_iota(jnp.int32, (SPAN, 1), 0) < length, 0.0, -1e30)
    for h in heads:
        cols = slice(h * HEAD_DIM, (h + 1) * HEAD_DIM)
        score = back_dot(ks[s, :, cols], qs[s, :, cols]) + outside
        power = jnp.exp2((score - jnp.max(score, axis=0, keepdims=True)) * EXP_SCALE)
        soft = (power * (1.0 / jnp.sum(power, axis=0, keepdims=True))).astype(bf16)
        os[s, :, cols] = outer(soft, vs[s, :, cols]).astype(bf16)


def attend_kernel(starts, q, k, v, out, qs, ks, vs, os):
    for src, dst in ((q, qs), (k, ks), (v, vs)):
        spread(starts, src, dst)

    def seg(s, carry):
        attend_slab(starts, s, qs, ks, vs, os, range(qs.shape[2] // HEAD_DIM))
        return carry

    lax.fori_loop(0, qs.shape[0], seg, 0)
    unspread(starts, os, out)

def back_slab(starts, s, qs, ks, vs, ups, dqs, dks, dvs, heads):
    scale = HEAD_DIM**-0.5
    length = starts[s + 1] - starts[s]
    outside = jnp.where(lax.broadcasted_iota(jnp.int32, (SPAN, 1), 0) < length, 0.0, -1e30)
    for h in heads:
        cols = slice(h * HEAD_DIM, (h + 1) * HEAD_DIM)
        query, key, value, upstream = (part[s, :, cols] for part in (qs, ks, vs, ups))
        score = back_dot(key, query) + outside
        power = jnp.exp2((score - jnp.max(score, axis=0, keepdims=True)) * EXP_SCALE)
        soft = power * (1.0 / jnp.sum(power, axis=0, keepdims=True))
        back_soft = back_dot(value, upstream)
        mean = jnp.sum(back_soft * soft, axis=0, keepdims=True)
        back_score = (soft * (back_soft - mean)).astype(bf16)
        dvs[s, :, cols] = dot(soft.astype(bf16), upstream).astype(bf16)
        dks[s, :, cols] = (dot(back_score, query) * scale).astype(bf16)
        dqs[s, :, cols] = (outer(back_score, key) * scale).astype(bf16)


class Slab:
    def __init__(self, ref, slot, rows):
        self.ref, self.slot, self.rows = ref, slot, rows

    def __getitem__(self, index):
        return self.ref[self.slot, self.rows, index[2]]

    def __setitem__(self, index, value):
        self.ref[self.slot, self.rows, index[2]] = value


def back_slab_flat(starts, s, rows, qs, ks, vs, space, heads):
    dqs, dks, dvs, ups = (Slab(space, slot, rows) for slot in range(4))
    back_slab(starts, s, qs, ks, vs, ups, dqs, dks, dvs, heads)


def back_kernel(starts, qs, ks, vs, up, dq, dk, dv, ups, dqs, dks, dvs):
    spread(starts, up, ups)

    def seg(s, carry):
        back_slab(
            starts, s, qs, ks, vs, ups, dqs, dks, dvs, range(qs.shape[2] // HEAD_DIM)
        )
        return carry

    lax.fori_loop(0, qs.shape[0], seg, 0)
    for slabs, out in ((dqs, dq), (dks, dk), (dvs, dv)):
        unspread(starts, slabs, out)


VM = pl.BlockSpec(memory_space=pltpu.VMEM)
SM = pl.BlockSpec(memory_space=pltpu.SMEM)
ANY = pl.BlockSpec(memory_space=pl.ANY)
def attend(starts,q,k,v):
    n=starts.shape[0]-1; rows,width=q.shape
    slab=jax.ShapeDtypeStruct((n,SPAN,width),bf16)
    return pl.pallas_call(attend_kernel,out_shape=(jax.ShapeDtypeStruct(q.shape,bf16),slab,slab,slab),
        in_specs=[SM,VM,VM,VM],out_specs=(VM,)*4,
        scratch_shapes=[pltpu.VMEM((n,SPAN,width),bf16)],
        compiler_params=pltpu.CompilerParams(vmem_limit_bytes=56<<20),
        cost_estimate=pl.CostEstimate(flops=2*2*16*n*SPAN*SPAN*128,bytes_accessed=rows*width*14,transcendentals=16*n*SPAN*SPAN),name="attend")(starts,q,k,v)
def attend_back(starts,qs,ks,vs,up):
    n=starts.shape[0]-1; rows,width=up.shape
    slab=pltpu.VMEM((n,SPAN,width),bf16); o=jax.ShapeDtypeStruct(up.shape,bf16)
    return pl.pallas_call(back_kernel,out_shape=(o,o,o),
        in_specs=[SM,VM,VM,VM,VM],out_specs=(VM,)*3,
        scratch_shapes=[slab]*4,
        compiler_params=pltpu.CompilerParams(vmem_limit_bytes=56<<20),
        cost_estimate=pl.CostEstimate(flops=5*2*16*n*SPAN*SPAN*128,bytes_accessed=rows*width*14,transcendentals=16*n*SPAN*SPAN),name="attend_back")(starts,qs,ks,vs,up)


def adam_update(gradient, master, first, second):
    first_new = beta_first * first + (1.0 - beta_first) * gradient
    second_new = beta_second * second + (1.0 - beta_second) * gradient * gradient
    first_hat = first_new / (1.0 - beta_first**STEP)
    second_hat = second_new / (1.0 - beta_second**STEP)
    master_new = master - learning * (
        first_hat / (jnp.sqrt(second_hat) + adam_epsilon) + weight_decay * master
    )
    return (master_new, first_new, second_new)


def gelu(v):
    return 0.5 * v * (1.0 + jnp.tanh(0.7978845608028654 * (v + 0.044715 * (v * v * v))))


def remote(src, dst, send, recv, device):
    return pltpu.make_async_remote_copy(
        src_ref=src,
        dst_ref=dst,
        send_sem=send,
        recv_sem=recv,
        device_id=device,
        device_id_type=pl.DeviceIdType.MESH,
    )


def greet(peers):
    barrier = pltpu.get_barrier_semaphore()
    for peer in peers:
        pl.semaphore_signal(
            barrier, inc=1, device_id=peer, device_id_type=pl.DeviceIdType.MESH
        )
    pl.semaphore_wait(barrier, len(peers))


def layer_rows(values):
    center = values - jnp.mean(values, axis=-1, keepdims=True)
    return center * lax.rsqrt(jnp.mean(center * center, axis=-1, keepdims=True) + norm_epsilon)


LEAD_FROM = 4
LEAD = (2, 1, 0)


def forward_kernel(
    att_low, proj_low, exp_low, con_low, cond, bias, w_mod, starts, seg_ids, tokens, *refs
):
    w_out, con_out, slab_out, before_out = refs[:8], refs[8:12], refs[12:15], refs[15:19]
    modulation, pair_out, proj_out, mid_out, h2_out, act_out, ff_out, y_out = refs[19:27]
    rest = refs[27:]
    w, w_con, conds, bias_in, bias_all, parts, x_parts, z_parts = rest[:8]
    slabs, padded, wide, hidden, turned = rest[8:13]
    small_s, small_r, part_s, part_r = rest[13:17]
    z_s, z_r, x_s, x_r, y_s, y_r, c_s, c_r, load_sem, out_sem, save_sem = rest[17:]
    row, seg = lax.axis_index("rows"), lax.axis_index("seg")
    x, z = row % 2, row // 2
    y, c = seg // 2, seg % 2
    n, width = proj_low.shape
    count = tokens.shape[0]
    units = ((0, 2), (1, 3), (4, 5), (6, 7), (8, 9), (10, 11))
    piece = n // 3
    part = pl.multiple_of(y * piece, piece)
    third = pl.multiple_of(y * 2 * piece, piece)
    far = [lax.rem(z + 4 - k, 4) for k in range(4)]

    def block_of(u):
        return units[u][0] + c * (units[u][1] - units[u][0])

    def slot(u, r, rows):
        if u < 4:
            return w.at[block_of(u), r, rows]
        return w_con.at[r, block_of(u) - 8, rows]

    def columns(number):
        return pl.ds(pl.multiple_of(number * width, width), width)

    mine = pl.ds(part, 2 * piece)
    own = (
        att_low.at[mine, columns(2 * c)],
        None,
        exp_low.at[mine, columns(c)],
        exp_low.at[mine, columns(2 + c)],
        con_low.at[pl.ds(pl.multiple_of(c * n + part, 16), 2 * piece)],
        con_low.at[pl.ds(pl.multiple_of((2 + c) * n + part, 16), 2 * piece)],
    )
    loads = []
    for u in range(6):
        dst = slot(u, row, mine)
        if u != 1:
            copy = pltpu.make_async_copy(own[u], dst, load_sem.at[u])
            copy.start()
        else:
            two = (att_low.at[mine, columns(1)], proj_low.at[mine])
            for core in range(2):

                @pl.when(c == core)
                def _():
                    pltpu.make_async_copy(two[core], dst, load_sem.at[u]).start()

            copy = pltpu.make_async_copy(two[1], dst, load_sem.at[u])
        loads.append(copy)
    z_peers = [(lax.rem(z + k, 4) * 2 + x, seg) for k in (1, 2, 3)]
    x_peer, y_peer, c_peer = (row + 1 - 2 * x, seg), (row, seg + 2 - 4 * y), (row, seg + 1 - 2 * c)
    cross_peers = [(lax.rem(z + k, 4) * 2 + 1 - x, seg) for k in (1, 2, 3)]
    row_peers = z_peers + cross_peers + [x_peer]
    greet(row_peers + [y_peer, c_peer])
    sent = []

    def go(copy):
        copy.start()
        sent.append(copy)

    small = []
    for i, peer in enumerate(row_peers):
        small.append(remote(cond.at[peer[0]], conds.at[row], small_s.at[i], small_r.at[i], peer))
        small.append(remote(bias, bias_in.at[row], small_s.at[7 + i], small_r.at[7 + i], peer))
    for copy in small:
        go(copy)
    conds[row] = cond[row]
    bias_in[row] = bias[...]

    def to_x():
        return remote(parts.at[:, 1 - x], x_parts, part_s.at[0], part_r.at[0], x_peer)

    def to_z(k):
        src = parts.at[lax.rem(z + k, 4), x]
        return remote(src, z_parts.at[k - 1], part_s.at[k], part_r.at[k], z_peers[k - 1])

    def multiply():
        for copy in small:
            copy.wait_recv()
        left = conds[...].reshape(-1, conds.shape[2])[:, :n].astype(bf16)
        half = w_mod.shape[1] // 2
        upper = lax.broadcasted_iota(jnp.int32, (left.shape[0], 1), 0) % 8 < 4
        for start in range(0, half, width):
            both = jnp.where(
                upper,
                dot(left, w_mod[:, start : start + width]),
                dot(left, w_mod[:, half + start : half + start + width]),
            )
            parts[:, :, :, start : start + width] = both.reshape(4, 2, 8, width)
        go(to_x())
        bias_all[...] = jnp.zeros_like(bias_all)
        for r in range(8):
            rows = slice(16 * max(r - 1, 0), 16 * max(r - 1, 0) + 32)
            bias_all[rows] = bias_all[rows] + bias_in[r].astype(f32)

    def sum_x():
        to_x().wait_recv()
        for level in range(4):
            parts[level, x] = parts[level, x] + x_parts[level]
        for k in (1, 3, 2):
            go(to_z(k))

    def sum_z():
        for k in (1, 3, 2):
            to_z(k).wait_recv()
        total = parts[z, x] + z_parts[0] + z_parts[1] + z_parts[2]
        first = 3 + w_expand // width + 1
        for part_no in range(3):
            cols = slice(part_no * width, (part_no + 1) * width)
            upper = lax.broadcasted_iota(jnp.int32, (8, 1), 0) < 4
            modulation[:, cols] = total[:, cols] + jnp.where(
                upper, bias_row(first + part_no), bias_row(first + 3 + part_no)
            )

    w_expand = 4 * width

    def bias_row(number):
        tall = width // 128
        return jnp.concatenate(
            [bias_all[number * tall + i : number * tall + i + 1, :] for i in range(tall)], axis=1
        )

    def along_z(u, k):
        ref = slot(u, row, pl.ds(part, 2 * piece))
        return remote(ref, ref, z_s.at[u, k - 1], z_r.at[u, k - 1], z_peers[k - 1])

    def along_x(u, k):
        ref = slot(u, far[k] * 2 + x, pl.ds(part, 2 * piece))
        return remote(ref, ref, x_s.at[u, k], x_r.at[u, k], x_peer)

    def along_y(u, k):
        ref = slot(u, pl.ds(far[k] * 2, 2), pl.ds(third, piece))
        return remote(ref, ref, y_s.at[u, k], y_r.at[u, k], y_peer)

    def across(u, k):
        ref = slot(u, pl.ds(far[k] * 2, 2), slice(None))
        return remote(ref, ref, c_s.at[u, k], c_r.at[u, k], c_peer)

    steps = [(u, k) for u in range(6) for k in (0, 1, 3, 2)]
    outs, kept = [], {}

    def keep(name, number, src, dst, sem):
        kept[name, number] = save(src, dst, save_sem.at[sem])

    def finish(name, number=None):
        kept.pop((name, number)).wait()

    def save(src, dst, sem):
        copy = pltpu.make_async_copy(src, dst, sem)
        copy.start()
        return copy

    def send_x(j):
        u, k = steps[j]
        if j == 0:
            loads[0].wait()
            for hop in (1, 3, 2):
                go(along_z(0, hop))
        if k:
            along_z(u, k).wait_recv()
        go(along_x(u, k))
        if u < 5 and j % 4 < 3:
            if k == 0:
                loads[u + 1].wait()
            go(along_z(u + 1, (1, 3, 2)[j % 4]))

    def send_y(j):
        along_x(*steps[j]).wait_recv()
        go(along_y(*steps[j]))

    def send_across(j):
        along_y(*steps[j]).wait_recv()
        go(across(*steps[j]))

    stages = [[send_x, 0], [send_y, 0], [send_across, 0]]

    def step(j):
        for i, stage in enumerate(stages):
            while stage[1] <= min(j - i + (LEAD[i] if j >= LEAD_FROM else 0), len(steps) - 1):
                stage[0](stage[1])
                stage[1] += 1
        if 0 <= j - 3 < len(steps):
            u, k = steps[j - 3]
            across(u, k).wait_recv()
            if k == 2:
                if u < 4:
                    for b in units[u]:
                        outs.append(save(w.at[b], w_out[b], out_sem.at[b]))
                elif u == 5:
                    for q in range(4):
                        outs.append(save(w_con.at[pl.ds(2 * q, 2)], con_out[q], out_sem.at[8 + q]))


    def of_segment(rows, number):
        ids = seg_ids[rows, :]
        base, col = number // 3 * 4, number % 3 * width
        result = jnp.zeros((ids.shape[0], width), f32)
        for s in range(4):
            line = modulation[base + s : base + s + 1, col : col + width]
            result = jnp.where(ids == s, line, result)
        return result

    def tiles(size, body):
        def one(i, carry):
            body(pl.ds(pl.multiple_of(i * size, size), size))
            return carry

        lax.fori_loop(0, count // size, one, 0)

    def matrix(b):
        return w[b].reshape(8 * n, width)

    def turn(source, out, sem):
        if ("turned", None) in kept:
            finish("turned")

        def body(i, carry):
            rows = pl.ds(pl.multiple_of(i * SPAN, SPAN), SPAN)
            turned[:, rows] = source[rows, :].T
            return carry

        lax.fori_loop(0, count // SPAN, body, 0)
        keep("turned", None, turned, out, sem)

    def norm_one():
        def body(rows):
            normed = layer_rows(tokens[rows, :].astype(f32))
            padded[rows, :] = (
                normed * (1.0 + of_segment(rows, 1)) + of_segment(rows, 0)
            ).astype(bf16)

        tiles(128, body)
        turn(padded, pair_out.at[0], 0)

    def spread_hidden():
        def one(s, carry):
            slabs[3, s] = spread_rows(starts, padded, s).astype(bf16)
            return carry

        lax.fori_loop(0, 4, one, 0)

    def project(which):
        def one(s, carry):
            result = dot(slabs[3, s], matrix(which))
            if which != 1:
                result = result + bias_row(which // 2)
            slabs[which, s] = result.astype(bf16)
            return carry

        lax.fori_loop(0, 4, one, 0)
        keep("slab", which, slabs.at[which], slab_out[which], 1 + which)

    def attend_heads(first, last):
        def one(s, carry):
            attend_slab(
                starts, s, slabs.at[0], slabs.at[1], slabs.at[2], slabs.at[3], range(first, last)
            )
            return carry

        lax.fori_loop(0, 4, one, 0)

    def gather_back():
        unspread(starts, slabs.at[3], padded)
        turn(padded, pair_out.at[1], 4)

    def add_projected():
        def body(rows):
            projected = dot(padded[rows, :], matrix(3)) + bias_row(2)
            wide[1, rows, :] = projected
            middle = tokens[rows, :].astype(f32) + of_segment(rows, 2) * projected
            wide[0, rows, :] = middle

        tiles(256, body)
        keep("wide", None, wide.at[1], proj_out, 5)
        keep("middle", None, wide.at[0], mid_out, 6)

    def norm_two():
        def body(rows):
            normed = layer_rows(wide[0, rows, :])
            hidden[rows, :] = (
                normed * (1.0 + of_segment(rows, 4)) + of_segment(rows, 3)
            ).astype(bf16)

        tiles(128, body)
        turn(hidden, h2_out, 7)

    def expand_block(j):
        finish("wide")
        finish("turned")
        if j < 3:
            finish("slab", j)

        def body(i, carry):
            rows = pl.ds(pl.multiple_of(i * SPAN, SPAN), SPAN)
            before = dot(hidden[rows, :], matrix(4 + j)) + bias_row(3 + j)
            wide[1, rows, :] = before
            low = gelu(before).astype(bf16)
            slabs[j, i] = low
            turned[:, rows] = low.T
            return carry

        lax.fori_loop(0, count // SPAN, body, 0)
        keep("wide", None, wide.at[1], before_out[j], 8 + j)
        keep("turned", None, turned, act_out.at[j], 12 + j)

    def contract():
        finish("wide")

        def body(i, carry):
            rows = pl.ds(pl.multiple_of(i * SPAN, SPAN), SPAN)
            result = dot(slabs[0, i], w_con[0:2].reshape(8 * n, width))
            for q in range(1, 4):
                result = result + dot(slabs[q, i], w_con[2 * q : 2 * q + 2].reshape(8 * n, width))
            result = result + bias_row(7)
            wide[1, rows, :] = result
            padded[rows, :] = (wide[0, rows, :] + of_segment(rows, 5) * result).astype(bf16)
            return carry

        lax.fori_loop(0, count // SPAN, body, 0)
        keep("wide", None, wide.at[1], ff_out, 16)
        keep("out", None, padded, y_out, 17)

    plan = [0, multiply, 1, 2, sum_x, 3, 4, sum_z, 5, norm_one, 6, spread_hidden, 7]
    plan += [partial(project, 0), 8, partial(project, 2), 9, 10, partial(project, 1), 11]
    for first in range(0, 16, 2):
        plan += [partial(attend_heads, first, first + 2)] + ([12 + first // 4] if first % 4 else [])
    plan += [gather_back, 16, add_projected, 17, norm_two, 18]
    plan += [partial(expand_block, 0), 19, partial(expand_block, 1), 20]
    plan += [partial(expand_block, 2), 21, partial(expand_block, 3), 22, 23, 24, 25, 26]
    for item in plan + [contract]:
        if isinstance(item, int):
            step(item)
        else:
            item()
    for copy in sent:
        copy.wait_send()
    for copy in outs + list(kept.values()):
        copy.wait()


def forward_fast(own_parts, cond_silu, bias_low, mod_low, starts, segments, tokens):
    attention, projection, expand, contract = own_parts
    width = projection.shape[1]
    n = attention.shape[0]
    count = tokens.shape[0]
    low = [part.astype(bf16) for part in own_parts]
    n_seg = cond_silu.shape[0]
    cond = cond_silu.astype(f32).reshape(n_seg, 8, n).transpose(1, 0, 2)
    cond = jnp.pad(jnp.concatenate([cond, cond], axis=1), ((0, 0), (0, 0), (0, 256 - n)))
    row = lax.axis_index("rows")
    window = 128 * 16 * jnp.maximum(row - 1, 0)
    bias = lax.dynamic_update_slice(
        jnp.zeros(4096, bf16), bias_low, (row * bias_low.shape[0] - window,)
    ).reshape(32, 128)
    sems = pltpu.SemaphoreType.DMA

    def shape(dtype, *dims):
        return jax.ShapeDtypeStruct(dims, dtype)

    outs = pl.pallas_call(
        forward_kernel,
        out_shape=(shape(bf16, 8, n, width),) * 8
        + (shape(bf16, 2, 4, n, width),) * 4
        + (shape(bf16, 4, SPAN, width),) * 3
        + (shape(f32, count, width),) * 4
        + (
            shape(f32, 8, 3 * width),
            shape(bf16, 2, width, count),
            shape(f32, count, width),
            shape(f32, count, width),
            shape(bf16, width, count),
            shape(bf16, 4, width, count),
            shape(f32, count, width),
            shape(bf16, count, width),
        ),
        in_specs=[ANY] * 4 + [VM, VM, VM, SM, VM, VM],
        out_specs=(ANY,) * 19 + (VM,) + (ANY,) * 7,
        scratch_shapes=[
            pltpu.VMEM((8, 8, n, width), bf16),
            pltpu.VMEM((8, 4, n, width), bf16),
            pltpu.VMEM((8, 8, 256), f32),
            pltpu.VMEM((8, 32, 128), bf16),
            pltpu.VMEM((128, 128), f32),
            pltpu.VMEM((4, 2, 8, 3 * width), f32),
            pltpu.VMEM((4, 8, 3 * width), f32),
            pltpu.VMEM((3, 8, 3 * width), f32),
            pltpu.VMEM((4, 4, SPAN, width), bf16),
            pltpu.VMEM((count, width), bf16),
            pltpu.VMEM((2, count, width), f32),
            pltpu.VMEM((count, width), bf16),
            pltpu.VMEM((width, count), bf16),
            sems((14,)),
            sems((14,)),
            sems((4,)),
            sems((4,)),
        ]
        + [sems((6, 3))] * 2
        + [sems((6, 4))] * 6
        + [sems((6,)), sems((12,)), sems((18,))],
        compiler_params=pltpu.CompilerParams(
            collective_id=0, has_side_effects=True, vmem_limit_bytes=60 << 20
        ),
        name="forward",
    )(*low, cond, bias, mod_low, starts, segments[:, None], tokens)
    w = [block.reshape(8 * n, width) for block in outs[:8]]
    con = [block.reshape(8 * n, width) for block in outs[8:12]]
    modulation = jnp.concatenate([outs[19][:n_seg], outs[19][n_seg:]], axis=1)
    weights = (tuple(w[:3]), w[3], tuple(w[4:]), con)
    pair, projected, middle, h2, act, feedforward, output = outs[20:]
    lefts = (
        pair.reshape(2, 8, n, count),
        h2.reshape(8, n, count),
        act.reshape(8, 4, n, count),
    )
    saved = (modulation, outs[12:15], projected, middle, outs[15:19], feedforward, lefts)
    return output, saved, weights


def of_tokens(onehot, modulation, width):
    parts = [modulation[:, j * width : (j + 1) * width] for j in range(6)]
    return [
        sum(onehot[:, s : s + 1] * part[s] for s in range(onehot.shape[1])) for part in parts
    ]


def forward_plain(own_parts, cond_silu, bias_low, mod_low, starts, segments, tokens):
    def whole(part):
        return lax.all_gather(part.astype(bf16), "rows", axis=0, tiled=True)

    attention, projection, expand, contract = own_parts
    width = projection.shape[1]
    att, w_proj, exp, w_con = map(whole, own_parts)
    w_att = tuple(att[:, j * width : (j + 1) * width] for j in range(3))
    w_exp = tuple(exp[:, j * width : (j + 1) * width] for j in range(4))
    shard = mod_low.shape[0]
    cond = lax.all_gather(cond_silu, "rows", axis=0, tiled=True)
    cond = lax.dynamic_slice_in_dim(cond, lax.axis_index("rows") * shard, shard, axis=1)
    modulation = lax.psum_scatter(dot(cond, mod_low), "rows", scatter_dimension=0, tiled=True)
    biases = whole(bias_low).astype(f32)
    bias = [biases[j * width : (j + 1) * width] for j in range(14)]
    modulation = modulation + biases[8 * width :]
    onehot = (segments[:, None] == jnp.arange(cond_silu.shape[0])[None, :]).astype(f32)
    shift_one, scale_one, gate_one, shift_two, scale_two, gate_two = of_tokens(
        onehot, modulation, width
    )
    wide = tokens.astype(f32)
    hidden_one = (layer_norm(wide)[0] * (1.0 + scale_one) + shift_one).astype(bf16)
    query = (dot(hidden_one, w_att[0]) + bias[0]).astype(bf16)
    key = dot(hidden_one, w_att[1]).astype(bf16)
    value = (dot(hidden_one, w_att[2]) + bias[1]).astype(bf16)
    attended, *slabs = attend(starts, query, key, value)
    projected = dot(attended, w_proj) + bias[2]
    middle = wide + gate_one * projected
    hidden_two = (layer_norm(middle)[0] * (1.0 + scale_two) + shift_two).astype(bf16)
    before = [dot(hidden_two, part) + bias[3 + j] for j, part in enumerate(w_exp)]
    activated = jnp.concatenate([gelu(part).astype(bf16) for part in before], axis=1)
    feedforward = dot(activated, w_con) + bias[7]
    output = (middle + gate_two * feedforward).astype(bf16)
    w_con = [w_con[j * width : (j + 1) * width] for j in range(4)]
    lefts = (hidden_one, attended, hidden_two, activated)
    saved = (modulation, slabs, projected, middle, before, feedforward, lefts)
    return output, saved, (w_att, w_proj, w_exp, w_con)


AHEAD = 2


def gather_last(value, beside):
    value = jnp.stack([value] + [over_z(value, k) for k in (1, 2, 3)])
    beside = list(beside)
    for i, over in enumerate((over_x, over_y, over_core)):
        if i < 2:
            value, beside[i] = lax.optimization_barrier((value, beside[i]))
        value = jnp.concatenate([value, over(value)])
    return value, beside


class Reduce:
    def __init__(self, out, refs, units):
        self.out = out
        self.d, self.y_in, self.x_in, self.z_in, self.total, self.y2_in, self.grad = refs[:7]
        self.y_s, self.y_r, self.x_s, self.x_r, self.z_s, self.z_r = refs[7:13]
        self.y2_s, self.y2_r, self.c_s, self.c_r, self.store = refs[13:]
        row, seg = lax.axis_index("rows"), lax.axis_index("seg")
        self.row, self.x, self.z = row, row % 2, row // 2
        self.y, self.c = seg // 2, seg % 2
        self.units = units
        self.slots, _, n, self.width = self.d.shape
        self.piece = piece = n // 3
        self.part = pl.multiple_of(self.y * piece, piece)
        self.mine = pl.multiple_of(self.y * 2 * piece, piece)
        self.theirs = pl.multiple_of((1 - self.y) * 2 * piece, piece)
        self.level = [lax.rem(self.z + k, 4) for k in range(4)]
        self.z_peers = [(self.level[k] * 2 + self.x, seg) for k in range(4)]
        self.x_peer = (row + 1 - 2 * self.x, seg)
        self.y_peer = (row, seg + 2 - 4 * self.y)
        self.c_peer = (row, seg + 1 - 2 * self.c)
        self.sent, self.outs = {u: [] for u in range(units)}, []
        self.ready, self.next_y = -1, 0
        self.steps = [(u, k) for u in range(self.units) for k in (1, 3, 2, 0)]
        self.count = len(self.steps) + 8

    def greet(self):
        greet(self.z_peers[1:] + [self.x_peer, self.y_peer, self.c_peer])

    def go(self, u, copy):
        copy.start()
        self.sent[u].append(copy)

    def drain(self, u):
        for copy in self.sent.pop(u, ()):
            copy.wait_send()

    def add(self, *terms):
        result = terms[0].astype(f32)
        for term in terms[1:]:
            result = result + term.astype(f32)
        return result.astype(bf16)


    def to_y(self, u, k):
        i = u % self.slots
        src = self.d.at[i, pl.ds(self.level[k] * 2, 2), pl.ds(self.theirs, self.piece)]
        return remote(src, self.y_in.at[i, k], self.y_s.at[u, k], self.y_r.at[u, k], self.y_peer)

    def to_x(self, u, k):
        i = u % self.slots
        src = self.d.at[i, self.level[k] * 2 + 1 - self.x, pl.ds(self.part, 2 * self.piece)]
        return remote(src, self.x_in.at[i, k], self.x_s.at[u, k], self.x_r.at[u, k], self.x_peer)

    def to_z(self, u, k):
        i = u % self.slots
        src = self.d.at[i, self.level[k] * 2 + self.x, pl.ds(self.part, 2 * self.piece)]
        return remote(
            src, self.z_in.at[i, k - 1], self.z_s.at[u, k - 1], self.z_r.at[u, k - 1], self.z_peers[k]
        )

    def to_y_again(self, u):
        i = u % self.slots
        return remote(
            self.total.at[i], self.y2_in.at[i], self.y2_s.at[u], self.y2_r.at[u], self.y_peer
        )

    def to_core(self, u):
        ref = self.grad.at[u, self.c]
        return remote(ref, ref, self.c_s.at[u], self.c_r.at[u], self.c_peer)

    def begin(self, u):
        self.ready = u

    def pump(self, limit):
        while self.next_y < min(limit, len(self.steps)) and self.steps[self.next_y][0] <= self.ready:
            u, k = self.steps[self.next_y]
            self.go(u, self.to_y(u, k))
            self.next_y += 1

    def step(self, j):
        self.pump(j + 1 + AHEAD)
        d, piece = self.d, self.piece
        mine, part = pl.ds(self.mine, piece), pl.ds(self.part, 2 * piece)
        if j < len(self.steps):
            u, k = self.steps[j]
            i = u % self.slots
            self.to_y(u, k).wait_recv()
            for side in range(2):
                r = self.level[k] * 2 + side
                d[i, r, mine] = self.add(d[i, r, mine], self.y_in[i, k, side])
            self.go(u, self.to_x(u, k))
        if 0 <= j - 1 < len(self.steps):
            u, k = self.steps[j - 1]
            i = u % self.slots
            self.to_x(u, k).wait_recv()
            r = self.level[k] * 2 + self.x
            d[i, r, part] = self.add(d[i, r, part], self.x_in[i, k])
            if k:
                self.go(u, self.to_z(u, k))
        if j >= 5 and (j - 5) % 4 == 0 and (j - 5) // 4 < self.units:
            u = (j - 5) // 4
            i = u % self.slots
            for k in (1, 3, 2):
                self.to_z(u, k).wait_recv()
            z_in = self.z_in
            self.total[i] = self.add(d[i, self.row, part], z_in[i, 0], z_in[i, 1], z_in[i, 2])
            self.go(u, self.to_y_again(u))
        if j >= 6 and (j - 6) % 4 == 0 and (j - 6) // 4 < self.units:
            u = (j - 6) // 4
            i = u % self.slots
            self.to_y_again(u).wait_recv()
            total, y2_in, grad, c = self.total, self.y2_in, self.grad, self.c
            here = pl.ds(pl.multiple_of(self.y * piece, piece), piece)
            there = pl.ds(pl.multiple_of((1 - self.y) * piece, piece), piece)
            grad[u, c, mine] = total[i, here]
            grad[u, c, pl.ds(self.theirs, piece)] = y2_in[i, there]
            grad[u, c, pl.ds(piece, piece)] = self.add(total[i, there], y2_in[i, here])
            self.go(u, self.to_core(u))
        if j >= 7 and (j - 7) % 4 == 0 and (j - 7) // 4 < self.units:
            u = (j - 7) // 4
            self.to_core(u).wait_recv()
            copy = pltpu.make_async_copy(self.grad.at[u], self.out.at[u], self.store.at[u])
            copy.start()
            self.outs.append(copy)

    def finish(self):
        for u in range(self.units):
            self.drain(u)
        for copy in self.outs:
            copy.wait()

    @staticmethod
    def scratch(units, slots, n, width):
        sems = pltpu.SemaphoreType.DMA

        def space(*shape):
            return pltpu.VMEM(shape + (width,), bf16)

        return (
            [
                space(slots, 8, n),
                space(slots, 4, 2, n // 3),
                space(slots, 4, 2 * n // 3),
                space(slots, 3, 2 * n // 3),
                space(slots, 2 * n // 3),
                space(slots, 2 * n // 3),
                space(units, 2, n),
            ]
            + [sems((units, 4))] * 4
            + [sems((units, 3))] * 2
            + [sems((units,))] * 5
        )


def multiply_pair(out, lefts, rights):
    n, width = out.shape[1:]

    def one(i, carry):
        rows = pl.ds(2 * i, 2)
        total = 0.0
        for left, right in zip(lefts, rights):
            total = total + dot(left[rows].reshape(2 * n, left.shape[2]), right[...])
        out[rows] = total.astype(bf16).reshape(2, n, width)
        return carry

    lax.fori_loop(0, 4, one, 0)


def reduce_kernel(
    act, feed, hidden, b0, b1, b2, b3, pair, project, starts, qs, ks, vs, up, out, qv, dk, left, right,
    near, far_s, far_r, save_sem, free, *refs
):
    red = Reduce(out, refs, 6)
    c, count = red.c, up.shape[0]
    rows = pl.ds(0, count)

    def near_copy(index, src, dst):
        return pltpu.make_async_copy(src, dst, near.at[index])

    def far_copy(index, src, dst):
        return remote(src, dst, far_s.at[index], far_r.at[index], red.c_peer)

    def lefts(i):
        return left.at[2 * i], left.at[2 * i + 1]

    def rights(i):
        return right.at[2 * i, rows], right.at[2 * i + 1, rows]

    fixed = [
        (act.at[:, c], act.at[:, 1 - c], lefts(0)),
        (feed, feed, rights(0)),
        (act.at[:, 2 + c], act.at[:, 3 - c], lefts(1)),
        (hidden, hidden, lefts(2)),
    ]
    pulls = [
        ((near_copy(i, here, dst[0]),) * 2, (far_copy(i, there, dst[1]),) * 2)
        for i, (here, there, dst) in enumerate(fixed)
    ]
    for i, two in ((4, (b0, b1)), (5, (b2, b3))):
        dst = rights(i - 3)
        pulls.append(
            (
                tuple(near_copy(i, two[core], dst[0]) for core in range(2)),
                tuple(far_copy(i, two[1 - core], dst[1]) for core in range(2)),
            )
        )
    late_far = right.at[0, rows], right.at[1, rows]
    pulls.append(((near_copy(6, pair.at[c], left.at[0]),) * 2, (far_copy(6, pair.at[1 - c], left.at[1]),) * 2))
    pulls.append(((near_copy(7, pair.at[0], left.at[2]),) * 2, (far_copy(7, pair.at[0], left.at[3]),) * 2))
    pulls.append(
        (
            (None, near_copy(8, project, right.at[2, rows])),
            (far_copy(8, project, late_far[0]), far_copy(8, right.at[3, rows], late_far[0])),
        )
    )
    pulls.append(
        ((None, None), (far_copy(9, right.at[5 - c, rows], late_far[1]),) * 2)
    )

    def start(index, side):
        two = pulls[index][side]
        if two[0] is two[1]:
            if two[0] is not None:
                two[0].start()
            return
        for core in range(2):
            if two[core] is not None:

                @pl.when(c == core)
                def _():
                    two[core].start()

    def arrive(index):
        two, far = pulls[index]
        if two[0] is None and two[1] is not None:

            @pl.when(c == 1)
            def _():
                two[1].wait()
        elif two[0] is not None:
            two[0].wait()
        far[0].wait()

    def block(u):
        for index in ((0, 1), (2,), (3, 4), (5,))[u]:
            arrive(index)
        for index in ((2, 3, 4), (5,), (), ())[u]:
            start(index, 1)
        multiply_pair(red.d.at[u], lefts(min(u, 2)), rights(max(u - 1, 0)))
        red.begin(u)
        if u == 0:
            red.pump(AHEAD)

    def late_pulls():
        pl.semaphore_signal(
            free, inc=1, device_id=red.c_peer, device_id_type=pl.DeviceIdType.MESH
        )
        for index in (6, 7, 8):
            start(index, 0)
        pl.semaphore_wait(free, 1)
        for index in (6, 8, 7, 9):
            start(index, 1)

    def late_block(u):
        for index in ((6, 8), (7, 9))[u - 4]:
            arrive(index)
        red.drain(u - 4)
        own = right.at[3 - c, rows] if u == 4 else right.at[4 + c, rows]
        multiply_pair(red.d.at[u - 4], lefts(u - 4), (own, late_far[u - 4]))
        red.begin(u)

    def spread_up():
        def one(s, carry):
            place = pl.ds(pl.multiple_of(s * SPAN, SPAN), SPAN)
            right[3, place, :] = spread_rows(starts, up, s).astype(bf16)
            return carry

        lax.fori_loop(0, 4, one, 0)

    def heads(first, last):
        def one(s, carry):
            place = pl.ds(pl.multiple_of(s * SPAN, SPAN), SPAN)
            back_slab_flat(starts, s, place, qs, ks, vs, right, range(first, last))
            return carry

        lax.fori_loop(0, 4, one, 0)

    kept = []

    def collect(which, slot, dst):
        def one(i, carry):
            place = pl.ds(pl.multiple_of(i * SPAN, SPAN), SPAN)
            right[slot, place, :] = home_rows(starts, i, right[which], 4).astype(bf16)
            return carry

        lax.fori_loop(0, count // SPAN, one, 0)
        copy = pltpu.make_async_copy(right.at[slot, rows], dst, save_sem.at[which])
        copy.start()
        kept.append(copy)

    for index in (0, 1, 2, 3, 4, 5):
        start(index, 0)
    red.greet()
    for index in (0, 1):
        start(index, 1)
    plan = [partial(block, 0), partial(block, 1), 0, partial(block, 2), 1, partial(block, 3), 2]
    plan += [spread_up, 3]
    for first in range(0, 16, 2):
        plan += [partial(heads, first, first + 2), 4 + first // 2]
    plan += [partial(collect, 0, 4, qv.at[0]), partial(collect, 2, 5, qv.at[1]), 12]
    plan += [partial(collect, 1, 3, dk), late_pulls, 13, 14, partial(late_block, 4), 15]
    plan += [partial(late_block, 5)] + list(range(16, red.count))
    for item in plan:
        if isinstance(item, int):
            red.step(item)
        else:
            item()
    red.finish()
    for copy in kept:
        copy.wait()


def reduce_all(lefts, feed, befores, project, starts, slabs, up):
    pair, hidden, act = lefts
    n = act.shape[2]
    count, width = feed.shape
    sems = pltpu.SemaphoreType.DMA
    return pl.pallas_call(
        reduce_kernel,
        out_shape=(
            jax.ShapeDtypeStruct((6, 2, n, width), bf16),
            jax.ShapeDtypeStruct((2, count, width), bf16),
            jax.ShapeDtypeStruct((count, width), bf16),
        ),
        in_specs=[ANY] * 9 + [SM] + [VM] * 4,
        out_specs=(ANY,) * 3,
        scratch_shapes=[
            pltpu.VMEM((6, 8, n, count), bf16),
            pltpu.VMEM((6, 4 * SPAN, width), bf16),
            sems((9,)),
            sems((10,)),
            sems((10,)),
            sems((3,)),
            pltpu.SemaphoreType.REGULAR,
        ]
        + Reduce.scratch(6, 4, n, width),
        compiler_params=pltpu.CompilerParams(
            collective_id=1, has_side_effects=True, vmem_limit_bytes=60 << 20
        ),
        cost_estimate=pl.CostEstimate(
            flops=180_000_000_000, bytes_accessed=60_000_000, transcendentals=0
        ),
        name="reduce",
    )(act, feed, hidden, *befores, pair, project, starts, *slabs, up)


def reduce_fast(lefts, feed, befores, starts, slabs, up, back_project):
    width = feed.shape[1]
    sums, qv, back_key = reduce_all(lefts, feed, befores, back_project, starts, slabs, up)

    def late():
        con = sums[0:2].reshape(-1, width)
        exp = jnp.concatenate([sums[2, 0], sums[2, 1], sums[3, 0], sums[3, 1]], axis=1)
        att = jnp.concatenate([sums[5, 0], sums[4, 0], sums[5, 1]], axis=1)
        return tuple(part.astype(f32) for part in (att, sums[4, 1], exp, con))

    return (qv[0], back_key, qv[1]), late


def reduce_plain(lefts, feed, befores, starts, slabs, up, back_project):
    hidden_one, attended, hidden_two, activated = lefts
    back_query, back_key, back_value = attend_back(starts, *slabs, up)

    def total(left, right):
        part = lax.psum_scatter(
            outer(left, right).astype(bf16), "rows", scatter_dimension=0, tiled=True
        )
        return lax.psum(part.astype(f32), "seg")

    def late():
        att = total(hidden_one, jnp.concatenate([back_query, back_key, back_value], axis=1))
        exp = total(hidden_two, jnp.concatenate(befores, axis=1))
        return att, total(attended, back_project), exp, total(activated, feed)

    return (back_query, back_key, back_value), late


def on_device(
    fast,
    tokens,
    condition,
    segment_ids,
    cotangent,
    modulation_master,
    modulation_first,
    modulation_second,
    attention_master,
    attention_first,
    attention_second,
    projection_master,
    projection_first,
    projection_second,
    expand_master,
    expand_first,
    expand_second,
    contract_master,
    contract_first,
    contract_second,
    bias_master,
    bias_first,
    bias_second,
):
    width = tokens.shape[1]
    hidden = expand_master.shape[1]
    shard = modulation_master.shape[0]
    n_seg = condition.shape[1]
    row = lax.axis_index("rows")
    segments = segment_ids[0]
    onehot = (segments[:, None] == jnp.arange(n_seg, dtype=jnp.int32)[None, :]).astype(f32)
    starts = jnp.sum(
        segments[:, None] < jnp.arange(n_seg + 1, dtype=jnp.int32)[None, :], axis=0, dtype=jnp.int32
    )
    tokens_wide = tokens.astype(f32)
    upstream = cotangent.astype(f32)

    cond_silu = jax.nn.silu(condition[0].astype(f32)).astype(bf16)
    forward = forward_fast if fast else forward_plain
    output, saved, (w_att, w_proj, w_exp, w_con) = forward(
        (attention_master, projection_master, expand_master, contract_master),
        cond_silu,
        bias_master.astype(bf16),
        modulation_master.astype(bf16),
        starts,
        segments,
        tokens,
    )
    modulation, slabs, projected, middle, before, feedforward, lefts = saved
    shift_one, scale_one, gate_one, shift_two, scale_two, gate_two = of_tokens(
        onehot, modulation, width
    )
    normed_one, inverse_one = layer_norm(tokens_wide)
    normed_two, inverse_two = layer_norm(middle)

    back_gate_two = upstream * feedforward
    back_feed = (upstream * gate_two).astype(bf16)
    back_before = []
    for j, part in enumerate(before):
        back_active = back_dot(back_feed, w_con[j])
        back_before.append(jax.vjp(gelu, part)[1](back_active)[0].astype(bf16))
    back_hidden_two = sum(back_dot(back_before[j], w_exp[j]) for j in range(4))
    back_middle = upstream + norm_back(back_hidden_two * (1.0 + scale_two), normed_two, inverse_two)
    back_gate_one = back_middle * projected
    back_project = (back_middle * gate_one).astype(bf16)
    back_attend = back_dot(back_project, w_proj).astype(bf16)
    def segment_sums(*parts):
        return [outer(onehot, part, highest) for part in parts]

    def column_sums(*parts):
        return [jnp.sum(part.astype(f32), axis=0, keepdims=True) for part in parts]

    early = jnp.concatenate(
        segment_sums(
            back_gate_one, back_hidden_two, back_hidden_two * normed_two, back_gate_two
        )
        + [cond_silu.astype(f32)]
        + column_sums(back_project, *back_before, back_feed),
        axis=0,
    )
    back_attend, early = lax.optimization_barrier((back_attend, early))
    early = lax.all_gather(early.astype(bf16), ("rows", "seg"), axis=0)
    reduce = reduce_fast if fast else reduce_plain
    (back_query, back_key, back_value), late = reduce(
        lefts, back_feed, back_before, starts, slabs, back_attend, back_project
    )
    back_hidden_one = (
        back_dot(back_query, w_att[0]) + back_dot(back_key, w_att[1]) + back_dot(back_value, w_att[2])
    )
    back_tokens = back_middle + norm_back(
        back_hidden_one * (1.0 + scale_one), normed_one, inverse_one
    )
    last = segment_sums(back_hidden_one, back_hidden_one * normed_one)
    last = last + [cond_silu.astype(f32)] + column_sums(back_query, back_value)
    last = jnp.concatenate(last, axis=0)
    last = jnp.pad(last, ((0, -last.shape[0] % 16), (0, 0))).astype(bf16)
    last, early = lax.optimization_barrier((last, early))
    grad_att, grad_proj, grad_exp, grad_con = late()
    if fast:
        last, (grad_con, grad_exp) = gather_last(last, (grad_con, grad_exp))
    else:
        last = lax.all_gather(last, ("rows", "seg"), axis=0)

    def part_of(rows, number):
        return rows[:, number * n_seg : (number + 1) * n_seg].reshape(-1, width)

    def mod_gradient(conds, parts):
        conds = lax.dynamic_slice_in_dim(conds, row * shard, shard, axis=1)
        return outer(conds, jnp.concatenate(parts, axis=1))

    mods = [part_of(last, j) for j in range(2)], [part_of(early, j) for j in range(4)]
    grad_mod = jnp.concatenate(
        [mod_gradient(part_of(last, 2), mods[0]), mod_gradient(part_of(early, 4), mods[1])], axis=1
    )
    totals = [last[:, 3 * n_seg : 3 * n_seg + 2], early[:, 5 * n_seg :]]
    totals = [jnp.sum(part.astype(f32), axis=0) for part in totals]
    totals += [
        jnp.sum(part.astype(f32), axis=0, keepdims=True) for part in mods[0] + mods[1]
    ]
    grad_bias = lax.dynamic_slice_in_dim(
        jnp.concatenate(totals, axis=0).reshape(-1),
        row * bias_master.shape[0],
        bias_master.shape[0],
    )
    results = [
        adam_update(*operands)
        for operands in (
            (grad_mod, modulation_master, modulation_first, modulation_second),
            (grad_att, attention_master, attention_first, attention_second),
            (grad_proj, projection_master, projection_first, projection_second),
            (grad_exp, expand_master, expand_first, expand_second),
            (grad_con, contract_master, contract_first, contract_second),
            (grad_bias, bias_master, bias_first, bias_second),
        )
    ]
    flat = tuple((item for result in results for item in result))
    return (output, back_tokens.astype(bf16)) + flat


def solution(mesh):
    both = ("rows", "seg")
    fast = mesh.shape["rows"] == 8 and mesh.shape["seg"] == 4
    token, matrix, vector = P(both, None), P("rows", None), P("rows")
    in_specs = (token, P(both, None, None), token, token) + (matrix,) * 15 + (vector,) * 3
    out_specs = (token, token) + (matrix,) * 15 + (vector,) * 3
    return jax.shard_map(
        partial(on_device, fast),
        mesh=mesh,
        in_specs=in_specs,
        out_specs=out_specs,
        check_vma=False,
    )
```
